32 devices in a mesh: dp: 16 (over z, y, x), tensor: 2 (over core).
Axes of the slice: x: 2, y: 2, z: 4, core: 2. Of those that a mesh axis runs over, the one named last changes fastest.
Arguments:
- tokens: bfloat16 [2, 16, 640, 1024], P(None, 'dp', 'tensor'), may hold values from -6 to 6
- d_mixed: bfloat16 [2, 16, 640, 1024], P(None, 'dp', 'tensor'), may hold values from -6 to 6
- phone_len: int32 [2, 16], P(None, 'dp'), may hold values from 20 to 320, as said below
- frame_len: int32 [2, 16], P(None, 'dp'), may hold values from 1 to 620
- ln1_gain: float32 [1024], replicated, may hold values from 0.1 to 1.9
- ln1_bias: float32 [1024], replicated, may hold values from -1 to 1
- w_qkv: bfloat16 [1024, 3, 1024], P(None, None, 'tensor'), may hold values from -0.25 to 0.25
- w_out: bfloat16 [1024, 1024], P('tensor'), may hold values from -0.75 to 0.75
- attn_bias: float32 [1024], replicated, may hold values from -1.5 to 1.5
- ln2_gain: float32 [1024], replicated, may hold values from 0.1 to 1.9
- ln2_bias: float32 [1024], replicated, may hold values from -1 to 1
- w_up: bfloat16 [1024, 4096], P(None, 'tensor'), may hold values from -0.1875 to 0.1875
- up_bias: float32 [4096], P('tensor'), may hold values from -1.5 to 1.5
- w_down: bfloat16 [4096, 1024], P('tensor'), may hold values from -0.09375 to 0.09375
- down_bias: float32 [1024], replicated, may hold values from -1.5 to 1.5
Outputs:
- mixed: bfloat16 [2, 16, 640, 1024], P(None, 'dp', 'tensor')
- d_tokens: bfloat16 [2, 16, 640, 1024], P(None, 'dp', 'tensor')
- grad_ln1_gain: float32 [1024], replicated
- grad_ln1_bias: float32 [1024], replicated
- grad_w_qkv: float32 [1024, 3, 1024], P('dp', None, 'tensor')
- grad_w_out: float32 [1024, 1024], P('tensor', 'dp')
- grad_attn_bias: float32 [1024], replicated
- grad_ln2_gain: float32 [1024], replicated
- grad_ln2_bias: float32 [1024], replicated
- grad_w_up: float32 [1024, 4096], P('dp', 'tensor')
- grad_up_bias: float32 [4096], P('tensor')
- grad_w_down: float32 [4096, 1024], P('tensor', 'dp')
- grad_down_bias: float32 [1024], replicated
The draws below stay inside these ranges and needn't reach their ends.
Inputs may be any that keep to these rules, and one draw needn't show every extreme that they name: phone_len + frame_len of a slot lies between 321 and 640; 640 is reached in every draw, once with 320 phonemes and once with 20.
All inputs are finite; a program needn't handle non-finite values.
Results may differ from the reference program's by a relative error of at most 0.017.
Values may be sent and summed in bfloat16 or wider, within the bound.
No kernel may reach another device: no remote copies, remote signals or barrier semaphores. Data moves between devices by JAX's collectives and lax.ppermute only.
A program may use at most 256 MiB of HBM per device.

```python
import math
import jax
import jax.numpy as jnp
from jax import lax

D = 1024
H = 16
HD = 64
FF = 4096
SLOT = 640
MB = 2
PH_MIN = 20
PH_MAX = 400
SEQS = 16


def length_pair(key):
    total_key, phone_key, pick_key = jax.random.split(key, 3)
    grid_shape = (MB, SEQS)
    most_phone = min(PH_MAX, SLOT // 2)
    totals = jax.random.randint(total_key, grid_shape, SLOT // 2 + 1, SLOT + 1)
    phones = jax.random.randint(phone_key, grid_shape, PH_MIN, most_phone + 1)
    shuffled = jax.random.permutation(pick_key, MB * SEQS)
    cell_ids = jnp.arange(MB * SEQS, dtype=jnp.int32).reshape(grid_shape)
    longest = cell_ids == shuffled[0]
    fewest = cell_ids == shuffled[1]
    totals = jnp.where(longest | fewest, SLOT, totals)
    phones = jnp.where(longest, most_phone, jnp.where(fewest, PH_MIN, phones))
    return (phones.astype(jnp.int32), (totals - phones).astype(jnp.int32))


def draw_phone_len(key, part):
    return length_pair(key)[0]


def draw_frame_len(key, part):
    return length_pair(key)[1]


def with_spikes(entries, stream_key, source, target, blocks, factor):
    owner, partner = [(jnp.arange(entries.shape[axis_at]) // (entries.shape[axis_at] // blocks)).reshape([-1 if axis == axis_at else 1 for axis in range(entries.ndim)]) for axis_at in (source, target)]
    chosen = jax.random.permutation(stream_key, blocks)[partner]
    strong = (owner == chosen) | (owner == (partner + blocks // 2) % blocks)
    return jnp.where(strong, factor * entries, entries)


def levels(own_key, extent, cuts, least, high):
    def one(dim, parts):
        heights = jax.random.uniform(jax.random.fold_in(jax.random.fold_in(own_key, 6), dim), (parts,), jnp.float32, least / len(cuts), high / len(cuts))
        return jnp.repeat(jnp.exp(heights), extent[dim] // parts).reshape((-1,) + (1,) * (len(extent) - dim - 1))

    loudness = one(*cuts[0])
    for cut in cuts[1:]:
        loudness = loudness * one(*cut)
    return loudness


def gaussian(key, extent, scale, bound, shards=(), kind=jnp.bfloat16):
    array = jax.random.normal(key, extent, jnp.float32) * scale
    if len(shards) > 0:
        array = levels(key, extent, shards, -0.22, 0.18) * array
    return jnp.clip(array, min=-bound, max=bound).astype(kind)


def heavy_noise(stream_key, extent, deviation, reach, shards, heavy, kind=jnp.bfloat16):
    result = deviation * jax.random.normal(stream_key, extent, jnp.float32)
    if shards:
        result = result * levels(stream_key, extent, shards, -0.22, 0.18)
    return jnp.clip(with_spikes(result, jax.random.fold_in(stream_key, 3), *heavy), -reach, reach).astype(kind)


def setup_inputs(seed: int = 0) -> dict:
    keys = jax.random.split(jax.random.key(seed), 16)
    return {
        "tokens": gaussian(keys[0], (MB, SEQS, SLOT, D), 1.0, 6.0, ((1, 16), (2, 2))),
        "d_mixed": heavy_noise(keys[1], (MB, SEQS, SLOT, D), 1.0, 6.0, ((1, 16), (2, 2)), (1, 3, 16, 2.0)),
        "phone_len": draw_phone_len(jax.random.fold_in(keys[15], 71), 0),
        "frame_len": draw_frame_len(jax.random.fold_in(keys[15], 71), 0),
        "ln1_gain": jnp.clip(1.0 + 0.18 * jax.random.normal(keys[4], (D,), jnp.float32), 0.1, 1.9),
        "ln1_bias": gaussian(keys[5], (D,), 0.2, 1.0, (), jnp.float32),
        "w_qkv": gaussian(keys[6], (D, 3, D), (D // 2) ** -0.5, 0.25, ((2, 2),)),
        "w_out": gaussian(keys[7], (D, D), (D // 16) ** -0.5, 0.75, ((0, 2),)),
        "attn_bias": gaussian(keys[8], (D,), 0.3, 1.5, (), jnp.float32),
        "ln2_gain": jnp.clip(1.0 + 0.18 * jax.random.normal(keys[9], (D,), jnp.float32), 0.1, 1.9),
        "ln2_bias": gaussian(keys[10], (D,), 0.2, 1.0, (), jnp.float32),
        "w_up": gaussian(keys[11], (D, FF), D ** -0.5, 0.1875, ((1, 2),)),
        "up_bias": gaussian(keys[12], (FF,), 0.3, 1.5, ((0, 2),), jnp.float32),
        "w_down": gaussian(keys[13], (FF, D), FF ** -0.5, 0.09375, ((0, 2),)),
        "down_bias": gaussian(keys[14], (D,), 0.3, 1.5, (), jnp.float32),
    }


@jax.custom_vjp
def low(v):
    return lax.optimization_barrier(v.astype(jnp.bfloat16)).astype(jnp.float32)

@jax.custom_vjp
def low_back(v):
    return v

def low_keep(v):
    return (low(v), None)

def low_pass(kept, grad):
    return (grad,)

def back_keep(v):
    return (v, None)

def back_low(kept, grad):
    return (low(grad),)
low.defvjp(low_keep, low_pass)
low_back.defvjp(back_keep, back_low)
norm_eps = 1e-05
highest = lax.Precision.HIGHEST

def norm_rows(values, gain_vec, shift_vec):
    center = values - lax.optimization_barrier(jnp.mean(values, axis=-1, keepdims=True))
    inv_std = lax.rsqrt(lax.optimization_barrier(jnp.mean(center * center, axis=-1, keepdims=True)) + norm_eps)
    return center * inv_std * gain_vec + shift_vec

def layer_rows(weight_set, seq_rows, phone_count, used_len):
    gain_one, shift_one, proj_qkv, proj_out, bias_attn, gain_two, shift_two, proj_up, bias_up, proj_down, bias_down = weight_set
    normed_one = low(norm_rows(seq_rows, gain_one, shift_one))
    qkv_rows = low(low_back(jnp.einsum('sd,dce->sce', normed_one, proj_qkv, precision=highest)))
    head_split = qkv_rows.reshape(SLOT, 3, H, HD)
    query_rows = head_split[:, 0]
    key_rows = head_split[:, 1]
    value_rows = head_split[:, 2]
    scores = low_back(jnp.einsum('qhe,khe->hqk', query_rows, key_rows, precision=highest) * (1.0 / math.sqrt(HD)))
    positions = jnp.arange(SLOT, dtype=jnp.int32)
    allowed = (positions[None, :] < used_len) & ((positions[None, :] <= positions[:, None]) | (positions[None, :] < phone_count))
    weights_low = low(jax.nn.softmax(jnp.where(allowed[None], scores, -1e+30), axis=-1))
    context = jnp.einsum('hqk,khe->qhe', weights_low, value_rows, precision=highest).reshape(SLOT, D)
    context = low(low_back(context))
    attn_out = low_back(jnp.dot(context, proj_out, precision=highest) + bias_attn)
    hidden = seq_rows + attn_out
    normed_two = low(norm_rows(hidden, gain_two, shift_two))
    pre_act = low_back(jnp.dot(normed_two, proj_up, precision=highest) + bias_up)
    activation = low(jax.nn.gelu(pre_act, approximate=True))
    ffn_out = jnp.dot(activation, proj_down, precision=highest) + bias_down
    return jnp.where((positions < used_len)[:, None], hidden + ffn_out, 0.0)

def reference(tokens, d_mixed, phone_len, frame_len, ln1_gain, ln1_bias, w_qkv, w_out, attn_bias, ln2_gain, ln2_bias, w_up, up_bias, w_down, down_bias):
    seq_count = MB * SEQS
    inputs = tokens.astype(jnp.float32).reshape(seq_count, SLOT, D)
    phones = phone_len.reshape(seq_count).astype(jnp.int32)
    totals = (phone_len + frame_len).reshape(seq_count).astype(jnp.int32)
    weight_set = tuple((entry.astype(jnp.float32) for entry in (ln1_gain, ln1_bias, w_qkv, w_out, attn_bias, ln2_gain, ln2_bias, w_up, up_bias, w_down, down_bias)))
    layer_fn = jax.checkpoint(layer_rows)

    def forward(weights_in, rows_all):
        return lax.map(lambda seq_entry: layer_fn(weights_in, seq_entry[0], seq_entry[1], seq_entry[2]), (rows_all, phones, totals))
    mixed, pull_back = jax.vjp(forward, weight_set, inputs)
    weight_grads, d_inputs = pull_back(d_mixed.astype(jnp.float32).reshape(seq_count, SLOT, D))
    return (mixed.astype(jnp.bfloat16).reshape(tokens.shape), d_inputs.astype(jnp.bfloat16).reshape(tokens.shape), weight_grads[0], weight_grads[1], weight_grads[2], weight_grads[3], weight_grads[4], weight_grads[5], weight_grads[6], weight_grads[7], weight_grads[8], weight_grads[9], weight_grads[10])
```

```python
import math

import jax
import jax.numpy as jnp
from jax import lax
from jax.experimental import pallas as pl
from jax.experimental.pallas import tpu as pltpu
from jax.sharding import PartitionSpec as P

HD = 64
EPS = 1e-05
LOW = jnp.bfloat16
F32 = jnp.float32
NT = (((1,), (1,)), ((), ()))
TN = (((0,), (0,)), ((), ()))
GELU_A = math.sqrt(2.0 / math.pi)
GELU_B = 0.044715

S_T, S_DP, S_LEN, S_PH = 0, 1, 2, 4


def dot(a, b, dims=(((1,), (0,)), ((), ()))):
    return lax.dot_general(a, b, dims, preferred_element_type=F32)


def shape(dims, dtype):
    if math.prod(dims) * jnp.dtype(dtype).itemsize >= 1 << 17:
        return pltpu.HBM(dims, dtype)
    return jax.ShapeDtypeStruct(dims, dtype)


def whole(dims, **more):
    return pl.BlockSpec(dims, lambda *_: (0,) * len(dims), **more)


def anywhere():
    return pl.BlockSpec(memory_space=pl.ANY)


class Line:
    def __init__(self, sc):
        self.sc = sc
        self.token = jnp.zeros((8, 128), F32)

    def run(self, kernel, name, grid, ins, outs, scratch=(), mib=24, flops=0, aliases=None):
        count_in, count_out = len(ins), len(outs)

        def body(*refs):
            mid = 1 + count_in
            kernel(*refs[:mid], *refs[mid + 1 : mid + 1 + count_out], *refs[mid + 2 + count_out :])

        arrays = [a for a, _ in ins]
        nbytes = sum(math.prod(a.shape) * a.dtype.itemsize for a in arrays)
        found = pl.pallas_call(
            body,
            grid_spec=pltpu.PrefetchScalarGridSpec(
                num_scalar_prefetch=1,
                grid=grid,
                in_specs=[s for _, s in ins] + [anywhere()],
                out_specs=[s for _, s in outs] + [anywhere()],
                scratch_shapes=list(scratch),
            ),
            out_shape=[o for o, _ in outs] + [jax.ShapeDtypeStruct((8, 128), F32)],
            input_output_aliases={1 + i: o for i, o in (aliases or {}).items()},
            compiler_params=pltpu.CompilerParams(vmem_limit_bytes=mib << 20),
            cost_estimate=pl.CostEstimate(
                flops=int(flops), bytes_accessed=nbytes, transcendentals=0
            ),
            name=name,
        )(self.sc, *arrays, self.token)
        self.token = found[-1]
        return found[:-1]


def center_rows(values):
    center = values - jnp.mean(values, axis=-1, keepdims=True)
    inv_std = lax.rsqrt(jnp.mean(center * center, axis=-1, keepdims=True) + EPS)
    return center * inv_std, inv_std


def norm_back(normed, inv_std, t):
    return inv_std * (
        t
        - jnp.mean(t, axis=-1, keepdims=True)
        - normed * jnp.mean(t * normed, axis=-1, keepdims=True)
    )


def column_sum(values):
    return jnp.sum(values, axis=0, keepdims=True)


def splits(slot):
    half = slot // 2
    cut = -(-half // 128) * 128
    return [(0, cut, cut), (cut, slot, slot)]


def front_kernel(
    sc, x, x_far, gain, shift, w,
    a1, q, k, v, ctx, probs, inv,
    low, qkv, bias, sem,
):
    m, j = pl.program_id(0), pl.program_id(1)
    rows = x.shape[1]
    slot = 2 * rows
    local = w.shape[2]
    here = pl.multiple_of(sc[S_T] * rows, rows)
    there = pl.multiple_of((1 - sc[S_T]) * rows, rows)

    def copy():
        return pltpu.make_async_copy(low, a1.at[m], sem.at[0])

    @pl.when(j == 0)
    def _():
        for source, at in ((x, here), (x_far, there)):
            normed, _ = center_rows(source[0].astype(F32))
            low[pl.ds(at, rows), :] = (normed * gain[...] + shift[...]).astype(LOW)
        copy().start()
        for c in range(3):
            qkv[:, c * local : (c + 1) * local] = dot(low[...], w[c]).astype(LOW)
        qi = lax.broadcasted_iota(jnp.int32, (slot, slot), 0)
        ki = lax.broadcasted_iota(jnp.int32, (slot, slot), 1)
        bias[...] = jnp.where((ki <= qi) | (ki < sc[S_PH + m]), 0.0, -1e30)

    def part(c):
        return qkv[:, pl.ds(pl.multiple_of(c * local + j * 128, 128), 128)]

    lane = lax.broadcasted_iota(jnp.int32, (slot, 128), 1) < HD
    query_all, key, value = part(0), part(1), part(2)
    q[0], k[0], v[0] = query_all, key, value
    widened = jnp.concatenate([value, jnp.ones_like(value)], axis=1)
    for lo, hi, ext in splits(slot):
        query = query_all[lo:hi] * LOW(1.0 / math.sqrt(HD))
        first = lane[lo:hi]
        sums = []
        for h in range(2):
            masked = jnp.where(first if h == 0 else ~first, query, LOW(0))
            s = dot(masked, key[:ext], NT) + bias[lo:hi, :ext]
            p = jnp.exp(s - jnp.max(s, axis=1, keepdims=True)).astype(LOW)
            probs[0, h, lo:hi, :ext] = p
            sums.append(dot(p, widened[:ext]))
        total = jnp.where(first, sums[0][:, :128], sums[1][:, :128])
        scale = 1.0 / jnp.where(first, sums[0][:, 128:], sums[1][:, 128:])
        ctx[0, lo:hi, :] = (total * scale).astype(LOW)
        inv[0, lo:hi, :] = scale

    @pl.when(j == pl.num_programs(1) - 1)
    def _():
        copy().wait()


def front_call(line, x, x_far, gain, shift, w):
    count, rows, width = x.shape
    slot, local = 2 * rows, w.shape[2]
    heads = local // HD
    own = pl.BlockSpec((1, rows, width), lambda m, j, s: (m, 0, 0))
    pair = pl.BlockSpec((1, slot, 128), lambda m, j, s: (m, 0, j))
    natural = shape((count, slot, width), LOW)
    heads_out = shape((count, slot, local), LOW)
    return line.run(
        front_kernel,
        "norm_attend",
        (count, local // 128),
        [(x, own), (x_far, own)]
        + [(gain, whole((1, width))), (shift, whole((1, width)))]
        + [(w, whole(w.shape, pipeline_mode=pl.Buffered(1)))],
        [(natural, anywhere())]
        + [(heads_out, pair)] * 4
        + [
            (
                shape((count, heads, slot, slot), LOW),
                pl.BlockSpec((1, 2, slot, slot), lambda m, j, s: (m, j, 0, 0)),
            ),
            (shape((count, slot, local), F32), pair),
        ],
        scratch=[
            pltpu.VMEM((slot, width), LOW),
            pltpu.VMEM((slot, 3 * local), LOW),
            pltpu.VMEM((slot, slot), F32),
            pltpu.SemaphoreType.DMA((1,)),
        ],
        mib=30,
        flops=2e10,
    )


def project_kernel(
    sc, ctx, far, w, w_far, x, x_far, dm, dm_far, bias, gain, shift, h, a2, e
):
    m, half = pl.program_id(0), pl.program_id(1)
    rows = x.shape[1]
    mine = jnp.full(x.shape[1:], half) == sc[S_T]
    both = dot(ctx[0], w[...]) + dot(far[0], w_far[...])
    hidden = jnp.where(mine, x[0], x_far[0]).astype(F32) + both + bias[...]
    h[...] = hidden.astype(LOW)
    normed, _ = center_rows(hidden)
    a2[...] = (normed * gain[...] + shift[...]).astype(LOW)
    ids = half * rows + lax.broadcasted_iota(jnp.int32, (rows, 1), 0)
    e[...] = jnp.where(ids < sc[S_LEN + m], jnp.where(mine, dm[0], dm_far[0]), LOW(0))


def project_call(line, ctx, far, w, w_far, x, x_far, dm, dm_far, bias, gain, shift):
    count, rows, width = x.shape
    local = ctx.shape[2]
    strip = pl.BlockSpec((1, rows, local), lambda m, i, s: (m, i, 0))
    held = pl.BlockSpec((1, rows, width), lambda m, i, s: (m, 0, 0))
    one = whole((1, width))
    out = (shape((2 * count * rows, width), LOW), pl.BlockSpec((rows, width), lambda m, i, s: (2 * m + i, 0)))
    return line.run(
        project_kernel,
        "project",
        (count, 2),
        [(ctx, strip), (far, strip), (w, whole(w.shape)), (w_far, whole(w.shape))]
        + [(x, held), (x_far, held), (dm, held), (dm_far, held)]
        + [(bias, one), (gain, one), (shift, one)],
        [out] * 3,
        flops=4 * count * rows * width * width,
    )


class Shards:
    def __init__(self, dp_count, width, sides):
        self.dp_count = dp_count
        self.width = width
        self.rows = width // dp_count
        self.sides = sides
        self.bits = dp_count.bit_length() - 1
        self.halving = dp_count == 1 << self.bits and self.bits > 1 and self.rows % 16 == 0

    def outs(self):
        if not self.halving:
            return [jax.ShapeDtypeStruct((self.width, n), LOW) for n in self.sides]
        return [
            jax.ShapeDtypeStruct((self.dp_count // 2, self.rows, n), LOW)
            for n in self.sides
            for _ in range(2)
        ]

    def buffers(self):
        return [pltpu.VMEM(o.shape, LOW) for o in self.outs()]

    def emit(self, sc, value, side, at, refs):
        value = value.astype(LOW)
        span = slice(at, at + value.shape[1])
        if not self.halving:
            refs[side][:, span] = value
            return
        send, keep = refs[2 * side], refs[2 * side + 1]
        blocks = value.reshape(self.dp_count, self.rows, value.shape[1])
        mine = jnp.full((self.rows, value.shape[1]), (sc[S_DP] >> side) & 1) == 1
        for i in range(self.dp_count // 2):
            zero = blocks[insert_bit(i, side, 0)]
            one = blocks[insert_bit(i, side, 1)]
            send[i, :, span] = jnp.where(mine, zero, one)
            keep[i, :, span] = jnp.where(mine, one, zero)


def insert_bit(index, place, bit):
    low = index & ((1 << place) - 1)
    return ((index >> place) << (place + 1)) + low + bit * (1 << place)


def swap_perm(count, bit):
    return [(i, i ^ (1 << bit)) for i in range(count)]


def split_kernel(sc, *refs):
    for side in range(2):
        keep, got = refs[2 * side : 2 * side + 2]
        send_out, keep_out = refs[4 + 2 * side : 6 + 2 * side]
        mine = (sc[S_DP] >> (1 - side)) & 1
        for j, ref in ((1 - mine, send_out), (mine, keep_out)):
            ref[0] = (keep[j].astype(F32) + got[j].astype(F32)).astype(LOW)


def spread_kernel(sc, *refs):
    place = sc[S_DP] >> 2
    at = 0
    for side in range(2):
        keep, got = refs[2 * side : 2 * side + 2]
        columns = keep.shape[2]
        for n, ref in enumerate(refs[4:]):
            j = place ^ n
            ref[:, at : at + columns] = (keep[j].astype(F32) + got[j].astype(F32)).astype(LOW)
        at += columns


class Reduction:
    def __init__(self, line, shards, arrays, finish):
        self.line, self.shards, self.finish = line, shards, finish
        self.step = 0
        if not shards.halving:
            both = jnp.concatenate(
                [
                    lax.psum_scatter(a.astype(F32), "dp", scatter_dimension=0, tiled=True)
                    for a in arrays
                ],
                axis=1,
            )
            self.step = 3
            self.finish(both, [])
            return
        self.keep = [arrays[1], arrays[3]]
        self.got = [self.move(arrays[0], 1), self.move(arrays[2], 2)]

    def move(self, value, mask):
        return lax.ppermute(value, "dp", [(i, i ^ mask) for i in range(self.shards.dp_count)])

    def advance(self):
        self.step += 1
        if self.step > 3:
            return
        if self.step == 3:
            self.finish(self.keep[0], self.got)
            return
        shards = self.shards
        args = [self.keep[0], self.got[0], self.keep[1], self.got[1]]
        rows = shards.rows
        blocks = args[0].shape[0]
        if self.step == 1:
            found = self.line.run(
                split_kernel,
                "add_split",
                (blocks // 2,),
                [(a, pl.BlockSpec((2, rows, a.shape[2]), lambda i, s: (i, 0, 0))) for a in args],
                [
                    (
                        jax.ShapeDtypeStruct((blocks // 2, rows, n), LOW),
                        pl.BlockSpec((1, rows, n), lambda i, s: (i, 0, 0)),
                    )
                    for n in shards.sides
                    for _ in range(2)
                ],
                mib=12,
                flops=3e10,
            )
            self.keep = [found[1], found[3]]
            self.got = [self.move(found[0], 2), self.move(found[2], 1)]
            return
        dims = (rows, sum(shards.sides))
        found = self.line.run(
            spread_kernel,
            "add_spread",
            (1,),
            [(a, whole(a.shape)) for a in args],
            [(jax.ShapeDtypeStruct(dims, LOW), whole(dims))] * blocks,
            mib=12,
            flops=3e10,
        )
        self.keep = [found[0]]
        self.got = [self.move(found[n], 4 * n) for n in range(1, blocks)]


def last_kernel(plan, terms, sc, *refs):
    outs, value, sems = refs[-2 - len({p[0] for p in plan}) : -2], refs[-2], refs[-1]
    total = refs[0][...].astype(F32)
    for ref in refs[1:terms]:
        total = total + ref[...].astype(F32)
    value[...] = total
    copies = []
    for n, (out, lead, column, source, columns) in enumerate(plan):
        target = outs[out] if lead is None else outs[out].at[lead]
        copies.append(
            pltpu.make_async_copy(
                value.at[:, pl.ds(source, columns)],
                target.at[:, pl.ds(column, columns)],
                sems.at[n],
            )
        )
    for copy in copies:
        copy.start()
    for copy in copies:
        copy.wait()


def last_call(line, plan, out_dims, keep, got, before):
    rows, columns = keep.shape
    ins = [(a, whole(a.shape)) for a in (keep, *got)]
    aliases = {}
    if before is not None:
        aliases = {len(ins) + i: i for i in range(len(before))}
        ins += [(b, anywhere()) for b in before]
    return line.run(
        lambda *refs: last_kernel(plan, 1 + len(got), *refs),
        "add_last",
        (1,),
        ins,
        [(pltpu.HBM(d, F32), anywhere()) for d in out_dims],
        scratch=[pltpu.VMEM((rows, columns), F32), pltpu.SemaphoreType.DMA((len(plan),))],
        mib=8,
        aliases=aliases,
    )


def gelu_both(u):
    square = u * u
    t = jnp.tanh(u * (GELU_A + (GELU_A * GELU_B) * square))
    half = 0.5 + 0.5 * t
    slope = half + (0.5 * u) * (1.0 - t * t) * (GELU_A + (3.0 * GELU_A * GELU_B) * square)
    return u * half, slope


def feed_kernel(shards, sc, a2, e, wu, wd, ub, gb, du, bias, *grads):
    rows = a2.shape[0]
    step = rows // 2
    total = jnp.zeros(bias.shape, F32)
    for r in range(0, rows, step):
        u = dot(a2[r : r + step, :], wu[...]) + ub[...]
        act, slope = gelu_both(u)
        gb[r : r + step, :] = act.astype(LOW)
        low = (dot(e[r : r + step, :], wd[...], NT) * slope).astype(LOW)
        du[r : r + step, :] = low
        total = total + column_sum(low.astype(F32))
    bias[...] = total
    shards.emit(sc, dot(e[...], gb[...], TN), 0, 0, grads)
    shards.emit(sc, dot(a2[...], du[...], TN), 1, 0, grads)


def feed_call(line, shards, a2, e, w_up, w_down, up_bias, at, chunk, tile=512):
    rows, width = a2.shape
    tile = min(tile, chunk)
    first = at // tile
    one = pl.Buffered(1)
    strip = pl.BlockSpec((rows, tile), lambda i, s: (0, i))
    outs = [(shape((rows, chunk), LOW), strip)] * 2
    outs.append((shape((1, chunk), F32), pl.BlockSpec((1, tile), lambda i, s: (0, i))))
    for o in shards.outs():
        block = o.shape[:-1] + (tile,)
        lead = (0,) * (len(block) - 1)
        outs.append((o, pl.BlockSpec(block, lambda i, s, lead=lead: (*lead, i))))
    found = line.run(
        lambda *refs: feed_kernel(shards, *refs),
        "feed_forward",
        (chunk // tile,),
        [
            (a2, whole(a2.shape, pipeline_mode=one)),
            (e, whole(e.shape, pipeline_mode=one)),
            (w_up, pl.BlockSpec((width, tile), lambda i, s: (0, first + i))),
            (w_down, pl.BlockSpec((tile, width), lambda i, s: (first + i, 0))),
            (up_bias, pl.BlockSpec((1, tile), lambda i, s: (0, first + i))),
        ],
        outs,
        mib=40,
        flops=8 * rows * width * chunk,
    )
    return found[:3], found[3:]


def up_back_kernel(sc, *refs):
    dus, (w, out) = refs[:-2], refs[-2:]
    total, at = None, 0
    for du in dus:
        term = dot(du[...], w[:, at : at + du.shape[1]], NT)
        at += du.shape[1]
        total = term if total is None else total + term
    out[...] = total.astype(LOW)


def up_back_call(line, dus, w_up, step):
    rows = dus[0].shape[0]
    width, units = w_up.shape
    return line.run(
        up_back_kernel,
        "up_back",
        (rows // step,),
        [(du, pl.BlockSpec((step, du.shape[1]), lambda i, s: (i, 0))) for du in dus]
        + [(w_up, whole(w_up.shape, pipeline_mode=pl.Buffered(1)))],
        [(shape((rows, width), LOW), pl.BlockSpec((step, width), lambda i, s: (i, 0)))],
        mib=32,
        flops=2 * rows * width * units,
    )[0]


def own_rows(rows, step):
    blocks = rows // step

    def place(m, j, i, s):
        half = jnp.where(j == 1, s[S_T], 1 - s[S_T])
        return ((2 * m + half) * blocks + i, 0)

    def send(m, j, i, s):
        return (m, jnp.where(j == 0, i, blocks - 1), 0)

    def keep(m, j, i, s):
        return (m, jnp.where(j == 1, i, 0), 0)

    return blocks, place, send, keep


def down_kernel(sc, *refs):
    acts, (w, keep, send) = refs[:-3], refs[-3:]
    total, at = None, 0
    for act in acts:
        term = dot(act[...], w[at : at + act.shape[1], :])
        at += act.shape[1]
        total = term if total is None else total + term

    @pl.when(pl.program_id(1) == 0)
    def _():
        send[0] = total.astype(LOW)

    @pl.when(pl.program_id(1) == 1)
    def _():
        keep[0] = total.astype(LOW)


def down_call(line, count, rows, acts, w, step):
    width = w.shape[1]
    blocks, place, send, keep = own_rows(rows, step)
    out = shape((count, rows, width), LOW)
    block = (1, step, width)
    return line.run(
        down_kernel,
        "feed_down",
        (count, 2, blocks),
        [(a, pl.BlockSpec((step, a.shape[1]), place)) for a in acts]
        + [(w, whole(w.shape, pipeline_mode=pl.Buffered(1)))],
        [(out, pl.BlockSpec(block, keep)), (out, pl.BlockSpec(block, send))],
        flops=4 * count * rows * w.shape[0] * width,
    )


def mixed_kernel(sc, h, own, got, bias, out):
    m, i = pl.program_id(0), pl.program_id(1)
    rows = own.shape[1]
    first = sc[S_T] * rows * pl.num_programs(1) + i * rows
    ids = first + lax.broadcasted_iota(jnp.int32, (rows, 1), 0)
    value = h[...].astype(F32) + (own[0].astype(F32) + got[0].astype(F32)) + bias[...]
    out[0, 0] = jnp.where(ids < sc[S_LEN + m], value, 0.0).astype(LOW)


def mixed_call(line, h, own, got, bias, step):
    count, rows, width = own.shape
    blocks = rows // step
    block = pl.BlockSpec((1, step, width), lambda m, i, s: (m, i, 0))
    natural = pl.BlockSpec((step, width), lambda m, i, s: ((2 * m + s[S_T]) * blocks + i, 0))
    return line.run(
        mixed_kernel,
        "mixed_rows",
        (count, blocks),
        [(h, natural), (own, block), (got, block), (bias, whole((1, width)))],
        [
            (
                shape((count, 1, rows, width), LOW),
                pl.BlockSpec((1, 1, step, width), lambda m, i, s: (m, 0, i, 0)),
            )
        ],
    )[0]


def hidden_back_kernel(per_half, sc, da, got, h, e, gain, w, dhb, dctx, sums):
    i = pl.program_id(0)
    da2 = da[...].astype(F32) + got[...].astype(F32)
    normed, inv_std = center_rows(h[...].astype(F32))
    out_grad = e[...].astype(F32)
    low = (out_grad + norm_back(normed, inv_std, da2 * gain[...])).astype(LOW)
    dhb[...] = low
    dctx[...] = dot(low, w[...], NT).astype(LOW)
    own = jnp.where((i // per_half) % 2 == sc[S_T], 1.0, 0.0)
    terms = jnp.concatenate(
        [
            column_sum(low.astype(F32)),
            column_sum(da2 * normed),
            column_sum(da2),
            column_sum(out_grad),
        ],
        axis=0,
    )

    @pl.when(i == 0)
    def _():
        sums[...] = terms * own

    @pl.when(i > 0)
    def _():
        sums[...] += terms * own


def hidden_back_call(line, rows, da, got, h, e, gain, w, step):
    total, width = da.shape
    local = w.shape[0]
    strip = lambda wide: pl.BlockSpec((step, wide), lambda i, s: (i, 0))
    wide = strip(width)
    return line.run(
        lambda *refs: hidden_back_kernel(rows // step, *refs),
        "hidden_back",
        (total // step,),
        [(da, wide), (got, wide), (h, wide), (e, wide), (gain, whole((1, width))), (w, whole(w.shape))],
        [
            (shape((total, width), LOW), wide),
            (shape((total, local), LOW), strip(local)),
            (shape((4, width), F32), whole((4, width))),
        ],
        flops=2 * total * width * local,
    )


def attend_back_kernel(shards, group, with_out, sc, q, k, v, ctx, inv, dctx, probs, a1_hbm, *refs):
    extra = [a1_hbm]
    if with_out:
        extra, refs = extra + list(refs[:2]), refs[2:]
    pieces = len(shards.outs())
    refs = refs[-(3 + pieces + 1 + len(extra) + 1) :]
    dq, dk, dv = refs[:3]
    grads = refs[3 : 3 + pieces]
    rows_all = refs[3 + pieces]
    held = refs[4 + pieces : 4 + pieces + len(extra)]
    sems = refs[-1]
    j, m = pl.program_id(0), pl.program_id(1)

    def copies():
        return [
            pltpu.make_async_copy(source, target, sems.at[n])
            for n, (source, target) in enumerate(zip(extra, held))
        ]

    @pl.when((j == 0) & (m == 0))
    def _():
        for copy in copies():
            copy.start()

    slot = q.shape[1]
    lane = lax.broadcasted_iota(jnp.int32, (slot, 128), 1) < HD
    scaled = dctx[0].astype(F32) * inv[0]
    product = scaled * ctx[0].astype(F32)
    low = scaled.astype(LOW)
    key, query, value = k[0], q[0], v[0]
    cuts = splits(slot)
    per_head = []
    for h in range(2):
        here = lane if h == 0 else ~lane
        delta = jnp.sum(jnp.where(here, product, 0.0), axis=1, keepdims=True)
        masked = jnp.where(here, low, LOW(0))
        dqs, dks, dvs = [], [], []
        for lo, hi, ext in cuts:
            p = probs[0, h, lo:hi, :ext]
            dp = dot(masked[lo:hi], value[:ext], NT)
            ds = (p.astype(F32) * (dp - delta[lo:hi])).astype(LOW)
            dqs.append(dot(ds, key[:ext]))
            dks.append(dot(ds, query[lo:hi], TN))
            dvs.append(dot(p, low[lo:hi], TN))
        first = cuts[0][2]
        join = lambda two: jnp.concatenate([two[0] + two[1][:first], two[1][first:]], axis=0)
        per_head.append((jnp.concatenate(dqs, axis=0), join(dks), join(dvs)))
    root = 1.0 / math.sqrt(HD)
    start = pl.multiple_of(m * slot, slot)
    for c, (ref, scale) in enumerate(((dq, root), (dk, root), (dv, 1.0))):
        both = (jnp.where(lane, per_head[0][c], per_head[1][c]) * scale).astype(LOW)
        ref[0] = both
        rows_all[j, pl.ds(start, slot), c * 128 : (c + 1) * 128] = both

    @pl.when((m == pl.num_programs(1) - 1) & (j == group - 1))
    def _():
        for copy in copies():
            copy.wait()
        at = [0, 0]
        for g in range(group):
            side = g * 2 // group
            shards.emit(sc, dot(held[0][...], rows_all[g], TN), side, at[side], grads)
            at[side] += 384
        if with_out:
            local = held[2].shape[1]
            for c in range(0, local, 256):
                side = c * 2 // local
                term = dot(held[1][...], held[2][:, c : c + 256], TN)
                shards.emit(sc, term, side, at[side], grads)
                at[side] += 256


def attend_back_call(line, shards, group, at, qkv, ctx, inv, dctx, probs, a1, out_pair=(), before=None):
    count, slot, local = ctx.shape
    pair = pl.BlockSpec((1, slot, 128), lambda j, m, s: (m, 0, at * group + j))
    ins = [(a, pair) for a in (*qkv, ctx, inv, dctx)]
    ins.append((probs, pl.BlockSpec((1, 2, slot, slot), lambda j, m, s: (m, at * group + j, 0, 0))))
    extra = [a1, *out_pair]
    ins += [(a, anywhere()) for a in extra]
    aliases = {}
    if before is not None:
        aliases = {len(ins) + i: i for i in range(3)}
        ins += [(b, anywhere()) for b in before]
    found = line.run(
        lambda *refs: attend_back_kernel(shards, group, len(out_pair) > 0, *refs),
        "attend_back",
        (group, count),
        ins,
        [(shape((count, slot, local), LOW), pair)] * 3 + [(o, whole(o.shape)) for o in shards.outs()],
        scratch=[pltpu.VMEM((group, count * slot, 384), LOW)]
        + [pltpu.VMEM(a.shape, LOW) for a in extra]
        + [pltpu.SemaphoreType.DMA((len(extra),))],
        mib=32,
        flops=12e9,
        aliases=aliases,
    )
    return found[:3], found[3:]


def rows_back_kernel(sc, dq, dk, dv, w, x, x_far, keep, send, sums):
    m, j, i = pl.program_id(0), pl.program_id(1), pl.program_id(2)
    total = dot(dq[...], w[0], NT) + dot(dk[...], w[1], NT) + dot(dv[...], w[2], NT)

    @pl.when(j == 0)
    def _():
        send[0] = total.astype(LOW)

    @pl.when(j == 1)
    def _():
        keep[0] = total.astype(LOW)

    mine = jnp.full(x.shape[1:], j) == 1
    normed, _ = center_rows(jnp.where(mine, x[0], x_far[0]).astype(F32))
    terms = jnp.concatenate([column_sum(total * normed), column_sum(total)], axis=0)
    start = (m == 0) & (j == 0) & (i == 0)

    @pl.when(start)
    def _():
        sums[...] = terms

    @pl.when(~start)
    def _():
        sums[...] += terms


def rows_back_call(line, grads, w, x, x_far, step):
    count, rows, width = x.shape
    total, local = 2 * count * rows, w.shape[2]
    blocks, place, send, keep = own_rows(rows, step)
    out = shape((count, rows, width), LOW)
    block = (1, step, width)
    return line.run(
        rows_back_kernel,
        "rows_back",
        (count, 2, blocks),
        [(g, pl.BlockSpec((step, local), place)) for g in grads]
        + [(w, whole(w.shape, pipeline_mode=pl.Buffered(1)))]
        + [(v, pl.BlockSpec((1, step, width), lambda m, j, i, s: (m, i, 0))) for v in (x, x_far)],
        [
            (out, pl.BlockSpec(block, keep)),
            (out, pl.BlockSpec(block, send)),
            (shape((2, width), F32), whole((2, width))),
        ],
        flops=6 * total * width * local,
    )


def tokens_back_kernel(sc, x, dh, own, got, gain, out):
    normed, inv_std = center_rows(x[0].astype(F32))
    da1 = own[0].astype(F32) + got[0].astype(F32)
    back = norm_back(normed, inv_std, da1 * gain[...])
    out[0, 0] = (dh[...].astype(F32) + back).astype(LOW)


def tokens_back_call(line, x, dh, own, got, gain, step):
    count, rows, width = own.shape
    blocks = rows // step
    block = pl.BlockSpec((1, step, width), lambda m, i, s: (m, i, 0))
    natural = pl.BlockSpec((step, width), lambda m, i, s: ((2 * m + s[S_T]) * blocks + i, 0))
    return line.run(
        tokens_back_kernel,
        "tokens_back",
        (count, blocks),
        [(x, block), (dh, natural), (own, block), (got, block), (gain, whole((1, width)))],
        [
            (
                shape((count, 1, rows, width), LOW),
                pl.BlockSpec((1, 1, step, width), lambda m, i, s: (m, 0, i, 0)),
            )
        ],
    )[0]


def swap(value):
    return lax.ppermute(value, "tensor", [(0, 1), (1, 0)])


def vector_kernel(sc, *refs):
    ins, out = refs[:-1], refs[-1]
    if len(ins) == 2:
        out[...] = ins[0][...] + ins[1][...]
    else:
        out[...] = (ins[0][...] + ins[1][...]) + (ins[2][...] + ins[3][...])


class Vectors:
    def __init__(self, line, dp_count, values, shared):
        self.line, self.dp_count, self.values = line, dp_count, values
        rows = lax.broadcasted_iota(jnp.int32, (values.shape[0], 1), 0)
        self.got = [swap(jnp.where(rows < shared, values, 0.0))]
        self.bits = [bit for bit in range(dp_count.bit_length() - 1)]
        if dp_count & (dp_count - 1):
            self.values = lax.psum(values + self.got[0], "dp")
            self.got, self.bits = [], []

    def advance(self):
        if not self.got:
            return
        dims = self.values.shape
        self.values = self.line.run(
            vector_kernel,
            "add_vectors",
            (1,),
            [(a, whole(dims)) for a in (self.values, *self.got)],
            [(jax.ShapeDtypeStruct(dims, F32), whole(dims))],
            mib=8,
        )[0]
        masks = [1 << bit for bit in self.bits[:2]]
        self.bits = self.bits[2:]
        if len(masks) == 2:
            masks.append(masks[0] | masks[1])
        self.got = [
            lax.ppermute(self.values, "dp", [(i, i ^ mask) for i in range(self.dp_count)])
            for mask in masks
        ]


def local(
    tokens,
    d_mixed,
    phone_len,
    frame_len,
    ln1_gain,
    ln1_bias,
    w_qkv,
    w_out,
    attn_bias,
    ln2_gain,
    ln2_bias,
    w_up,
    up_bias,
    w_down,
    down_bias,
):
    count, _, rows, width = tokens.shape
    dp_count = lax.axis_size("dp")
    slot = 2 * rows
    local_width = w_qkv.shape[2]
    units = w_up.shape[1]
    shard_rows = width // dp_count
    step = rows
    row = lambda v: v.reshape(1, -1)
    x, dm = tokens[:, 0], d_mixed[:, 0]
    phones = phone_len[:, 0]
    sc = jnp.concatenate(
        [
            jnp.stack([lax.axis_index("tensor"), lax.axis_index("dp")]).astype(jnp.int32),
            phones + frame_len[:, 0],
            phones,
        ]
    )
    line = Line(sc)
    w3 = jnp.transpose(w_qkv, (1, 0, 2))
    g1, b1, g2, b2 = row(ln1_gain), row(ln1_bias), row(ln2_gain), row(ln2_bias)
    flat = lambda v: v.reshape(count * slot, v.shape[-1])

    x_far, dm_far, w_out_far = swap(x), swap(dm), swap(w_out)
    a1, *qkv, ctx, probs, inv = front_call(line, x, x_far, g1, b1, w3)
    h, a2, en = project_call(
        line, ctx, swap(ctx), w_out, w_out_far, x, x_far, dm, dm_far, row(attn_bias), g2, b2
    )

    downs, ups, outs, qkvs = [None], [None], [None], [None]

    def finish_feed(at, chunk):
        def finish(keep, got):
            plan = [(0, None, at, 0, chunk), (1, None, at, chunk, chunk)]
            before = None if downs[0] is None else [downs[0], ups[0]]
            dims = [(shard_rows, units)] * 2
            downs[0], ups[0] = last_call(line, plan, dims, keep, got, before)

        return finish

    chunks = (units // 2, units // 2)
    reds, acts, dus, up_sums, at = [], [], [], [], 0
    for chunk in chunks:
        shards = Shards(dp_count, width, (chunk, chunk))
        (act, du, up_sum), grads = feed_call(
            line, shards, a2, en, w_up, w_down, row(up_bias), at, chunk
        )
        reds.append(Reduction(line, shards, grads, finish_feed(at, chunk)))
        acts.append(act)
        dus.append(du)
        up_sums.append(up_sum)
        at += chunk
    red1, red2 = reds
    da = up_back_call(line, dus, w_up, step)
    da_far = swap(da)
    red1.advance()

    dhb, dctx, hidden_sums = hidden_back_call(line, rows, da, da_far, h, en, g2, w_out, step)
    red2.advance()
    red1.advance()

    groups = 2
    group = local_width // 128 // groups
    side = group * 192
    dctx = dctx.reshape(count, slot, local_width)
    out_side = local_width // 2
    shards3 = Shards(dp_count, width, (side + out_side, side + out_side))
    shards4 = Shards(dp_count, width, (side, side))

    def finish_heads(at, wide, with_out):
        def finish(keep, got):
            plan = []
            for g in range(group):
                start = (g * 2 // group) * wide + (g % (group // 2)) * 384
                for c in range(3):
                    plan.append((0, c, (at * group + g) * 128, start + c * 128, 128))
            dims = [(3, shard_rows, local_width)]
            if with_out:
                for n in range(2):
                    plan.append((1, None, n * out_side, n * wide + side, out_side))
                dims.append((shard_rows, local_width))
            before = None if qkvs[0] is None else [qkvs[0]]
            found = last_call(line, plan, dims, keep, got, before)
            qkvs[0] = found[0]
            if with_out:
                outs[0] = found[1]

        return finish

    grads, parts = attend_back_call(
        line, shards3, group, 0, qkv, ctx, inv, dctx, probs, flat(a1), (dhb, flat(ctx))
    )
    red3 = Reduction(line, shards3, parts, finish_heads(0, side + out_side, True))
    red2.advance()
    red1.advance()
    grads, parts = attend_back_call(
        line, shards4, group, 1, qkv, ctx, inv, dctx, probs, flat(a1), (), grads
    )
    red4 = Reduction(line, shards4, parts, finish_heads(1, side, False))
    red3.advance()
    red2.advance()
    red1.advance()
    own, far, token_sums = rows_back_call(
        line, [flat(g) for g in grads], w3, x, x_far, step
    )
    far = swap(far)
    up_rows = jnp.concatenate(up_sums, axis=1).reshape(-1, width)
    sums = Vectors(line, dp_count, jnp.concatenate([token_sums, hidden_sums, up_rows]), 6)
    red4.advance()
    red3.advance()
    red2.advance()
    sums.advance()
    own_down, far_down = down_call(line, count, rows, acts, w_down, step)
    far_down = swap(far_down)
    red4.advance()
    red3.advance()
    sums.advance()
    d_tokens = tokens_back_call(line, x, dhb, own, far, g1, step)
    mixed = mixed_call(line, h, own_down, far_down, row(down_bias), step)
    red4.advance()
    sums.advance()
    while sums.got:
        sums.advance()
    vectors = sums.values

    return (
        mixed,
        d_tokens,
        vectors[0],
        vectors[1],
        jnp.transpose(qkvs[0], (1, 0, 2)),
        outs[0].T,
        vectors[2],
        vectors[3],
        vectors[4],
        ups[0],
        vectors[6:].reshape(-1),
        downs[0].T,
        vectors[5],
    )


def solution(mesh):
    in_specs = (
        P(None, "dp", "tensor", None),
        P(None, "dp", "tensor", None),
        P(None, "dp"),
        P(None, "dp"),
        P(),
        P(),
        P(None, None, "tensor"),
        P("tensor", None),
        P(),
        P(),
        P(),
        P(None, "tensor"),
        P("tensor"),
        P("tensor", None),
        P(),
    )
    out_specs = (
        P(None, "dp", "tensor", None),
        P(None, "dp", "tensor", None),
        P(),
        P(),
        P("dp", None, "tensor"),
        P("tensor", "dp"),
        P(),
        P(),
        P(),
        P("dp", "tensor"),
        P("tensor"),
        P("tensor", "dp"),
        P(),
    )
    return jax.shard_map(local, mesh=mesh, in_specs=in_specs, out_specs=out_specs, check_vma=False)
```

```python
import math

import jax
import jax.numpy as jnp
from jax import lax
from jax.experimental import pallas as pl
from jax.experimental.pallas import tpu as pltpu
from jax.sharding import PartitionSpec as P

HD = 64
EPS = 1e-05
LOW = jnp.bfloat16
F32 = jnp.float32
NT = (((1,), (1,)), ((), ()))
TN = (((0,), (0,)), ((), ()))
GELU_A = math.sqrt(2.0 / math.pi)
GELU_B = 0.044715

S_T, S_DP, S_LEN, S_PH = 0, 1, 2, 4


def dot(a, b, dims=(((1,), (0,)), ((), ()))):
    return lax.dot_general(a, b, dims, preferred_element_type=F32)


def shape(dims, dtype):
    if math.prod(dims) * jnp.dtype(dtype).itemsize >= 1 << 17:
        return pltpu.HBM(dims, dtype)
    return jax.ShapeDtypeStruct(dims, dtype)


def near(dims, dtype):
    return pltpu.VMEM(dims, dtype)


def whole(dims, **more):
    return pl.BlockSpec(dims, lambda *_: (0,) * len(dims), **more)


def anywhere():
    return pl.BlockSpec(memory_space=pl.ANY)


ADD_FLOPS = 3e10


class Line:
    def __init__(self, sc):
        self.sc = sc
        self.token = jnp.zeros((8, 128), F32)
        self.pending, self.carried = [], []

    def run(self, kernel, name, grid, ins, outs, scratch=(), mib=24, flops=0, aliases=None):
        count_in, count_out = len(ins), len(outs)
        through, self.pending = [self.token, *self.pending], []
        extra = len(through)

        def body(*refs):
            mid = 1 + count_in
            end = mid + extra + count_out
            kernel(*refs[:mid], *refs[mid + extra : end], *refs[end + extra :])

        arrays = [a for a, _ in ins]
        nbytes = sum(math.prod(a.shape) * a.dtype.itemsize for a in arrays)
        aliases = {1 + i: o for i, o in (aliases or {}).items()}
        aliases.update({1 + count_in + n: count_out + n for n in range(extra)})
        found = pl.pallas_call(
            body,
            grid_spec=pltpu.PrefetchScalarGridSpec(
                num_scalar_prefetch=1,
                grid=grid,
                in_specs=[s for _, s in ins] + [anywhere()] * extra,
                out_specs=[s for _, s in outs] + [anywhere()] * extra,
                scratch_shapes=list(scratch),
            ),
            out_shape=[o for o, _ in outs]
            + [jax.ShapeDtypeStruct(t.shape, t.dtype) for t in through],
            input_output_aliases=aliases,
            compiler_params=pltpu.CompilerParams(vmem_limit_bytes=mib << 20),
            cost_estimate=pl.CostEstimate(
                flops=int(flops * 1), bytes_accessed=int(nbytes * 1), transcendentals=0
            ),
            name=name,
        )(self.sc, *arrays, *through)
        self.token, self.carried = found[count_out], list(found[count_out + 1 :])
        return found[:count_out]


def center_rows(values):
    center = values - jnp.mean(values, axis=-1, keepdims=True)
    inv_std = lax.rsqrt(jnp.mean(center * center, axis=-1, keepdims=True) + EPS)
    return center * inv_std, inv_std


def norm_back(normed, inv_std, t):
    return inv_std * (
        t
        - jnp.mean(t, axis=-1, keepdims=True)
        - normed * jnp.mean(t * normed, axis=-1, keepdims=True)
    )


def column_sum(values):
    return jnp.sum(values, axis=0, keepdims=True)


def bring(arrays):
    vm = pl.BlockSpec(memory_space=pltpu.VMEM)
    hbm = pl.BlockSpec(memory_space=pltpu.HBM)

    def kernel(*refs):
        count = len(arrays)
        sems = refs[-1]
        copies = [
            pltpu.make_async_copy(source, target, sems.at[n])
            for n, (source, target) in enumerate(zip(refs[:count], refs[count:-1]))
        ]
        for copy in copies:
            copy.start()
        for copy in copies:
            copy.wait()

    return pl.pallas_call(
        kernel,
        in_specs=[hbm] * len(arrays),
        out_specs=[vm] * len(arrays),
        out_shape=[near(a.shape, a.dtype) for a in arrays],
        scratch_shapes=[pltpu.SemaphoreType.DMA((len(arrays),))],
        compiler_params=pltpu.CompilerParams(vmem_limit_bytes=4 << 20),
        name="bring",
    )(*arrays)


def splits(slot):
    half = slot // 2
    cut = -(-half // 128) * 128
    return [(0, cut, cut), (cut, slot, slot)]


def front_kernel(
    sc, x, x_far, gain, shift, w,
    a1, q, k, v, ctx, probs, inv,
    low, qkv, bias, sem,
):
    m, j = pl.program_id(0), pl.program_id(1)
    rows = x.shape[1]
    slot = 2 * rows
    local = w.shape[2]
    here = pl.multiple_of(sc[S_T] * rows, rows)
    there = pl.multiple_of((1 - sc[S_T]) * rows, rows)

    def copy():
        return pltpu.make_async_copy(low, a1.at[m], sem.at[0])

    @pl.when(j == 0)
    def _():
        for source, at in ((x, here), (x_far, there)):
            normed, _ = center_rows(source[0].astype(F32))
            low[pl.ds(at, rows), :] = (normed * gain[...] + shift[...]).astype(LOW)
        copy().start()
        for c in range(3):
            qkv[:, c * local : (c + 1) * local] = dot(low[...], w[c]).astype(LOW)
        qi = lax.broadcasted_iota(jnp.int32, (slot, slot), 0)
        ki = lax.broadcasted_iota(jnp.int32, (slot, slot), 1)
        bias[...] = jnp.where((ki <= qi) | (ki < sc[S_PH + m]), 0.0, -1e30)

    def part(c):
        return qkv[:, pl.ds(pl.multiple_of(c * local + j * 128, 128), 128)]

    lane = lax.broadcasted_iota(jnp.int32, (slot, 128), 1) < HD
    query_all, key, value = part(0), part(1), part(2)
    q[0], k[0], v[0] = query_all, key, value
    widened = jnp.concatenate([value, jnp.ones_like(value)], axis=1)
    for lo, hi, ext in splits(slot):
        query = query_all[lo:hi] * LOW(1.0 / math.sqrt(HD))
        first = lane[lo:hi]
        sums = []
        for h in range(2):
            masked = jnp.where(first if h == 0 else ~first, query, LOW(0))
            s = dot(masked, key[:ext], NT) + bias[lo:hi, :ext]
            p = jnp.exp(s - jnp.max(s, axis=1, keepdims=True)).astype(LOW)
            probs[0, h, lo:hi, :ext] = p
            sums.append(dot(p, widened[:ext]))
        total = jnp.where(first, sums[0][:, :128], sums[1][:, :128])
        scale = 1.0 / jnp.where(first, sums[0][:, 128:], sums[1][:, 128:])
        ctx[0, lo:hi, :] = (total * scale).astype(LOW)
        inv[0, lo:hi, :] = scale

    @pl.when(j == pl.num_programs(1) - 1)
    def _():
        copy().wait()


def front_call(line, x, x_far, gain, shift, w):
    count, rows, width = x.shape
    slot, local = 2 * rows, w.shape[2]
    heads = local // HD
    own = pl.BlockSpec((1, rows, width), lambda m, j, s: (m, 0, 0))
    pair = pl.BlockSpec((1, slot, 128), lambda m, j, s: (m, 0, j))
    natural = shape((count, slot, width), LOW)
    heads_out = shape((count, slot, local), LOW)
    return line.run(
        front_kernel,
        "norm_attend",
        (count, local // 128),
        [(x, own), (x_far, own)]
        + [(gain, whole((1, width))), (shift, whole((1, width)))]
        + [(w, whole(w.shape, pipeline_mode=pl.Buffered(1)))],
        [(natural, anywhere())]
        + [(heads_out, pair)] * 4
        + [
            (
                shape((count, heads, slot, slot), LOW),
                pl.BlockSpec((1, 2, slot, slot), lambda m, j, s: (m, j, 0, 0)),
            ),
            (shape((count, slot, local), F32), pair),
        ],
        scratch=[
            pltpu.VMEM((slot, width), LOW),
            pltpu.VMEM((slot, 3 * local), LOW),
            pltpu.VMEM((slot, slot), F32),
            pltpu.SemaphoreType.DMA((1,)),
        ],
        mib=30,
        flops=2e10,
    )


def mark_kernel(sc, dm, dm_far, e):
    m, half = pl.program_id(0), pl.program_id(1)
    rows = dm.shape[1]
    mine = jnp.full(dm.shape[1:], half) == sc[S_T]
    ids = half * rows + lax.broadcasted_iota(jnp.int32, (rows, 1), 0)
    e[...] = jnp.where(ids < sc[S_LEN + m], jnp.where(mine, dm[0], dm_far[0]), LOW(0))


def mark_call(line, dm, dm_far):
    count, rows, width = dm.shape
    held = pl.BlockSpec((1, rows, width), lambda m, i, s: (m, 0, 0))
    return line.run(
        mark_kernel,
        "mark_rows",
        (count, 2),
        [(dm, held), (dm_far, held)],
        [(near((2 * count * rows, width), LOW), pl.BlockSpec((rows, width), lambda m, i, s: (2 * m + i, 0)))],
    )[0]


def project_kernel(sc, ctx, far, w, w_far, x, x_far, bias, gain, shift, h, a2):
    m, half = pl.program_id(0), pl.program_id(1)
    mine = jnp.full(x.shape[1:], half) == sc[S_T]
    both = dot(ctx[0], w[...]) + dot(far[0], w_far[...])
    hidden = jnp.where(mine, x[0], x_far[0]).astype(F32) + both + bias[...]
    h[...] = hidden.astype(LOW)
    normed, _ = center_rows(hidden)
    a2[...] = (normed * gain[...] + shift[...]).astype(LOW)


def project_call(line, ctx, far, w, w_far, x, x_far, bias, gain, shift):
    count, rows, width = x.shape
    local = ctx.shape[2]
    strip = pl.BlockSpec((1, rows, local), lambda m, i, s: (m, i, 0))
    held = pl.BlockSpec((1, rows, width), lambda m, i, s: (m, 0, 0))
    one = whole((1, width))
    out = (shape((2 * count * rows, width), LOW), pl.BlockSpec((rows, width), lambda m, i, s: (2 * m + i, 0)))
    return line.run(
        project_kernel,
        "project",
        (count, 2),
        [(ctx, strip), (far, strip), (w, whole(w.shape)), (w_far, whole(w.shape))]
        + [(x, held), (x_far, held)]
        + [(bias, one), (gain, one), (shift, one)],
        [out, (near((2 * count * rows, width), LOW), out[1])],
        flops=4 * count * rows * width * width,
    )


class Shards:
    def __init__(self, dp_count, width, sides):
        self.dp_count = dp_count
        self.width = width
        self.rows = width // dp_count
        self.sides = sides
        self.bits = dp_count.bit_length() - 1
        self.halving = dp_count == 1 << self.bits and self.bits > 2 and self.rows % 16 == 0
        late = list(range(3, self.bits))
        orders = ([0, 1, 2], [1, 0, 2]) if len(sides) == 2 else ([0, 1, 2], [1, 2, 0], [2, 0, 1])
        self.orders = [order + late for order in orders]

    def outs(self):
        if not self.halving:
            return [jax.ShapeDtypeStruct((self.width, n), LOW) for n in self.sides]
        return [
            kind((self.dp_count // 2, self.rows, n), LOW)
            for n in self.sides
            for kind in (pltpu.HBM, near if sum(self.sides) < 0 else pltpu.HBM)
        ]

    def emit(self, sc, value, side, at, refs):
        value = value.astype(LOW)
        span = slice(at, at + value.shape[1])
        if not self.halving:
            refs[side][:, span] = value
            return
        send, keep = refs[2 * side], refs[2 * side + 1]
        blocks = value.reshape(self.dp_count, self.rows, value.shape[1])
        order = self.orders[side]
        mine = jnp.full((self.rows, value.shape[1]), (sc[S_DP] >> order[0]) & 1) == 1
        for i in range(self.dp_count // 2):
            at_zero = sum(((i >> n) & 1) << bit for n, bit in enumerate(order[1:]))
            zero = blocks[at_zero]
            one = blocks[at_zero + (1 << order[0])]
            send[i, :, span] = jnp.where(mine, zero, one)
            keep[i, :, span] = jnp.where(mine, one, zero)


def split_kernel(bits, sc, *refs):
    sides = len(bits)
    ins, outs = refs[: 2 * sides], refs[2 * sides :]
    joined = len(outs) == 2
    at = 0
    for n, bit in enumerate(bits):
        keep, got = ins[2 * n], ins[2 * n + 1]
        send_out, keep_out = outs[:2] if joined else outs[2 * n : 2 * n + 2]
        columns = keep.shape[2]
        mine = (sc[S_DP] >> bit) & 1
        for j, ref in ((1 - mine, send_out), (mine, keep_out)):
            total = (keep[j].astype(F32) + got[j].astype(F32)).astype(LOW)
            ref[0, :, at : at + columns] = total
        if joined:
            at += columns


def split_call(line, bits, args, widths, name, flops):
    blocks, rows, _ = args[0].shape
    return line.run(
        lambda *refs: split_kernel(bits, *refs),
        name,
        (blocks // 2,),
        [(a, pl.BlockSpec((2, rows, a.shape[2]), lambda i, s: (i, 0, 0))) for a in args],
        [
            (
                jax.ShapeDtypeStruct((blocks // 2, rows, n), LOW),
                pl.BlockSpec((1, rows, n), lambda i, s: (i, 0, 0)),
            )
            for n in widths
            for _ in range(2)
        ],
        mib=12,
        flops=flops,
    )


def move(value, dp_count, mask):
    return lax.ppermute(value, "dp", [(i, i ^ mask) for i in range(dp_count)])


class Reduction:
    def __init__(self, line, shards, arrays):
        self.line, self.shards = line, shards
        self.step = 0
        if not shards.halving:
            self.keep = jnp.concatenate(
                [
                    lax.psum_scatter(a.astype(F32), "dp", scatter_dimension=0, tiled=True)
                    for a in arrays
                ],
                axis=1,
            )
            self.got, self.step = [], shards.bits
            return
        self.orders = shards.orders
        self.sides = shards.sides
        self.keep = arrays[1::2]
        self.send(arrays[::2])

    def send(self, arrays):
        count = self.shards.dp_count
        self.got = [
            lax.ppermute(a, "dp", [(i, i ^ (1 << order[self.step])) for i in range(count)])
            for a, order in zip(arrays, self.orders)
        ]
        self.step += 1

    def advance(self, flops=ADD_FLOPS):
        if self.step >= self.shards.bits:
            return
        bits = [order[self.step] for order in self.orders]
        joined = all(order[self.step :] == self.orders[0][self.step :] for order in self.orders)
        args = [a for pair in zip(self.keep, self.got) for a in pair]
        widths = [sum(self.sides)] if joined else self.sides
        found = split_call(self.line, bits, args, widths, "add_split", flops)
        if joined:
            self.orders, self.sides = self.orders[:1], widths
        self.keep = found[1::2]
        self.send(found[::2])

    def finish(self, plan, out_dims, before=None):
        while self.step < self.shards.bits:
            self.advance()
        keep, got = self.keep, self.got
        if self.shards.halving:
            keep, got = (v[0].reshape(v[0].shape[-2:]) for v in (keep, got))
            got = [got]
        return last_call(self.line, plan, out_dims, keep, got, before)


def last_kernel(plan, terms, sc, *refs):
    outs, value, sems = refs[-2 - len({p[0] for p in plan}) : -2], refs[-2], refs[-1]
    total = refs[0][...].astype(F32)
    for ref in refs[1:terms]:
        total = total + ref[...].astype(F32)
    value[...] = total
    copies = []
    for n, (out, lead, column, source, columns) in enumerate(plan):
        target = outs[out] if lead is None else outs[out].at[lead]
        copies.append(
            pltpu.make_async_copy(
                value.at[:, pl.ds(source, columns)],
                target.at[:, pl.ds(column, columns)],
                sems.at[n],
            )
        )
    for copy in copies:
        copy.start()
    for copy in copies:
        copy.wait()


def last_call(line, plan, out_dims, keep, got, before):
    rows, columns = keep.shape
    ins = [(a, whole(a.shape)) for a in (keep, *got)]
    aliases = {}
    if before is not None:
        aliases = {len(ins) + i: i for i in range(len(before))}
        ins += [(b, anywhere()) for b in before]
    return line.run(
        lambda *refs: last_kernel(plan, 1 + len(got), *refs),
        "add_last",
        (1,),
        ins,
        [(pltpu.HBM(d, F32), anywhere()) for d in out_dims],
        scratch=[pltpu.VMEM((rows, columns), F32), pltpu.SemaphoreType.DMA((len(plan),))],
        mib=8,
        aliases=aliases,
    )


def gelu_both(u):
    square = u * u
    t = jnp.tanh(u * (GELU_A + (GELU_A * GELU_B) * square))
    half = 0.5 + 0.5 * t
    slope = half + (0.5 * u) * (1.0 - t * t) * (GELU_A + (3.0 * GELU_A * GELU_B) * square)
    return u * half, slope


def feed_kernel(shards, sc, a2, e, wu, wd, ub, gb, du, bias, *grads):
    rows = a2.shape[0]
    step = rows // 2
    total = jnp.zeros(bias.shape, F32)
    for r in range(0, rows, step):
        u = dot(a2[r : r + step, :], wu[...]) + ub[...]
        act, slope = gelu_both(u)
        gb[r : r + step, :] = act.astype(LOW)
        low = (dot(e[r : r + step, :], wd[...], NT) * slope).astype(LOW)
        du[r : r + step, :] = low
        total = total + column_sum(low.astype(F32))
    bias[...] = total
    shards.emit(sc, dot(e[...], gb[...], TN), 0, 0, grads)
    shards.emit(sc, dot(a2[...], du[...], TN), 1, 0, grads)


def feed_call(line, shards, a2, e, w_up, w_down, up_bias, at, chunk, tile=512):
    rows, width = a2.shape
    tile = min(tile, chunk)
    first = at // tile
    one = pl.Buffered(1)
    strip = pl.BlockSpec((rows, tile), lambda i, s: (0, i))
    outs = [(shape((rows, chunk), LOW), strip), (near((rows, chunk), LOW), strip)]
    outs.append((shape((1, chunk), F32), pl.BlockSpec((1, tile), lambda i, s: (0, i))))
    for o in shards.outs():
        block = o.shape[:-1] + (tile,)
        lead = (0,) * (len(block) - 1)
        outs.append((o, pl.BlockSpec(block, lambda i, s, lead=lead: (*lead, i))))
    found = line.run(
        lambda *refs: feed_kernel(shards, *refs),
        "feed_forward",
        (chunk // tile,),
        [
            (a2, whole(a2.shape, pipeline_mode=one)),
            (e, whole(e.shape, pipeline_mode=one)),
            (w_up, pl.BlockSpec((width, tile), lambda i, s: (0, first + i))),
            (w_down, pl.BlockSpec((tile, width), lambda i, s: (first + i, 0))),
            (up_bias, pl.BlockSpec((1, tile), lambda i, s: (0, first + i))),
        ],
        outs,
        mib=40,
        flops=8 * rows * width * chunk,
    )
    return found[:3], found[3:]


def up_back_kernel(sc, *refs):
    dus, (w, out) = refs[:-2], refs[-2:]
    total, at = None, 0
    for du in dus:
        term = dot(du[...], w[:, at : at + du.shape[1]], NT)
        at += du.shape[1]
        total = term if total is None else total + term
    out[...] = total.astype(LOW)


def up_back_call(line, dus, w_up, step):
    rows = dus[0].shape[0]
    width, units = w_up.shape
    return line.run(
        up_back_kernel,
        "up_back",
        (rows // step,),
        [(du, pl.BlockSpec((step, du.shape[1]), lambda i, s: (i, 0))) for du in dus]
        + [(w_up, whole(w_up.shape, pipeline_mode=pl.Buffered(1)))],
        [(shape((rows, width), LOW), pl.BlockSpec((step, width), lambda i, s: (i, 0)))],
        mib=32,
        flops=2 * rows * width * units,
    )[0]


def own_rows(rows, step):
    blocks = rows // step

    def place(m, j, i, s):
        half = jnp.where(j == 1, s[S_T], 1 - s[S_T])
        return ((2 * m + half) * blocks + i, 0)

    def send(m, j, i, s):
        return (m, jnp.where(j == 0, i, blocks - 1), 0)

    def keep(m, j, i, s):
        return (m, jnp.where(j == 1, i, 0), 0)

    return blocks, place, send, keep


def down_kernel(sc, *refs):
    acts, (w, keep, send) = refs[:-3], refs[-3:]
    total, at = None, 0
    for act in acts:
        term = dot(act[...], w[at : at + act.shape[1], :])
        at += act.shape[1]
        total = term if total is None else total + term

    @pl.when(pl.program_id(1) == 0)
    def _():
        send[0] = total.astype(LOW)

    @pl.when(pl.program_id(1) == 1)
    def _():
        keep[0] = total.astype(LOW)


def down_call(line, count, rows, acts, w, step):
    width = w.shape[1]
    blocks, place, send, keep = own_rows(rows, step)
    out = shape((count, rows, width), LOW)
    block = (1, step, width)
    return line.run(
        down_kernel,
        "feed_down",
        (count, 2, blocks),
        [(a, pl.BlockSpec((step, a.shape[1]), place)) for a in acts]
        + [(w, whole(w.shape, pipeline_mode=pl.Buffered(1)))],
        [(out, pl.BlockSpec(block, keep)), (out, pl.BlockSpec(block, send))],
        flops=4 * count * rows * w.shape[0] * width,
    )


def mixed_kernel(sc, h, own, got, bias, out):
    m, i = pl.program_id(0), pl.program_id(1)
    rows = own.shape[1]
    first = sc[S_T] * rows * pl.num_programs(1) + i * rows
    ids = first + lax.broadcasted_iota(jnp.int32, (rows, 1), 0)
    value = h[...].astype(F32) + (own[0].astype(F32) + got[0].astype(F32)) + bias[...]
    out[0, 0] = jnp.where(ids < sc[S_LEN + m], value, 0.0).astype(LOW)


def mixed_call(line, h, own, got, bias, step):
    count, rows, width = own.shape
    blocks = rows // step
    block = pl.BlockSpec((1, step, width), lambda m, i, s: (m, i, 0))
    natural = pl.BlockSpec((step, width), lambda m, i, s: ((2 * m + s[S_T]) * blocks + i, 0))
    return line.run(
        mixed_kernel,
        "mixed_rows",
        (count, blocks),
        [(h, natural), (own, block), (got, block), (bias, whole((1, width)))],
        [
            (
                shape((count, 1, rows, width), LOW),
                pl.BlockSpec((1, 1, step, width), lambda m, i, s: (m, 0, i, 0)),
            )
        ],
    )[0]


def hidden_back_kernel(per_half, sc, da, got, h, e, gain, w, dhb, dctx, sums):
    i = pl.program_id(0)
    da2 = da[...].astype(F32) + got[...].astype(F32)
    normed, inv_std = center_rows(h[...].astype(F32))
    out_grad = e[...].astype(F32)
    low = (out_grad + norm_back(normed, inv_std, da2 * gain[...])).astype(LOW)
    dhb[...] = low
    dctx[...] = dot(low, w[...], NT).astype(LOW)
    own = jnp.where((i // per_half) % 2 == sc[S_T], 1.0, 0.0)
    terms = jnp.concatenate(
        [
            column_sum(low.astype(F32)),
            column_sum(da2 * normed),
            column_sum(da2),
            column_sum(out_grad),
        ],
        axis=0,
    )

    @pl.when(i == 0)
    def _():
        sums[...] = terms * own

    @pl.when(i > 0)
    def _():
        sums[...] += terms * own


def hidden_back_call(line, rows, da, got, h, e, gain, w, step):
    total, width = da.shape
    local = w.shape[0]
    strip = lambda wide: pl.BlockSpec((step, wide), lambda i, s: (i, 0))
    wide = strip(width)
    return line.run(
        lambda *refs: hidden_back_kernel(rows // step, *refs),
        "hidden_back",
        (total // step,),
        [(da, wide), (got, wide), (h, wide), (e, wide), (gain, whole((1, width))), (w, whole(w.shape))],
        [
            (shape((total, width), LOW), wide),
            (shape((total, local), LOW), strip(local)),
            (shape((4, width), F32), whole((4, width))),
        ],
        flops=2 * total * width * local,
    )


def attend_back_kernel(shards, pair_places, out_places, sc, q, k, v, ctx, inv, dctx, probs, a1_hbm, *refs):
    extra = [a1_hbm]
    group = len(pair_places)
    if out_places:
        extra, refs = extra + list(refs[:2]), refs[2:]
    pieces = len(shards.outs())
    refs = refs[-(3 + pieces + 1 + len(extra) + 1) :]
    dq, dk, dv = refs[:3]
    grads = refs[3 : 3 + pieces]
    rows_all = refs[3 + pieces]
    held = refs[4 + pieces : 4 + pieces + len(extra)]
    sems = refs[-1]
    j, m = pl.program_id(0), pl.program_id(1)

    def copies():
        return [
            pltpu.make_async_copy(source, target, sems.at[n])
            for n, (source, target) in enumerate(zip(extra, held))
        ]

    @pl.when((j == 0) & (m == 0))
    def _():
        for copy in copies():
            copy.start()

    slot = q.shape[1]
    lane = lax.broadcasted_iota(jnp.int32, (slot, 128), 1) < HD
    scaled = dctx[0].astype(F32) * inv[0]
    product = scaled * ctx[0].astype(F32)
    low = scaled.astype(LOW)
    key, query, value = k[0], q[0], v[0]
    cuts = splits(slot)
    per_head = []
    for h in range(2):
        here = lane if h == 0 else ~lane
        delta = jnp.sum(jnp.where(here, product, 0.0), axis=1, keepdims=True)
        masked = jnp.where(here, low, LOW(0))
        dqs, dks, dvs = [], [], []
        for lo, hi, ext in cuts:
            p = probs[0, h, lo:hi, :ext]
            dp = dot(masked[lo:hi], value[:ext], NT)
            ds = (p.astype(F32) * (dp - delta[lo:hi])).astype(LOW)
            dqs.append(dot(ds, key[:ext]))
            dks.append(dot(ds, query[lo:hi], TN))
            dvs.append(dot(p, low[lo:hi], TN))
        first = cuts[0][2]
        join = lambda two: jnp.concatenate([two[0] + two[1][:first], two[1][first:]], axis=0)
        per_head.append((jnp.concatenate(dqs, axis=0), join(dks), join(dvs)))
    root = 1.0 / math.sqrt(HD)
    start = pl.multiple_of(m * slot, slot)
    for c, (ref, scale) in enumerate(((dq, root), (dk, root), (dv, 1.0))):
        both = (jnp.where(lane, per_head[0][c], per_head[1][c]) * scale).astype(LOW)
        ref[0] = both
        rows_all[j, pl.ds(start, slot), c * 128 : (c + 1) * 128] = both

    @pl.when((m == pl.num_programs(1) - 1) & (j == group - 1))
    def _():
        for copy in copies():
            copy.wait()
        for g in range(group):
            side, column = pair_places[g]
            shards.emit(sc, dot(held[0][...], rows_all[g], TN), side, column, grads)
        for side, column, first, wide in out_places:
            term = dot(held[1][...], held[2][:, first : first + wide], TN)
            shards.emit(sc, term, side, column, grads)


def attend_back_call(
    line, shards, at, pair_places, out_places, qkv, ctx, inv, dctx, probs, a1, out_pair=(), before=None
):
    count, slot, local = ctx.shape
    group = len(pair_places)
    pair = pl.BlockSpec((1, slot, 128), lambda j, m, s: (m, 0, at + j))
    ins = [(a, pair) for a in (*qkv, ctx, inv, dctx)]
    ins.append((probs, pl.BlockSpec((1, 2, slot, slot), lambda j, m, s: (m, at + j, 0, 0))))
    extra = [a1, *out_pair]
    ins += [(a, anywhere()) for a in extra]
    aliases = {}
    if before is not None:
        aliases = {len(ins) + i: i for i in range(3)}
        ins += [(b, anywhere()) for b in before]
    found = line.run(
        lambda *refs: attend_back_kernel(shards, pair_places, out_places, *refs),
        "attend_back",
        (group, count),
        ins,
        [(near((count, slot, local), LOW), pair)] * 3 + [(o, whole(o.shape)) for o in shards.outs()],
        scratch=[pltpu.VMEM((group, count * slot, 384), LOW)]
        + [pltpu.VMEM(a.shape, LOW) for a in extra]
        + [pltpu.SemaphoreType.DMA((len(extra),))],
        mib=32,
        flops=12e9,
        aliases=aliases,
    )
    return found[:3], found[3:]


def rows_back_kernel(sc, dq, dk, dv, w, x, x_far, keep, send, sums):
    m, j, i = pl.program_id(0), pl.program_id(1), pl.program_id(2)
    total = dot(dq[...], w[0], NT) + dot(dk[...], w[1], NT) + dot(dv[...], w[2], NT)

    @pl.when(j == 0)
    def _():
        send[0] = total.astype(LOW)

    @pl.when(j == 1)
    def _():
        keep[0] = total.astype(LOW)

    mine = jnp.full(x.shape[1:], j) == 1
    normed, _ = center_rows(jnp.where(mine, x[0], x_far[0]).astype(F32))
    terms = jnp.concatenate([column_sum(total * normed), column_sum(total)], axis=0)
    start = (m == 0) & (j == 0) & (i == 0)

    @pl.when(start)
    def _():
        sums[...] = terms

    @pl.when(~start)
    def _():
        sums[...] += terms


def rows_back_call(line, grads, w, x, x_far, step):
    count, rows, width = x.shape
    total, local = 2 * count * rows, w.shape[2]
    blocks, place, send, keep = own_rows(rows, step)
    out = shape((count, rows, width), LOW)
    block = (1, step, width)
    return line.run(
        rows_back_kernel,
        "rows_back",
        (count, 2, blocks),
        [(g, pl.BlockSpec((step, local), place)) for g in grads]
        + [(w, whole(w.shape, pipeline_mode=pl.Buffered(1)))]
        + [(v, pl.BlockSpec((1, step, width), lambda m, j, i, s: (m, i, 0))) for v in (x, x_far)],
        [
            (out, pl.BlockSpec(block, keep)),
            (out, pl.BlockSpec(block, send)),
            (shape((2, width), F32), whole((2, width))),
        ],
        flops=6 * total * width * local,
    )


def tokens_back_kernel(sc, x, dh, own, got, gain, out):
    normed, inv_std = center_rows(x[0].astype(F32))
    da1 = own[0].astype(F32) + got[0].astype(F32)
    back = norm_back(normed, inv_std, da1 * gain[...])
    out[0, 0] = (dh[...].astype(F32) + back).astype(LOW)


def tokens_back_call(line, x, dh, own, got, gain, step):
    count, rows, width = own.shape
    blocks = rows // step
    block = pl.BlockSpec((1, step, width), lambda m, i, s: (m, i, 0))
    natural = pl.BlockSpec((step, width), lambda m, i, s: ((2 * m + s[S_T]) * blocks + i, 0))
    return line.run(
        tokens_back_kernel,
        "tokens_back",
        (count, blocks),
        [(x, block), (dh, natural), (own, block), (got, block), (gain, whole((1, width)))],
        [
            (
                shape((count, 1, rows, width), LOW),
                pl.BlockSpec((1, 1, step, width), lambda m, i, s: (m, 0, i, 0)),
            )
        ],
    )[0]


def swap(value):
    return lax.ppermute(value, "tensor", [(0, 1), (1, 0)])


def vector_kernel(sc, one, two, out):
    out[...] = one[...] + two[...]


class Vectors:
    def __init__(self, line, dp_count, values, shared):
        self.line, self.dp_count, self.values = line, dp_count, values
        rows = lax.broadcasted_iota(jnp.int32, (values.shape[0], 1), 0)
        self.got = swap(jnp.where(rows < shared, values, 0.0))
        self.mask = 1
        if dp_count & (dp_count - 1):
            self.values, self.got = lax.psum(values + self.got, "dp"), None

    def advance(self):
        if self.got is None:
            return
        dims = self.values.shape
        self.values = self.line.run(
            vector_kernel,
            "add_vectors",
            (1,),
            [(a, whole(dims)) for a in (self.values, self.got)],
            [(jax.ShapeDtypeStruct(dims, F32), whole(dims))],
            mib=8,
        )[0]
        self.got = move(self.values, self.dp_count, self.mask) if self.mask < self.dp_count else None
        self.mask *= 2


def head_places(pairs, out_width):
    sides = [0, 0]
    places, out_places = [], []
    for pair in range(pairs):
        side = pair * 2 // pairs
        places.append((side, sides[side]))
        sides[side] += 384
    for side in range(2 if out_width else 0):
        wide = out_width // 2
        out_places.append((side, sides[side], side * wide, wide))
        sides[side] += wide
    return places, out_places, sides


def local(
    tokens,
    d_mixed,
    phone_len,
    frame_len,
    ln1_gain,
    ln1_bias,
    w_qkv,
    w_out,
    attn_bias,
    ln2_gain,
    ln2_bias,
    w_up,
    up_bias,
    w_down,
    down_bias,
):
    count, _, rows, width = tokens.shape
    dp_count = lax.axis_size("dp")
    slot = 2 * rows
    local_width = w_qkv.shape[2]
    units = w_up.shape[1]
    shard_rows = width // dp_count
    step = rows
    row = lambda v: v.reshape(1, -1)
    x, dm = tokens[:, 0], d_mixed[:, 0]
    phones = phone_len[:, 0]
    sc = jnp.concatenate(
        [
            jnp.stack([lax.axis_index("tensor"), lax.axis_index("dp")]).astype(jnp.int32),
            phones + frame_len[:, 0],
            phones,
        ]
    )
    line = Line(sc)
    w3 = jnp.transpose(w_qkv, (1, 0, 2))
    g1, b1, g2, b2 = row(ln1_gain), row(ln1_bias), row(ln2_gain), row(ln2_bias)
    flat = lambda v: v.reshape(count * slot, v.shape[-1])

    x_far, dm_far, w_out_far = swap(x), swap(dm), swap(w_out)
    x_near, w_near = bring([x, w3])
    a1, *qkv, ctx, probs, inv = front_call(line, x_near, x_far, g1, b1, w_near)
    ctx_far = swap(ctx)
    en = mark_call(line, dm, dm_far)
    h, a2 = project_call(line, ctx, ctx_far, w_out, w_out_far, x, x_far, row(attn_bias), g2, b2)

    chunks = (units // 2, units // 2)
    reds, acts, dus, up_sums, at = [], [], [], [], 0
    for chunk in chunks:
        shards = Shards(dp_count, width, (chunk, chunk))
        (act, du, up_sum), grads = feed_call(
            line, shards, a2, en, w_up, w_down, row(up_bias), at, chunk
        )
        reds.append(Reduction(line, shards, grads))
        acts.append(act)
        dus.append(du)
        up_sums.append(up_sum)
        at += chunk
    da = up_back_call(line, dus, w_up, step)
    da_far = swap(da)
    red1, red2 = reds
    red1.advance()
    dhb, dctx, hidden_sums = hidden_back_call(line, rows, da, da_far, h, en, g2, w_out, step)
    own_down, far_down = down_call(line, count, rows, acts, w_down, step)
    far_down = swap(far_down)
    red2.advance()
    mixed = mixed_call(line, h, own_down, far_down, row(down_bias), step)
    red1.advance()

    pairs = local_width // 128
    dctx = dctx.reshape(count, slot, local_width)
    half = pairs // 2
    places3, outs3, sides3 = head_places(half, local_width)
    places4, _, sides4 = head_places(pairs - half, 0)
    shards3, shards4 = Shards(dp_count, width, sides3), Shards(dp_count, width, sides4)
    rest = (qkv, ctx, inv, dctx, probs, flat(a1))
    grads, parts = attend_back_call(line, shards3, 0, places3, outs3, *rest, (dhb, flat(ctx)))
    red3 = Reduction(line, shards3, parts)
    red2.advance()
    red1.advance()
    grads, parts = attend_back_call(line, shards4, half, places4, [], *rest, (), grads)
    red4 = Reduction(line, shards4, parts)
    feed_dims = [(shard_rows, units)] * 2
    feed_places = lambda at, chunk: [(n, None, at, n * chunk, chunk) for n in range(2)]
    feed_grads = red1.finish(feed_places(0, chunks[0]), feed_dims)
    red3.advance()
    red2.advance()
    own, far, token_sums = rows_back_call(
        line, [flat(g) for g in grads], w3, x, x_far, step
    )
    far = swap(far)
    up_rows = jnp.concatenate(up_sums, axis=1).reshape(-1, width)
    sums = Vectors(line, dp_count, jnp.concatenate([token_sums, hidden_sums, up_rows]), 6)
    red4.advance()
    sums.advance()
    red3.advance()
    d_tokens = tokens_back_call(line, x, dhb, own, far, g1, step)
    red4.advance()
    sums.advance()
    grad_down, grad_up = red2.finish(feed_places(chunks[0], chunks[1]), feed_dims, feed_grads)
    red3.advance()
    red4.advance()
    sums.advance()

    def finish(red, at, pair_places, out_places, sides, dims, before=None):
        starts = [sum(sides[:n]) for n in range(len(sides))]
        places = []
        for g, (side, column) in enumerate(pair_places):
            for c in range(3):
                places.append((0, c, (at + g) * 128, starts[side] + column + c * 128, 128))
        for side, column, first, wide in out_places:
            places.append((1, None, first, starts[side] + column, wide))
        return red.finish(places, dims, before)

    dims = [(3, shard_rows, local_width), (shard_rows, local_width)]
    grad_qkv, grad_out = finish(red3, 0, places3, outs3, sides3, dims)
    sums.advance()
    (grad_qkv,) = finish(red4, half, places4, [], sides4, dims[:1], [grad_qkv])
    while sums.got is not None:
        sums.advance()
    vectors = sums.values

    return (
        mixed,
        d_tokens,
        vectors[0],
        vectors[1],
        jnp.transpose(grad_qkv, (1, 0, 2)),
        grad_out.T,
        vectors[2],
        vectors[3],
        vectors[4],
        grad_up,
        vectors[6:].reshape(-1),
        grad_down.T,
        vectors[5],
    )


def solution(mesh):
    in_specs = (
        P(None, "dp", "tensor", None),
        P(None, "dp", "tensor", None),
        P(None, "dp"),
        P(None, "dp"),
        P(),
        P(),
        P(None, None, "tensor"),
        P("tensor", None),
        P(),
        P(),
        P(),
        P(None, "tensor"),
        P("tensor"),
        P("tensor", None),
        P(),
    )
    out_specs = (
        P(None, "dp", "tensor", None),
        P(None, "dp", "tensor", None),
        P(),
        P(),
        P("dp", None, "tensor"),
        P("tensor", "dp"),
        P(),
        P(),
        P(),
        P("dp", "tensor"),
        P("tensor"),
        P("tensor", "dp"),
        P(),
    )
    return jax.shard_map(local, mesh=mesh, in_specs=in_specs, out_specs=out_specs, check_vma=False)
```

```python
import math

import jax
import jax.numpy as jnp
from jax import lax
from jax.experimental import pallas as pl
from jax.experimental.pallas import tpu as pltpu
from jax.sharding import PartitionSpec as P

HD = 64
EPS = 1e-05
LOW = jnp.bfloat16
F32 = jnp.float32
NT = (((1,), (1,)), ((), ()))
TN = (((0,), (0,)), ((), ()))
GELU_A = math.sqrt(2.0 / math.pi)
GELU_B = 0.044715

S_T, S_DP, S_LEN, S_PH = 0, 1, 2, 4


def dot(a, b, dims=(((1,), (0,)), ((), ()))):
    return lax.dot_general(a, b, dims, preferred_element_type=F32)


def shape(dims, dtype):
    if math.prod(dims) * jnp.dtype(dtype).itemsize >= 1 << 17:
        return pltpu.HBM(dims, dtype)
    return jax.ShapeDtypeStruct(dims, dtype)


def near(dims, dtype):
    return pltpu.VMEM(dims, dtype)


def whole(dims, **more):
    return pl.BlockSpec(dims, lambda *_: (0,) * len(dims), **more)


def anywhere():
    return pl.BlockSpec(memory_space=pl.ANY)


ADD_FLOPS = 3e10


class Line:
    def __init__(self, sc):
        self.sc = sc
        self.token = jnp.zeros((8, 128), F32)
        self.pending, self.carried = [], []

    def run(self, kernel, name, grid, ins, outs, scratch=(), mib=24, flops=0, aliases=None):
        count_in, count_out = len(ins), len(outs)
        through, self.pending = [self.token, *self.pending], []
        extra = len(through)

        def body(*refs):
            mid = 1 + count_in
            end = mid + extra + count_out
            kernel(*refs[:mid], *refs[mid + extra : end], *refs[end + extra :])

        arrays = [a for a, _ in ins]
        nbytes = sum(math.prod(a.shape) * a.dtype.itemsize for a in arrays)
        aliases = {1 + i: o for i, o in (aliases or {}).items()}
        aliases.update({1 + count_in + n: count_out + n for n in range(extra)})
        found = pl.pallas_call(
            body,
            grid_spec=pltpu.PrefetchScalarGridSpec(
                num_scalar_prefetch=1,
                grid=grid,
                in_specs=[s for _, s in ins] + [anywhere()] * extra,
                out_specs=[s for _, s in outs] + [anywhere()] * extra,
                scratch_shapes=list(scratch),
            ),
            out_shape=[o for o, _ in outs]
            + [jax.ShapeDtypeStruct(t.shape, t.dtype) for t in through],
            input_output_aliases=aliases,
            compiler_params=pltpu.CompilerParams(vmem_limit_bytes=mib << 20),
            cost_estimate=pl.CostEstimate(
                flops=int(flops * 1), bytes_accessed=int(nbytes * 1), transcendentals=0
            ),
            name=name,
        )(self.sc, *arrays, *through)
        self.token, self.carried = found[count_out], list(found[count_out + 1 :])
        return found[:count_out]


def center_rows(values):
    center = values - jnp.mean(values, axis=-1, keepdims=True)
    inv_std = lax.rsqrt(jnp.mean(center * center, axis=-1, keepdims=True) + EPS)
    return center * inv_std, inv_std


def norm_back(normed, inv_std, t):
    return inv_std * (
        t
        - jnp.mean(t, axis=-1, keepdims=True)
        - normed * jnp.mean(t * normed, axis=-1, keepdims=True)
    )


def column_sum(values):
    return jnp.sum(values, axis=0, keepdims=True)


def bring(arrays):
    vm = pl.BlockSpec(memory_space=pltpu.VMEM)
    hbm = pl.BlockSpec(memory_space=pltpu.HBM)

    def kernel(*refs):
        count = len(arrays)
        sems = refs[-1]
        copies = [
            pltpu.make_async_copy(source, target, sems.at[n])
            for n, (source, target) in enumerate(zip(refs[:count], refs[count:-1]))
        ]
        for copy in copies:
            copy.start()
        for copy in copies:
            copy.wait()

    return pl.pallas_call(
        kernel,
        in_specs=[hbm] * len(arrays),
        out_specs=[vm] * len(arrays),
        out_shape=[near(a.shape, a.dtype) for a in arrays],
        scratch_shapes=[pltpu.SemaphoreType.DMA((len(arrays),))],
        compiler_params=pltpu.CompilerParams(vmem_limit_bytes=4 << 20),
        name="bring",
    )(*arrays)


def splits(slot):
    half = slot // 2
    cut = -(-half // 128) * 128
    return [(0, cut, cut), (cut, slot, slot)]


def front_kernel(
    sc, x, x_far, gain, shift, w,
    a1, q, k, v, ctx, probs, inv,
    low, qkv, bias, sem,
):
    m, j = pl.program_id(0), pl.program_id(1)
    rows = x.shape[1]
    slot = 2 * rows
    local = w.shape[2]
    here = pl.multiple_of(sc[S_T] * rows, rows)
    there = pl.multiple_of((1 - sc[S_T]) * rows, rows)

    def copy():
        return pltpu.make_async_copy(low, a1.at[m], sem.at[0])

    @pl.when(j == 0)
    def _():
        for source, at in ((x, here), (x_far, there)):
            normed, _ = center_rows(source[0].astype(F32))
            low[pl.ds(at, rows), :] = (normed * gain[...] + shift[...]).astype(LOW)
        copy().start()
        for c in range(3):
            qkv[:, c * local : (c + 1) * local] = dot(low[...], w[c]).astype(LOW)
        qi = lax.broadcasted_iota(jnp.int32, (slot, slot), 0)
        ki = lax.broadcasted_iota(jnp.int32, (slot, slot), 1)
        bias[...] = jnp.where((ki <= qi) | (ki < sc[S_PH + m]), 0.0, -1e30)

    def part(c):
        return qkv[:, pl.ds(pl.multiple_of(c * local + j * 128, 128), 128)]

    lane = lax.broadcasted_iota(jnp.int32, (slot, 128), 1) < HD
    query_all, key, value = part(0), part(1), part(2)
    q[0], k[0], v[0] = query_all, key, value
    widened = jnp.concatenate([value, jnp.ones_like(value)], axis=1)
    for lo, hi, ext in splits(slot):
        query = query_all[lo:hi] * LOW(1.0 / math.sqrt(HD))
        first = lane[lo:hi]
        sums = []
        for h in range(2):
            masked = jnp.where(first if h == 0 else ~first, query, LOW(0))
            s = dot(masked, key[:ext], NT) + bias[lo:hi, :ext]
            p = jnp.exp(s - jnp.max(s, axis=1, keepdims=True)).astype(LOW)
            probs[0, h, lo:hi, :ext] = p
            sums.append(dot(p, widened[:ext]))
        total = jnp.where(first, sums[0][:, :128], sums[1][:, :128])
        scale = 1.0 / jnp.where(first, sums[0][:, 128:], sums[1][:, 128:])
        ctx[0, lo:hi, :] = (total * scale).astype(LOW)
        inv[0, lo:hi, :] = scale

    @pl.when(j == pl.num_programs(1) - 1)
    def _():
        copy().wait()


def front_call(line, x, x_far, gain, shift, w):
    count, rows, width = x.shape
    slot, local = 2 * rows, w.shape[2]
    heads = local // HD
    own = pl.BlockSpec((1, rows, width), lambda m, j, s: (m, 0, 0))
    pair = pl.BlockSpec((1, slot, 128), lambda m, j, s: (m, 0, j))
    natural = shape((count, slot, width), LOW)
    heads_out = shape((count, slot, local), LOW)
    return line.run(
        front_kernel,
        "norm_attend",
        (count, local // 128),
        [(x, own), (x_far, own)]
        + [(gain, whole((1, width))), (shift, whole((1, width)))]
        + [(w, whole(w.shape, pipeline_mode=pl.Buffered(1)))],
        [(natural, anywhere())]
        + [(heads_out, pair)] * 4
        + [
            (
                shape((count, heads, slot, slot), LOW),
                pl.BlockSpec((1, 2, slot, slot), lambda m, j, s: (m, j, 0, 0)),
            ),
            (shape((count, slot, local), F32), pair),
        ],
        scratch=[
            pltpu.VMEM((slot, width), LOW),
            pltpu.VMEM((slot, 3 * local), LOW),
            pltpu.VMEM((slot, slot), F32),
            pltpu.SemaphoreType.DMA((1,)),
        ],
        mib=30,
        flops=2e10,
    )


def mark_kernel(sc, dm, dm_far, e):
    m, half = pl.program_id(0), pl.program_id(1)
    rows = dm.shape[1]
    mine = jnp.full(dm.shape[1:], half) == sc[S_T]
    ids = half * rows + lax.broadcasted_iota(jnp.int32, (rows, 1), 0)
    e[...] = jnp.where(ids < sc[S_LEN + m], jnp.where(mine, dm[0], dm_far[0]), LOW(0))


def mark_call(line, dm, dm_far):
    count, rows, width = dm.shape
    held = pl.BlockSpec((1, rows, width), lambda m, i, s: (m, 0, 0))
    return line.run(
        mark_kernel,
        "mark_rows",
        (count, 2),
        [(dm, held), (dm_far, held)],
        [(near((2 * count * rows, width), LOW), pl.BlockSpec((rows, width), lambda m, i, s: (2 * m + i, 0)))],
    )[0]


def project_kernel(sc, ctx, far, w, w_far, x, x_far, bias, gain, shift, h, a2):
    m, half = pl.program_id(0), pl.program_id(1)
    mine = jnp.full(x.shape[1:], half) == sc[S_T]
    both = dot(ctx[0], w[...]) + dot(far[0], w_far[...])
    hidden = jnp.where(mine, x[0], x_far[0]).astype(F32) + both + bias[...]
    h[...] = hidden.astype(LOW)
    normed, _ = center_rows(hidden)
    a2[...] = (normed * gain[...] + shift[...]).astype(LOW)


def project_call(line, ctx, far, w, w_far, x, x_far, bias, gain, shift):
    count, rows, width = x.shape
    local = ctx.shape[2]
    strip = pl.BlockSpec((1, rows, local), lambda m, i, s: (m, i, 0))
    held = pl.BlockSpec((1, rows, width), lambda m, i, s: (m, 0, 0))
    one = whole((1, width))
    out = (shape((2 * count * rows, width), LOW), pl.BlockSpec((rows, width), lambda m, i, s: (2 * m + i, 0)))
    return line.run(
        project_kernel,
        "project",
        (count, 2),
        [(ctx, strip), (far, strip), (w, whole(w.shape)), (w_far, whole(w.shape))]
        + [(x, held), (x_far, held)]
        + [(bias, one), (gain, one), (shift, one)],
        [out, (near((2 * count * rows, width), LOW), out[1])],
        flops=4 * count * rows * width * width,
    )


class Shards:
    def __init__(self, dp_count, width, sides):
        self.dp_count = dp_count
        self.width = width
        self.rows = width // dp_count
        self.sides = sides
        self.bits = dp_count.bit_length() - 1
        self.halving = dp_count == 1 << self.bits and self.bits > 2 and self.rows % 16 == 0
        late = list(range(3, self.bits))
        orders = ([0, 1, 2], [1, 0, 2]) if len(sides) == 2 else ([0, 1, 2], [1, 2, 0], [2, 0, 1])
        self.orders = [order + late for order in orders]

    def outs(self):
        if not self.halving:
            return [jax.ShapeDtypeStruct((self.width, n), LOW) for n in self.sides]
        return [
            kind((self.dp_count // 2, self.rows, n), LOW)
            for n in self.sides
            for kind in (pltpu.HBM, near if sum(self.sides) < 0 else pltpu.HBM)
        ]

    def emit(self, sc, value, side, at, refs):
        value = value.astype(LOW)
        span = slice(at, at + value.shape[1])
        if not self.halving:
            refs[side][:, span] = value
            return
        send, keep = refs[2 * side], refs[2 * side + 1]
        blocks = value.reshape(self.dp_count, self.rows, value.shape[1])
        order = self.orders[side]
        mine = jnp.full((self.rows, value.shape[1]), (sc[S_DP] >> order[0]) & 1) == 1
        for i in range(self.dp_count // 2):
            at_zero = sum(((i >> n) & 1) << bit for n, bit in enumerate(order[1:]))
            zero = blocks[at_zero]
            one = blocks[at_zero + (1 << order[0])]
            send[i, :, span] = jnp.where(mine, zero, one)
            keep[i, :, span] = jnp.where(mine, one, zero)


def split_kernel(bits, sc, *refs):
    sides = len(bits)
    ins, outs = refs[: 2 * sides], refs[2 * sides :]
    joined = len(outs) == 2
    at = 0
    for n, bit in enumerate(bits):
        keep, got = ins[2 * n], ins[2 * n + 1]
        send_out, keep_out = outs[:2] if joined else outs[2 * n : 2 * n + 2]
        columns = keep.shape[2]
        mine = (sc[S_DP] >> bit) & 1
        for j, ref in ((1 - mine, send_out), (mine, keep_out)):
            total = (keep[j].astype(F32) + got[j].astype(F32)).astype(LOW)
            ref[0, :, at : at + columns] = total
        if joined:
            at += columns


def far_keep_kernel(bits, sc, *refs):
    sides = len(bits)
    keeps, gots, outs = refs[:sides], refs[sides : 2 * sides], refs[2 * sides : 4 * sides]
    held, sems = refs[4 * sides : 5 * sides], refs[-1]
    i, blocks = pl.program_id(0), keeps[0].shape[0] // 2

    def copy(n, side):
        span = pl.ds(2 * n, 2)
        return pltpu.make_async_copy(keeps[side].at[span], held[side].at[span], sems.at[n, side])

    @pl.when(i == 0)
    def _():
        for n in range(blocks):
            for side in range(sides):
                copy(n, side).start()

    for n in range(blocks):

        @pl.when(i == n)
        def _():
            for side in range(sides):
                copy(n, side).wait()

    for side, bit in enumerate(bits):
        mine = (sc[S_DP] >> bit) & 1
        for j, ref in ((1 - mine, outs[2 * side]), (mine, outs[2 * side + 1])):
            keep = held[side][2 * i + j]
            ref[0] = (keep.astype(F32) + gots[side][j].astype(F32)).astype(LOW)


def far_keep_call(line, bits, args, flops):
    blocks, rows, _ = args[0].shape
    keeps, gots = args[::2], args[1::2]
    return line.run(
        lambda *refs: far_keep_kernel(bits, *refs),
        "add_far",
        (blocks // 2,),
        [(a, pl.BlockSpec(memory_space=pltpu.HBM)) for a in keeps]
        + [(a, pl.BlockSpec((2, rows, a.shape[2]), lambda i, s: (i, 0, 0))) for a in gots],
        [
            (
                jax.ShapeDtypeStruct((blocks // 2, rows, a.shape[2]), LOW),
                pl.BlockSpec((1, rows, a.shape[2]), lambda i, s: (i, 0, 0)),
            )
            for a in keeps
            for _ in range(2)
        ],
        scratch=[pltpu.VMEM(a.shape, LOW) for a in keeps]
        + [pltpu.SemaphoreType.DMA((blocks // 2, len(keeps)))],
        mib=12,
        flops=flops,
    )


def split_call(line, bits, args, widths, name, flops):
    blocks, rows, _ = args[0].shape
    if len(widths) == len(bits) > 1 and sum(math.prod(a.shape) for a in args) >= 1 << 21:
        return far_keep_call(line, bits, args, flops)
    return line.run(
        lambda *refs: split_kernel(bits, *refs),
        name,
        (blocks // 2,),
        [(a, pl.BlockSpec((2, rows, a.shape[2]), lambda i, s: (i, 0, 0))) for a in args],
        [
            (
                jax.ShapeDtypeStruct((blocks // 2, rows, n), LOW),
                pl.BlockSpec((1, rows, n), lambda i, s: (i, 0, 0)),
            )
            for n in widths
            for _ in range(2)
        ],
        mib=12,
        flops=flops,
    )


def move(value, dp_count, mask):
    return lax.ppermute(value, "dp", [(i, i ^ mask) for i in range(dp_count)])


class Reduction:
    def __init__(self, line, shards, arrays):
        self.line, self.shards = line, shards
        self.step = 0
        if not shards.halving:
            self.keep = jnp.concatenate(
                [
                    lax.psum_scatter(a.astype(F32), "dp", scatter_dimension=0, tiled=True)
                    for a in arrays
                ],
                axis=1,
            )
            self.got, self.step = [], shards.bits
            return
        self.orders = shards.orders
        self.sides = shards.sides
        self.keep = arrays[1::2]
        self.send(arrays[::2])

    def send(self, arrays):
        count = self.shards.dp_count
        self.got = [
            lax.ppermute(a, "dp", [(i, i ^ (1 << order[self.step])) for i in range(count)])
            for a, order in zip(arrays, self.orders)
        ]
        self.step += 1

    def advance(self, flops=ADD_FLOPS):
        if self.step >= self.shards.bits:
            return
        bits = [order[self.step] for order in self.orders]
        joined = all(order[self.step :] == self.orders[0][self.step :] for order in self.orders)
        args = [a for pair in zip(self.keep, self.got) for a in pair]
        widths = [sum(self.sides)] if joined else self.sides
        found = split_call(self.line, bits, args, widths, "add_split", flops)
        if joined:
            self.orders, self.sides = self.orders[:1], widths
        self.keep = found[1::2]
        self.send(found[::2])

    def finish(self, plan, out_dims, before=None):
        while self.step < self.shards.bits:
            self.advance()
        keep, got = self.keep, self.got
        if self.shards.halving:
            keep, got = (v[0].reshape(v[0].shape[-2:]) for v in (keep, got))
            got = [got]
        return last_call(self.line, plan, out_dims, keep, got, before)


def last_kernel(plan, terms, sc, *refs):
    outs, value, sems = refs[-2 - len({p[0] for p in plan}) : -2], refs[-2], refs[-1]
    total = refs[0][...].astype(F32)
    for ref in refs[1:terms]:
        total = total + ref[...].astype(F32)
    value[...] = total
    copies = []
    for n, (out, lead, column, source, columns) in enumerate(plan):
        target = outs[out] if lead is None else outs[out].at[lead]
        copies.append(
            pltpu.make_async_copy(
                value.at[:, pl.ds(source, columns)],
                target.at[:, pl.ds(column, columns)],
                sems.at[n],
            )
        )
    for copy in copies:
        copy.start()
    for copy in copies:
        copy.wait()


def last_call(line, plan, out_dims, keep, got, before):
    rows, columns = keep.shape
    ins = [(a, whole(a.shape)) for a in (keep, *got)]
    aliases = {}
    if before is not None:
        aliases = {len(ins) + i: i for i in range(len(before))}
        ins += [(b, anywhere()) for b in before]
    return line.run(
        lambda *refs: last_kernel(plan, 1 + len(got), *refs),
        "add_last",
        (1,),
        ins,
        [(pltpu.HBM(d, F32), anywhere()) for d in out_dims],
        scratch=[pltpu.VMEM((rows, columns), F32), pltpu.SemaphoreType.DMA((len(plan),))],
        mib=8,
        aliases=aliases,
    )


def gelu_both(u):
    square = u * u
    t = jnp.tanh(u * (GELU_A + (GELU_A * GELU_B) * square))
    half = 0.5 + 0.5 * t
    slope = half + (0.5 * u) * (1.0 - t * t) * (GELU_A + (3.0 * GELU_A * GELU_B) * square)
    return u * half, slope


def feed_kernel(shards, sc, a2, e, wu, wd, ub, gb, du, bias, *grads):
    rows = a2.shape[0]
    step = rows // 2
    total = jnp.zeros(bias.shape, F32)
    for r in range(0, rows, step):
        u = dot(a2[r : r + step, :], wu[...]) + ub[...]
        act, slope = gelu_both(u)
        gb[r : r + step, :] = act.astype(LOW)
        low = (dot(e[r : r + step, :], wd[...], NT) * slope).astype(LOW)
        du[r : r + step, :] = low
        total = total + column_sum(low.astype(F32))
    bias[...] = total
    shards.emit(sc, dot(e[...], gb[...], TN), 0, 0, grads)
    shards.emit(sc, dot(a2[...], du[...], TN), 1, 0, grads)


def feed_call(line, shards, a2, e, w_up, w_down, up_bias, at, chunk, tile=512):
    rows, width = a2.shape
    tile = min(tile, chunk)
    first = at // tile
    one = pl.Buffered(1)
    strip = pl.BlockSpec((rows, tile), lambda i, s: (0, i))
    outs = [(shape((rows, chunk), LOW), strip), (near((rows, chunk), LOW), strip)]
    outs.append((shape((1, chunk), F32), pl.BlockSpec((1, tile), lambda i, s: (0, i))))
    for o in shards.outs():
        block = o.shape[:-1] + (tile,)
        lead = (0,) * (len(block) - 1)
        outs.append((o, pl.BlockSpec(block, lambda i, s, lead=lead: (*lead, i))))
    found = line.run(
        lambda *refs: feed_kernel(shards, *refs),
        "feed_forward",
        (chunk // tile,),
        [
            (a2, whole(a2.shape, pipeline_mode=one)),
            (e, whole(e.shape, pipeline_mode=one)),
            (w_up, pl.BlockSpec((width, tile), lambda i, s: (0, first + i))),
            (w_down, pl.BlockSpec((tile, width), lambda i, s: (first + i, 0))),
            (up_bias, pl.BlockSpec((1, tile), lambda i, s: (0, first + i))),
        ],
        outs,
        mib=40,
        flops=8 * rows * width * chunk,
    )
    return found[:3], found[3:]


def up_back_kernel(sc, *refs):
    dus, (w, out) = refs[:-2], refs[-2:]
    total, at = None, 0
    for du in dus:
        term = dot(du[...], w[:, at : at + du.shape[1]], NT)
        at += du.shape[1]
        total = term if total is None else total + term
    out[...] = total.astype(LOW)


def up_back_call(line, dus, w_up, step):
    rows = dus[0].shape[0]
    width, units = w_up.shape
    return line.run(
        up_back_kernel,
        "up_back",
        (rows // step,),
        [(du, pl.BlockSpec((step, du.shape[1]), lambda i, s: (i, 0))) for du in dus]
        + [(w_up, whole(w_up.shape, pipeline_mode=pl.Buffered(1)))],
        [(shape((rows, width), LOW), pl.BlockSpec((step, width), lambda i, s: (i, 0)))],
        mib=32,
        flops=2 * rows * width * units,
    )[0]


def own_rows(rows, step):
    blocks = rows // step

    def place(m, j, i, s):
        half = jnp.where(j == 1, s[S_T], 1 - s[S_T])
        return ((2 * m + half) * blocks + i, 0)

    def send(m, j, i, s):
        return (m, jnp.where(j == 0, i, blocks - 1), 0)

    def keep(m, j, i, s):
        return (m, jnp.where(j == 1, i, 0), 0)

    return blocks, place, send, keep


def down_kernel(sc, *refs):
    acts, (w, keep, send) = refs[:-3], refs[-3:]
    total, at = None, 0
    for act in acts:
        term = dot(act[...], w[at : at + act.shape[1], :])
        at += act.shape[1]
        total = term if total is None else total + term

    @pl.when(pl.program_id(1) == 0)
    def _():
        send[0] = total.astype(LOW)

    @pl.when(pl.program_id(1) == 1)
    def _():
        keep[0] = total.astype(LOW)


def down_call(line, count, rows, acts, w, step):
    width = w.shape[1]
    blocks, place, send, keep = own_rows(rows, step)
    out = shape((count, rows, width), LOW)
    block = (1, step, width)
    return line.run(
        down_kernel,
        "feed_down",
        (count, 2, blocks),
        [(a, pl.BlockSpec((step, a.shape[1]), place)) for a in acts]
        + [(w, whole(w.shape, pipeline_mode=pl.Buffered(1)))],
        [(out, pl.BlockSpec(block, keep)), (out, pl.BlockSpec(block, send))],
        flops=4 * count * rows * w.shape[0] * width,
    )


def mixed_kernel(sc, h, own, got, bias, out):
    m, i = pl.program_id(0), pl.program_id(1)
    rows = own.shape[1]
    first = sc[S_T] * rows * pl.num_programs(1) + i * rows
    ids = first + lax.broadcasted_iota(jnp.int32, (rows, 1), 0)
    value = h[...].astype(F32) + (own[0].astype(F32) + got[0].astype(F32)) + bias[...]
    out[0, 0] = jnp.where(ids < sc[S_LEN + m], value, 0.0).astype(LOW)


def mixed_call(line, h, own, got, bias, step):
    count, rows, width = own.shape
    blocks = rows // step
    block = pl.BlockSpec((1, step, width), lambda m, i, s: (m, i, 0))
    natural = pl.BlockSpec((step, width), lambda m, i, s: ((2 * m + s[S_T]) * blocks + i, 0))
    return line.run(
        mixed_kernel,
        "mixed_rows",
        (count, blocks),
        [(h, natural), (own, block), (got, block), (bias, whole((1, width)))],
        [
            (
                shape((count, 1, rows, width), LOW),
                pl.BlockSpec((1, 1, step, width), lambda m, i, s: (m, 0, i, 0)),
            )
        ],
    )[0]


def hidden_back_kernel(per_half, sc, da, got, h, e, gain, w, dhb, dctx, sums):
    i = pl.program_id(0)
    da2 = da[...].astype(F32) + got[...].astype(F32)
    normed, inv_std = center_rows(h[...].astype(F32))
    out_grad = e[...].astype(F32)
    low = (out_grad + norm_back(normed, inv_std, da2 * gain[...])).astype(LOW)
    dhb[...] = low
    dctx[...] = dot(low, w[...], NT).astype(LOW)
    own = jnp.where((i // per_half) % 2 == sc[S_T], 1.0, 0.0)
    terms = jnp.concatenate(
        [
            column_sum(low.astype(F32)),
            column_sum(da2 * normed),
            column_sum(da2),
            column_sum(out_grad),
        ],
        axis=0,
    )

    @pl.when(i == 0)
    def _():
        sums[...] = terms * own

    @pl.when(i > 0)
    def _():
        sums[...] += terms * own


def hidden_back_call(line, rows, da, got, h, e, gain, w, step):
    total, width = da.shape
    local = w.shape[0]
    strip = lambda wide: pl.BlockSpec((step, wide), lambda i, s: (i, 0))
    wide = strip(width)
    return line.run(
        lambda *refs: hidden_back_kernel(rows // step, *refs),
        "hidden_back",
        (total // step,),
        [(da, wide), (got, wide), (h, wide), (e, wide), (gain, whole((1, width))), (w, whole(w.shape))],
        [
            (shape((total, width), LOW), wide),
            (shape((total, local), LOW), strip(local)),
            (shape((4, width), F32), whole((4, width))),
        ],
        flops=2 * total * width * local,
    )


def attend_back_kernel(shards, pair_places, out_places, sc, q, k, v, ctx, inv, dctx, probs, a1_hbm, *refs):
    extra = [a1_hbm]
    group = len(pair_places)
    if out_places:
        extra, refs = extra + list(refs[:2]), refs[2:]
    pieces = len(shards.outs())
    refs = refs[-(3 + pieces + 1 + len(extra) + 1) :]
    dq, dk, dv = refs[:3]
    grads = refs[3 : 3 + pieces]
    rows_all = refs[3 + pieces]
    held = refs[4 + pieces : 4 + pieces + len(extra)]
    sems = refs[-1]
    j, m = pl.program_id(0), pl.program_id(1)

    def copies():
        return [
            pltpu.make_async_copy(source, target, sems.at[n])
            for n, (source, target) in enumerate(zip(extra, held))
        ]

    @pl.when((j == 0) & (m == 0))
    def _():
        for copy in copies():
            copy.start()

    slot = q.shape[1]
    lane = lax.broadcasted_iota(jnp.int32, (slot, 128), 1) < HD
    scaled = dctx[0].astype(F32) * inv[0]
    product = scaled * ctx[0].astype(F32)
    low = scaled.astype(LOW)
    key, query, value = k[0], q[0], v[0]
    cuts = splits(slot)
    per_head = []
    for h in range(2):
        here = lane if h == 0 else ~lane
        delta = jnp.sum(jnp.where(here, product, 0.0), axis=1, keepdims=True)
        masked = jnp.where(here, low, LOW(0))
        dqs, dks, dvs = [], [], []
        for lo, hi, ext in cuts:
            p = probs[0, h, lo:hi, :ext]
            dp = dot(masked[lo:hi], value[:ext], NT)
            ds = (p.astype(F32) * (dp - delta[lo:hi])).astype(LOW)
            dqs.append(dot(ds, key[:ext]))
            dks.append(dot(ds, query[lo:hi], TN))
            dvs.append(dot(p, low[lo:hi], TN))
        first = cuts[0][2]
        join = lambda two: jnp.concatenate([two[0] + two[1][:first], two[1][first:]], axis=0)
        per_head.append((jnp.concatenate(dqs, axis=0), join(dks), join(dvs)))
    root = 1.0 / math.sqrt(HD)
    start = pl.multiple_of(m * slot, slot)
    for c, (ref, scale) in enumerate(((dq, root), (dk, root), (dv, 1.0))):
        both = (jnp.where(lane, per_head[0][c], per_head[1][c]) * scale).astype(LOW)
        ref[0] = both
        rows_all[j, pl.ds(start, slot), c * 128 : (c + 1) * 128] = both

    @pl.when((m == pl.num_programs(1) - 1) & (j == group - 1))
    def _():
        for copy in copies():
            copy.wait()
        for g in range(group):
            side, column = pair_places[g]
            shards.emit(sc, dot(held[0][...], rows_all[g], TN), side, column, grads)
        for side, column, first, wide in out_places:
            term = dot(held[1][...], held[2][:, first : first + wide], TN)
            shards.emit(sc, term, side, column, grads)


def attend_back_call(
    line, shards, at, pair_places, out_places, qkv, ctx, inv, dctx, probs, a1, out_pair=(), before=None
):
    count, slot, local = ctx.shape
    group = len(pair_places)
    pair = pl.BlockSpec((1, slot, 128), lambda j, m, s: (m, 0, at + j))
    ins = [(a, pair) for a in (*qkv, ctx, inv, dctx)]
    ins.append((probs, pl.BlockSpec((1, 2, slot, slot), lambda j, m, s: (m, at + j, 0, 0))))
    extra = [a1, *out_pair]
    ins += [(a, pl.BlockSpec(memory_space=pltpu.HBM)) for a in extra]
    aliases = {}
    if before is not None:
        aliases = {len(ins) + i: i for i in range(3)}
        ins += [(b, anywhere()) for b in before]
    found = line.run(
        lambda *refs: attend_back_kernel(shards, pair_places, out_places, *refs),
        "attend_back",
        (group, count),
        ins,
        [(near((count, slot, local), LOW), pair)] * 3 + [(o, whole(o.shape)) for o in shards.outs()],
        scratch=[pltpu.VMEM((group, count * slot, 384), LOW)]
        + [pltpu.VMEM(a.shape, LOW) for a in extra]
        + [pltpu.SemaphoreType.DMA((len(extra),))],
        mib=32,
        flops=12e9,
        aliases=aliases,
    )
    return found[:3], found[3:]


def rows_back_kernel(sc, dq, dk, dv, w, x, x_far, keep, send, sums):
    m, j, i = pl.program_id(0), pl.program_id(1), pl.program_id(2)
    total = dot(dq[...], w[0], NT) + dot(dk[...], w[1], NT) + dot(dv[...], w[2], NT)

    @pl.when(j == 0)
    def _():
        send[0] = total.astype(LOW)

    @pl.when(j == 1)
    def _():
        keep[0] = total.astype(LOW)

    mine = jnp.full(x.shape[1:], j) == 1
    normed, _ = center_rows(jnp.where(mine, x[0], x_far[0]).astype(F32))
    terms = jnp.concatenate([column_sum(total * normed), column_sum(total)], axis=0)
    start = (m == 0) & (j == 0) & (i == 0)

    @pl.when(start)
    def _():
        sums[...] = terms

    @pl.when(~start)
    def _():
        sums[...] += terms


def rows_back_call(line, grads, w, x, x_far, step):
    count, rows, width = x.shape
    total, local = 2 * count * rows, w.shape[2]
    blocks, place, send, keep = own_rows(rows, step)
    out = shape((count, rows, width), LOW)
    block = (1, step, width)
    return line.run(
        rows_back_kernel,
        "rows_back",
        (count, 2, blocks),
        [(g, pl.BlockSpec((step, local), place)) for g in grads]
        + [(w, whole(w.shape, pipeline_mode=pl.Buffered(1)))]
        + [(v, pl.BlockSpec((1, step, width), lambda m, j, i, s: (m, i, 0))) for v in (x, x_far)],
        [
            (out, pl.BlockSpec(block, keep)),
            (out, pl.BlockSpec(block, send)),
            (shape((2, width), F32), whole((2, width))),
        ],
        flops=6 * total * width * local,
    )


def tokens_back_kernel(sc, x, dh, own, got, gain, out):
    normed, inv_std = center_rows(x[0].astype(F32))
    da1 = own[0].astype(F32) + got[0].astype(F32)
    back = norm_back(normed, inv_std, da1 * gain[...])
    out[0, 0] = (dh[...].astype(F32) + back).astype(LOW)


def tokens_back_call(line, x, dh, own, got, gain, step):
    count, rows, width = own.shape
    blocks = rows // step
    block = pl.BlockSpec((1, step, width), lambda m, i, s: (m, i, 0))
    natural = pl.BlockSpec((step, width), lambda m, i, s: ((2 * m + s[S_T]) * blocks + i, 0))
    return line.run(
        tokens_back_kernel,
        "tokens_back",
        (count, blocks),
        [(x, block), (dh, natural), (own, block), (got, block), (gain, whole((1, width)))],
        [
            (
                shape((count, 1, rows, width), LOW),
                pl.BlockSpec((1, 1, step, width), lambda m, i, s: (m, 0, i, 0)),
            )
        ],
    )[0]


def swap(value):
    return lax.ppermute(value, "tensor", [(0, 1), (1, 0)])


def vector_kernel(sc, one, two, out):
    out[...] = one[...] + two[...]


def last_vector_kernel(sc, one, two, *outs):
    total = one[...] + two[...]
    for n, out in enumerate(outs[:-1]):
        out[...] = total[n : n + 1, :]
    rest, width = len(outs) - 1, total.shape[1]
    for n in range(rest, total.shape[0]):
        outs[-1][:, (n - rest) * width : (n - rest + 1) * width] = total[n : n + 1, :]


class Vectors:
    def __init__(self, line, dp_count, values, shared):
        self.line, self.dp_count, self.values = line, dp_count, values
        rows = lax.broadcasted_iota(jnp.int32, (values.shape[0], 1), 0)
        self.got = swap(jnp.where(rows < shared, values, 0.0))
        self.mask = 1
        if dp_count & (dp_count - 1):
            self.values, self.got = lax.psum(values + self.got, "dp"), None

    def finish(self, rest):
        while self.got is not None and self.mask < self.dp_count:
            self.advance()
        count, width = self.values.shape
        if self.got is None:
            return [*self.values[:rest], self.values[rest:].reshape(-1)]
        dims = [(1, width)] * rest + [(1, (count - rest) * width)]
        found = self.line.run(
            last_vector_kernel,
            "add_vectors",
            (1,),
            [(a, whole(a.shape)) for a in (self.values, self.got)],
            [(jax.ShapeDtypeStruct(d, F32), whole(d)) for d in dims],
            mib=8,
        )
        return [v.reshape(-1) for v in found]

    def advance(self):
        if self.got is None:
            return
        dims = self.values.shape
        self.values = self.line.run(
            vector_kernel,
            "add_vectors",
            (1,),
            [(a, whole(dims)) for a in (self.values, self.got)],
            [(jax.ShapeDtypeStruct(dims, F32), whole(dims))],
            mib=8,
        )[0]
        self.got = move(self.values, self.dp_count, self.mask) if self.mask < self.dp_count else None
        self.mask *= 2


def head_places(pairs, out_width):
    sides = [0, 0]
    places, out_places = [], []
    for pair in range(pairs):
        side = pair * 2 // pairs
        places.append((side, sides[side]))
        sides[side] += 384
    for side in range(2 if out_width else 0):
        wide = out_width // 2
        out_places.append((side, sides[side], side * wide, wide))
        sides[side] += wide
    return places, out_places, sides


def local(
    tokens,
    d_mixed,
    phone_len,
    frame_len,
    ln1_gain,
    ln1_bias,
    w_qkv,
    w_out,
    attn_bias,
    ln2_gain,
    ln2_bias,
    w_up,
    up_bias,
    w_down,
    down_bias,
):
    count, _, rows, width = tokens.shape
    dp_count = lax.axis_size("dp")
    slot = 2 * rows
    local_width = w_qkv.shape[2]
    units = w_up.shape[1]
    shard_rows = width // dp_count
    step = rows
    row = lambda v: v.reshape(1, -1)
    x, dm = tokens[:, 0], d_mixed[:, 0]
    phones = phone_len[:, 0]
    sc = jnp.concatenate(
        [
            jnp.stack([lax.axis_index("tensor"), lax.axis_index("dp")]).astype(jnp.int32),
            phones + frame_len[:, 0],
            phones,
        ]
    )
    line = Line(sc)
    w3 = jnp.transpose(w_qkv, (1, 0, 2))
    g1, b1, g2, b2 = row(ln1_gain), row(ln1_bias), row(ln2_gain), row(ln2_bias)
    flat = lambda v: v.reshape(count * slot, v.shape[-1])

    x_far, dm_far, w_out_far = swap(x), swap(dm), swap(w_out)
    x_near, w_near = bring([x, w3])
    a1, *qkv, ctx, probs, inv = front_call(line, x_near, x_far, g1, b1, w_near)
    ctx_far = swap(ctx)
    en = mark_call(line, dm, dm_far)
    h, a2 = project_call(line, ctx, ctx_far, w_out, w_out_far, x, x_far, row(attn_bias), g2, b2)

    chunks = (units // 2, units // 2)
    reds, acts, dus, up_sums, at = [], [], [], [], 0
    for chunk in chunks:
        shards = Shards(dp_count, width, (chunk, chunk))
        (act, du, up_sum), grads = feed_call(
            line, shards, a2, en, w_up, w_down, row(up_bias), at, chunk
        )
        reds.append(Reduction(line, shards, grads))
        acts.append(act)
        dus.append(du)
        up_sums.append(up_sum)
        at += chunk
    da = up_back_call(line, dus, w_up, step)
    da_far = swap(da)
    red1, red2 = reds
    red1.advance()
    dhb, dctx, hidden_sums = hidden_back_call(line, rows, da, da_far, h, en, g2, w_out, step)
    own_down, far_down = down_call(line, count, rows, acts, w_down, step)
    far_down = swap(far_down)
    red2.advance()
    mixed = mixed_call(line, h, own_down, far_down, row(down_bias), step // 2)
    red1.advance()

    pairs = local_width // 128
    dctx = dctx.reshape(count, slot, local_width)
    half = pairs // 2
    places3, outs3, sides3 = head_places(half, local_width)
    places4, _, sides4 = head_places(pairs - half, 0)
    shards3, shards4 = Shards(dp_count, width, sides3), Shards(dp_count, width, sides4)
    rest = (qkv, ctx, inv, dctx, probs, flat(a1))
    grads, parts = attend_back_call(line, shards3, 0, places3, outs3, *rest, (dhb, flat(ctx)))
    red3 = Reduction(line, shards3, parts)
    red2.advance()
    red1.advance()
    grads, parts = attend_back_call(line, shards4, half, places4, [], *rest, (), grads)
    red4 = Reduction(line, shards4, parts)
    feed_dims = [(shard_rows, units)] * 2
    feed_places = lambda at, chunk: [(n, None, at, n * chunk, chunk) for n in range(2)]
    feed_grads = red1.finish(feed_places(0, chunks[0]), feed_dims)
    red3.advance()
    red2.advance()
    own, far, token_sums = rows_back_call(
        line, [flat(g) for g in grads], w3, x, x_far, step
    )
    far = swap(far)
    up_rows = [v.reshape(-1, width) for v in up_sums]
    sums = Vectors(line, dp_count, jnp.concatenate([token_sums, hidden_sums, *up_rows]), 6)
    red3.advance()
    red4.advance()
    sums.advance()
    d_tokens = tokens_back_call(line, x, dhb, own, far, g1, step // 2)
    sums.advance()
    red3.advance()
    red4.advance()
    sums.advance()
    grad_down, grad_up = red2.finish(feed_places(chunks[0], chunks[1]), feed_dims, feed_grads)
    sums.advance()
    red4.advance()

    def finish(red, at, pair_places, out_places, sides, dims, before=None):
        starts = [sum(sides[:n]) for n in range(len(sides))]
        places = []
        for g, (side, column) in enumerate(pair_places):
            for c in range(3):
                places.append((0, c, (at + g) * 128, starts[side] + column + c * 128, 128))
        for side, column, first, wide in out_places:
            places.append((1, None, first, starts[side] + column, wide))
        return red.finish(places, dims, before)

    dims = [(3, shard_rows, local_width), (shard_rows, local_width)]
    grad_qkv, grad_out = finish(red3, 0, places3, outs3, sides3, dims)
    vectors = sums.finish(6)
    (grad_qkv,) = finish(red4, half, places4, [], sides4, dims[:1], [grad_qkv])

    return (
        mixed,
        d_tokens,
        vectors[0],
        vectors[1],
        jnp.transpose(grad_qkv, (1, 0, 2)),
        grad_out.T,
        vectors[2],
        vectors[3],
        vectors[4],
        grad_up,
        vectors[6],
        grad_down.T,
        vectors[5],
    )


def solution(mesh):
    in_specs = (
        P(None, "dp", "tensor", None),
        P(None, "dp", "tensor", None),
        P(None, "dp"),
        P(None, "dp"),
        P(),
        P(),
        P(None, None, "tensor"),
        P("tensor", None),
        P(),
        P(),
        P(),
        P(None, "tensor"),
        P("tensor"),
        P("tensor", None),
        P(),
    )
    out_specs = (
        P(None, "dp", "tensor", None),
        P(None, "dp", "tensor", None),
        P(),
        P(),
        P("dp", None, "tensor"),
        P("tensor", "dp"),
        P(),
        P(),
        P(),
        P("dp", "tensor"),
        P("tensor"),
        P("tensor", "dp"),
        P(),
    )
    return jax.shard_map(local, mesh=mesh, in_specs=in_specs, out_specs=out_specs, check_vma=False)
```

```python
import math

import jax
import jax.numpy as jnp
from jax import lax
from jax.experimental import pallas as pl
from jax.experimental.pallas import tpu as pltpu
from jax.sharding import PartitionSpec as P

HD = 64
EPS = 1e-05
LOW = jnp.bfloat16
F32 = jnp.float32
NT = (((1,), (1,)), ((), ()))
TN = (((0,), (0,)), ((), ()))
GELU_A = math.sqrt(2.0 / math.pi)
GELU_B = 0.044715

S_T, S_DP, S_LEN, S_PH = 0, 1, 2, 4


def dot(a, b, dims=(((1,), (0,)), ((), ()))):
    return lax.dot_general(a, b, dims, preferred_element_type=F32)


def shape(dims, dtype):
    if math.prod(dims) * jnp.dtype(dtype).itemsize >= 1 << 17:
        return pltpu.HBM(dims, dtype)
    return jax.ShapeDtypeStruct(dims, dtype)


def near(dims, dtype):
    return pltpu.VMEM(dims, dtype)


def whole(dims, **more):
    return pl.BlockSpec(dims, lambda *_: (0,) * len(dims), **more)


def anywhere():
    return pl.BlockSpec(memory_space=pl.ANY)


ADD_FLOPS = 3e10


class Line:
    def __init__(self, sc):
        self.sc = sc
        self.token = jnp.zeros((8, 128), F32)
        self.pending, self.carried = [], []

    def run(self, kernel, name, grid, ins, outs, scratch=(), mib=24, flops=0, aliases=None):
        count_in, count_out = len(ins), len(outs)
        through, self.pending = [self.token, *self.pending], []
        extra = len(through)

        def body(*refs):
            mid = 1 + count_in
            end = mid + extra + count_out
            kernel(*refs[:mid], *refs[mid + extra : end], *refs[end + extra :])

        arrays = [a for a, _ in ins]
        nbytes = sum(math.prod(a.shape) * a.dtype.itemsize for a in arrays)
        aliases = {1 + i: o for i, o in (aliases or {}).items()}
        aliases.update({1 + count_in + n: count_out + n for n in range(extra)})
        found = pl.pallas_call(
            body,
            grid_spec=pltpu.PrefetchScalarGridSpec(
                num_scalar_prefetch=1,
                grid=grid,
                in_specs=[s for _, s in ins] + [anywhere()] * extra,
                out_specs=[s for _, s in outs] + [anywhere()] * extra,
                scratch_shapes=list(scratch),
            ),
            out_shape=[o for o, _ in outs]
            + [jax.ShapeDtypeStruct(t.shape, t.dtype) for t in through],
            input_output_aliases=aliases,
            compiler_params=pltpu.CompilerParams(vmem_limit_bytes=mib << 20),
            cost_estimate=pl.CostEstimate(
                flops=int(flops * 1), bytes_accessed=int(nbytes * 1), transcendentals=0
            ),
            name=name,
        )(self.sc, *arrays, *through)
        self.token, self.carried = found[count_out], list(found[count_out + 1 :])
        return found[:count_out]


def center_rows(values):
    center = values - jnp.mean(values, axis=-1, keepdims=True)
    inv_std = lax.rsqrt(jnp.mean(center * center, axis=-1, keepdims=True) + EPS)
    return center * inv_std, inv_std


def norm_back(normed, inv_std, t):
    return inv_std * (
        t
        - jnp.mean(t, axis=-1, keepdims=True)
        - normed * jnp.mean(t * normed, axis=-1, keepdims=True)
    )


def column_sum(values):
    return jnp.sum(values, axis=0, keepdims=True)


def bring(arrays):
    vm = pl.BlockSpec(memory_space=pltpu.VMEM)
    hbm = pl.BlockSpec(memory_space=pltpu.HBM)

    def kernel(*refs):
        count = len(arrays)
        sems = refs[-1]
        copies = [
            pltpu.make_async_copy(source, target, sems.at[n])
            for n, (source, target) in enumerate(zip(refs[:count], refs[count:-1]))
        ]
        for copy in copies:
            copy.start()
        for copy in copies:
            copy.wait()

    return pl.pallas_call(
        kernel,
        in_specs=[hbm] * len(arrays),
        out_specs=[vm] * len(arrays),
        out_shape=[near(a.shape, a.dtype) for a in arrays],
        scratch_shapes=[pltpu.SemaphoreType.DMA((len(arrays),))],
        compiler_params=pltpu.CompilerParams(vmem_limit_bytes=4 << 20),
        name="bring",
    )(*arrays)


def splits(slot):
    half = slot // 2
    cut = -(-half // 128) * 128
    return [(0, cut, cut), (cut, slot, slot)]


def front_kernel(
    sc, x, x_far, gain, shift, w,
    a1, q, k, v, ctx, probs, inv,
    low, qkv, bias, sem,
):
    m, j = pl.program_id(0), pl.program_id(1)
    rows = x.shape[1]
    slot = 2 * rows
    local = w.shape[2]
    here = pl.multiple_of(sc[S_T] * rows, rows)
    there = pl.multiple_of((1 - sc[S_T]) * rows, rows)

    def copy():
        return pltpu.make_async_copy(low, a1.at[m], sem.at[0])

    @pl.when(j == 0)
    def _():
        for source, at in ((x, here), (x_far, there)):
            normed, _ = center_rows(source[0].astype(F32))
            low[pl.ds(at, rows), :] = (normed * gain[...] + shift[...]).astype(LOW)
        copy().start()
        for c in range(3):
            qkv[:, c * local : (c + 1) * local] = dot(low[...], w[c]).astype(LOW)
        qi = lax.broadcasted_iota(jnp.int32, (slot, slot), 0)
        ki = lax.broadcasted_iota(jnp.int32, (slot, slot), 1)
        bias[...] = jnp.where((ki <= qi) | (ki < sc[S_PH + m]), 0.0, -1e30)

    def part(c):
        return qkv[:, pl.ds(pl.multiple_of(c * local + j * 128, 128), 128)]

    lane = lax.broadcasted_iota(jnp.int32, (slot, 128), 1) < HD
    query_all, key, value = part(0), part(1), part(2)
    q[0], k[0], v[0] = query_all, key, value
    widened = jnp.concatenate([value, jnp.ones_like(value)], axis=1)
    for lo, hi, ext in splits(slot):
        query = query_all[lo:hi] * LOW(1.0 / math.sqrt(HD))
        first = lane[lo:hi]
        sums = []
        for h in range(2):
            masked = jnp.where(first if h == 0 else ~first, query, LOW(0))
            s = dot(masked, key[:ext], NT) + bias[lo:hi, :ext]
            p = jnp.exp(s - jnp.max(s, axis=1, keepdims=True)).astype(LOW)
            probs[0, h, lo:hi, :ext] = p
            sums.append(dot(p, widened[:ext]))
        total = jnp.where(first, sums[0][:, :128], sums[1][:, :128])
        scale = 1.0 / jnp.where(first, sums[0][:, 128:], sums[1][:, 128:])
        ctx[0, lo:hi, :] = (total * scale).astype(LOW)
        inv[0, lo:hi, :] = scale

    @pl.when(j == pl.num_programs(1) - 1)
    def _():
        copy().wait()


def front_call(line, x, x_far, gain, shift, w):
    count, rows, width = x.shape
    slot, local = 2 * rows, w.shape[2]
    heads = local // HD
    own = pl.BlockSpec((1, rows, width), lambda m, j, s: (m, 0, 0))
    pair = pl.BlockSpec((1, slot, 128), lambda m, j, s: (m, 0, j))
    natural = shape((count, slot, width), LOW)
    heads_out = shape((count, slot, local), LOW)
    return line.run(
        front_kernel,
        "norm_attend",
        (count, local // 128),
        [(x, own), (x_far, own)]
        + [(gain, whole((1, width))), (shift, whole((1, width)))]
        + [(w, whole(w.shape, pipeline_mode=pl.Buffered(1)))],
        [(natural, anywhere())]
        + [(heads_out, pair)] * 4
        + [
            (
                shape((count, heads, slot, slot), LOW),
                pl.BlockSpec((1, 2, slot, slot), lambda m, j, s: (m, j, 0, 0)),
            ),
            (shape((count, slot, local), F32), pair),
        ],
        scratch=[
            pltpu.VMEM((slot, width), LOW),
            pltpu.VMEM((slot, 3 * local), LOW),
            pltpu.VMEM((slot, slot), F32),
            pltpu.SemaphoreType.DMA((1,)),
        ],
        mib=30,
        flops=2e10,
    )


def mark_kernel(sc, dm, dm_far, e):
    m, half = pl.program_id(0), pl.program_id(1)
    rows = dm.shape[1]
    mine = jnp.full(dm.shape[1:], half) == sc[S_T]
    ids = half * rows + lax.broadcasted_iota(jnp.int32, (rows, 1), 0)
    e[...] = jnp.where(ids < sc[S_LEN + m], jnp.where(mine, dm[0], dm_far[0]), LOW(0))


def mark_call(line, dm, dm_far):
    count, rows, width = dm.shape
    held = pl.BlockSpec((1, rows, width), lambda m, i, s: (m, 0, 0))
    return line.run(
        mark_kernel,
        "mark_rows",
        (count, 2),
        [(dm, held), (dm_far, held)],
        [(near((2 * count * rows, width), LOW), pl.BlockSpec((rows, width), lambda m, i, s: (2 * m + i, 0)))],
    )[0]


def project_kernel(sc, ctx, far, w, w_far, x, x_far, bias, gain, shift, h, a2):
    m, half = pl.program_id(0), pl.program_id(1)
    mine = jnp.full(x.shape[1:], half) == sc[S_T]
    both = dot(ctx[0], w[...]) + dot(far[0], w_far[...])
    hidden = jnp.where(mine, x[0], x_far[0]).astype(F32) + both + bias[...]
    h[...] = hidden.astype(LOW)
    normed, _ = center_rows(hidden)
    a2[...] = (normed * gain[...] + shift[...]).astype(LOW)


def project_call(line, ctx, far, w, w_far, x, x_far, bias, gain, shift):
    count, rows, width = x.shape
    local = ctx.shape[2]
    strip = pl.BlockSpec((1, rows, local), lambda m, i, s: (m, i, 0))
    held = pl.BlockSpec((1, rows, width), lambda m, i, s: (m, 0, 0))
    one = whole((1, width))
    out = (shape((2 * count * rows, width), LOW), pl.BlockSpec((rows, width), lambda m, i, s: (2 * m + i, 0)))
    return line.run(
        project_kernel,
        "project",
        (count, 2),
        [(ctx, strip), (far, strip), (w, whole(w.shape)), (w_far, whole(w.shape))]
        + [(x, held), (x_far, held)]
        + [(bias, one), (gain, one), (shift, one)],
        [out, (near((2 * count * rows, width), LOW), out[1])],
        flops=4 * count * rows * width * width,
    )


class Shards:
    def __init__(self, dp_count, width, sides):
        self.dp_count = dp_count
        self.width = width
        self.rows = width // dp_count
        self.sides = sides
        self.bits = dp_count.bit_length() - 1
        self.halving = dp_count == 1 << self.bits and self.bits > 2 and self.rows % 16 == 0
        late = list(range(3, self.bits))
        orders = ([0, 1, 2], [1, 0, 2]) if len(sides) == 2 else ([0, 1, 2], [1, 2, 0], [2, 0, 1])
        self.orders = [order + late for order in orders]

    def outs(self):
        if not self.halving:
            return [jax.ShapeDtypeStruct((self.width, n), LOW) for n in self.sides]
        return [
            kind((self.dp_count // 2, self.rows, n), LOW)
            for n in self.sides
            for kind in (pltpu.HBM, near if sum(self.sides) < 0 else pltpu.HBM)
        ]

    def emit(self, sc, value, side, at, refs):
        value = value.astype(LOW)
        span = slice(at, at + value.shape[1])
        if not self.halving:
            refs[side][:, span] = value
            return
        send, keep = refs[2 * side], refs[2 * side + 1]
        blocks = value.reshape(self.dp_count, self.rows, value.shape[1])
        order = self.orders[side]
        mine = jnp.full((self.rows, value.shape[1]), (sc[S_DP] >> order[0]) & 1) == 1
        for i in range(self.dp_count // 2):
            at_zero = sum(((i >> n) & 1) << bit for n, bit in enumerate(order[1:]))
            zero = blocks[at_zero]
            one = blocks[at_zero + (1 << order[0])]
            send[i, :, span] = jnp.where(mine, zero, one)
            keep[i, :, span] = jnp.where(mine, one, zero)


def split_kernel(bits, sc, *refs):
    sides = len(bits)
    ins, outs = refs[: 2 * sides], refs[2 * sides :]
    joined = len(outs) == 2
    at = 0
    for n, bit in enumerate(bits):
        keep, got = ins[2 * n], ins[2 * n + 1]
        send_out, keep_out = outs[:2] if joined else outs[2 * n : 2 * n + 2]
        columns = keep.shape[2]
        mine = (sc[S_DP] >> bit) & 1
        for j, ref in ((1 - mine, send_out), (mine, keep_out)):
            total = (keep[j].astype(F32) + got[j].astype(F32)).astype(LOW)
            ref[0, :, at : at + columns] = total
        if joined:
            at += columns


def far_keep_kernel(bits, sc, *refs):
    sides = len(bits)
    keeps, gots, outs = refs[:sides], refs[sides : 2 * sides], refs[2 * sides : 4 * sides]
    held, sems = refs[4 * sides : 5 * sides], refs[-1]
    i, blocks = pl.program_id(0), keeps[0].shape[0] // 2

    def copy(n, side):
        span = pl.ds(2 * n, 2)
        return pltpu.make_async_copy(keeps[side].at[span], held[side].at[span], sems.at[n, side])

    @pl.when(i == 0)
    def _():
        for n in range(blocks):
            for side in range(sides):
                copy(n, side).start()

    for n in range(blocks):

        @pl.when(i == n)
        def _():
            for side in range(sides):
                copy(n, side).wait()

    for side, bit in enumerate(bits):
        mine = (sc[S_DP] >> bit) & 1
        for j, ref in ((1 - mine, outs[2 * side]), (mine, outs[2 * side + 1])):
            keep = held[side][2 * i + j]
            ref[0] = (keep.astype(F32) + gots[side][j].astype(F32)).astype(LOW)


def far_keep_call(line, bits, args, flops):
    blocks, rows, _ = args[0].shape
    keeps, gots = args[::2], args[1::2]
    return line.run(
        lambda *refs: far_keep_kernel(bits, *refs),
        "add_far",
        (blocks // 2,),
        [(a, pl.BlockSpec(memory_space=pltpu.HBM)) for a in keeps]
        + [(a, pl.BlockSpec((2, rows, a.shape[2]), lambda i, s: (i, 0, 0))) for a in gots],
        [
            (
                jax.ShapeDtypeStruct((blocks // 2, rows, a.shape[2]), LOW),
                pl.BlockSpec((1, rows, a.shape[2]), lambda i, s: (i, 0, 0)),
            )
            for a in keeps
            for _ in range(2)
        ],
        scratch=[pltpu.VMEM(a.shape, LOW) for a in keeps]
        + [pltpu.SemaphoreType.DMA((blocks // 2, len(keeps)))],
        mib=12,
        flops=flops,
    )


def split_call(line, bits, args, widths, name, flops):
    blocks, rows, _ = args[0].shape
    if len(widths) == len(bits) > 1 and sum(math.prod(a.shape) for a in args) >= 1 << 21:
        return far_keep_call(line, bits, args, flops)
    return line.run(
        lambda *refs: split_kernel(bits, *refs),
        name,
        (blocks // 2,),
        [(a, pl.BlockSpec((2, rows, a.shape[2]), lambda i, s: (i, 0, 0))) for a in args],
        [
            (
                jax.ShapeDtypeStruct((blocks // 2, rows, n), LOW),
                pl.BlockSpec((1, rows, n), lambda i, s: (i, 0, 0)),
            )
            for n in widths
            for _ in range(2)
        ],
        mib=12,
        flops=flops,
    )


def move(value, dp_count, mask):
    return lax.ppermute(value, "dp", [(i, i ^ mask) for i in range(dp_count)])


class Reduction:
    def __init__(self, line, shards, arrays):
        self.line, self.shards = line, shards
        self.step = 0
        if not shards.halving:
            self.keep = jnp.concatenate(
                [
                    lax.psum_scatter(a.astype(F32), "dp", scatter_dimension=0, tiled=True)
                    for a in arrays
                ],
                axis=1,
            )
            self.got, self.step = [], shards.bits
            return
        self.orders = shards.orders
        self.sides = shards.sides
        self.keep = arrays[1::2]
        self.send(arrays[::2])

    def send(self, arrays):
        count = self.shards.dp_count
        self.got = [
            lax.ppermute(a, "dp", [(i, i ^ (1 << order[self.step])) for i in range(count)])
            for a, order in zip(arrays, self.orders)
        ]
        self.step += 1

    def advance(self, flops=ADD_FLOPS):
        if self.step >= self.shards.bits:
            return
        bits = [order[self.step] for order in self.orders]
        joined = all(order[self.step :] == self.orders[0][self.step :] for order in self.orders)
        args = [a for pair in zip(self.keep, self.got) for a in pair]
        widths = [sum(self.sides)] if joined else self.sides
        found = split_call(self.line, bits, args, widths, "add_split", flops)
        if joined:
            self.orders, self.sides = self.orders[:1], widths
        self.keep = found[1::2]
        self.send(found[::2])

    def rest(self):
        while self.step < self.shards.bits:
            self.advance()
        if not self.shards.halving:
            return [self.keep]
        return [v[0].reshape(v[0].shape[-2:]) for v in (self.keep, self.got)]


def last_kernel(plans, terms, rest, count_out, sc, *refs):
    groups = len(plans)
    values, sems = refs[-1 - groups : -1], refs[-1]
    made = refs[: -1 - groups]
    outs, vectors = made[len(made) - count_out :], []
    if rest is not None:
        outs, vectors = outs[: count_out - rest - 1], outs[count_out - rest - 1 :]
    copies, at, used = [], 0, 0
    for plan, count, value in zip(plans, terms, values):
        total = refs[at][...].astype(F32)
        for ref in refs[at + 1 : at + count]:
            total = total + ref[...].astype(F32)
        at += count
        value[...] = total
        for out, lead, column, source, columns in plan:
            target = outs[out] if lead is None else outs[out].at[lead]
            copy = pltpu.make_async_copy(
                value.at[:, pl.ds(source, columns)],
                target.at[:, pl.ds(column, columns)],
                sems.at[used],
            )
            used += 1
            copy.start()
            copies.append(copy)
    if rest is not None:
        write_vectors(refs[at][...] + refs[at + 1][...], vectors)
    for copy in copies:
        copy.wait()


def write_vectors(total, outs):
    for n, out in enumerate(outs[:-1]):
        out[...] = total[n : n + 1, :]
    rest, width = len(outs) - 1, total.shape[1]
    for n in range(rest, total.shape[0]):
        outs[-1][:, (n - rest) * width : (n - rest + 1) * width] = total[n : n + 1, :]


def last_call(line, groups, out_dims, sums=None, rest=6, before=()):
    ins, plans, terms, scratch = [], [], [], []
    for red, plan in groups:
        arrays = red.rest()
        ins += [(a, whole(a.shape)) for a in arrays]
        plans.append(plan)
        terms.append(len(arrays))
        scratch.append(pltpu.VMEM(arrays[0].shape, F32))
    outs = [(pltpu.HBM(d, F32), anywhere()) for d in out_dims]
    if sums is not None:
        pair = sums.rest()
        ins += [(a, whole(a.shape)) for a in pair]
        count, width = pair[0].shape
        for d in [(1, width)] * rest + [(1, (count - rest) * width)]:
            outs.append((jax.ShapeDtypeStruct(d, F32), whole(d)))
    aliases = {len(ins) + n: n for n in range(len(before))}
    ins += [(b, anywhere()) for b in before]
    found = line.run(
        lambda *refs: last_kernel(plans, terms, None if sums is None else rest, len(outs), *refs),
        "add_last",
        (1,),
        ins,
        outs,
        scratch=scratch + [pltpu.SemaphoreType.DMA((sum(len(p) for p in plans),))],
        mib=12,
        aliases=aliases,
    )
    return found[: len(out_dims)], [v.reshape(-1) for v in found[len(out_dims) :]]


def gelu_both(u):
    square = u * u
    t = jnp.tanh(u * (GELU_A + (GELU_A * GELU_B) * square))
    half = 0.5 + 0.5 * t
    slope = half + (0.5 * u) * (1.0 - t * t) * (GELU_A + (3.0 * GELU_A * GELU_B) * square)
    return u * half, slope


def feed_kernel(shards, sc, a2, e, wu, wd, ub, gb, du, bias, *grads):
    rows = a2.shape[0]
    step = rows // 2
    total = jnp.zeros(bias.shape, F32)
    for r in range(0, rows, step):
        u = dot(a2[r : r + step, :], wu[...]) + ub[...]
        act, slope = gelu_both(u)
        gb[r : r + step, :] = act.astype(LOW)
        low = (dot(e[r : r + step, :], wd[...], NT) * slope).astype(LOW)
        du[r : r + step, :] = low
        total = total + column_sum(low.astype(F32))
    bias[...] = total
    shards.emit(sc, dot(e[...], gb[...], TN), 0, 0, grads)
    shards.emit(sc, dot(a2[...], du[...], TN), 1, 0, grads)


def feed_call(line, shards, a2, e, w_up, w_down, up_bias, at, chunk, tile=512):
    rows, width = a2.shape
    tile = min(tile, chunk)
    first = at // tile
    one = pl.Buffered(1)
    strip = pl.BlockSpec((rows, tile), lambda i, s: (0, i))
    outs = [(shape((rows, chunk), LOW), strip), (near((rows, chunk), LOW), strip)]
    outs.append((shape((1, chunk), F32), pl.BlockSpec((1, tile), lambda i, s: (0, i))))
    for o in shards.outs():
        block = o.shape[:-1] + (tile,)
        lead = (0,) * (len(block) - 1)
        outs.append((o, pl.BlockSpec(block, lambda i, s, lead=lead: (*lead, i))))
    found = line.run(
        lambda *refs: feed_kernel(shards, *refs),
        "feed_forward",
        (chunk // tile,),
        [
            (a2, whole(a2.shape, pipeline_mode=one)),
            (e, whole(e.shape, pipeline_mode=one)),
            (w_up, pl.BlockSpec((width, tile), lambda i, s: (0, first + i))),
            (w_down, pl.BlockSpec((tile, width), lambda i, s: (first + i, 0))),
            (up_bias, pl.BlockSpec((1, tile), lambda i, s: (0, first + i))),
        ],
        outs,
        mib=40,
        flops=8 * rows * width * chunk,
    )
    return found[:3], found[3:]


def up_back_kernel(sc, *refs):
    dus, (w, out) = refs[:-2], refs[-2:]
    total, at = None, 0
    for du in dus:
        term = dot(du[...], w[:, at : at + du.shape[1]], NT)
        at += du.shape[1]
        total = term if total is None else total + term
    out[...] = total.astype(LOW)


def up_back_call(line, dus, w_up, step):
    rows = dus[0].shape[0]
    width, units = w_up.shape
    return line.run(
        up_back_kernel,
        "up_back",
        (rows // step,),
        [(du, pl.BlockSpec((step, du.shape[1]), lambda i, s: (i, 0))) for du in dus]
        + [(w_up, whole(w_up.shape, pipeline_mode=pl.Buffered(1)))],
        [(shape((rows, width), LOW), pl.BlockSpec((step, width), lambda i, s: (i, 0)))],
        mib=32,
        flops=2 * rows * width * units,
    )[0]


def own_rows(rows, step):
    blocks = rows // step

    def place(m, j, i, s):
        half = jnp.where(j == 1, s[S_T], 1 - s[S_T])
        return ((2 * m + half) * blocks + i, 0)

    def send(m, j, i, s):
        return (m, jnp.where(j == 0, i, blocks - 1), 0)

    def keep(m, j, i, s):
        return (m, jnp.where(j == 1, i, 0), 0)

    return blocks, place, send, keep


def down_kernel(sc, *refs):
    acts, (w, keep, send) = refs[:-3], refs[-3:]
    total, at = None, 0
    for act in acts:
        term = dot(act[...], w[at : at + act.shape[1], :])
        at += act.shape[1]
        total = term if total is None else total + term

    @pl.when(pl.program_id(1) == 0)
    def _():
        send[0] = total.astype(LOW)

    @pl.when(pl.program_id(1) == 1)
    def _():
        keep[0] = total.astype(LOW)


def down_call(line, count, rows, acts, w, step):
    width = w.shape[1]
    blocks, place, send, keep = own_rows(rows, step)
    out = shape((count, rows, width), LOW)
    block = (1, step, width)
    return line.run(
        down_kernel,
        "feed_down",
        (count, 2, blocks),
        [(a, pl.BlockSpec((step, a.shape[1]), place)) for a in acts]
        + [(w, whole(w.shape, pipeline_mode=pl.Buffered(1)))],
        [(out, pl.BlockSpec(block, keep)), (out, pl.BlockSpec(block, send))],
        flops=4 * count * rows * w.shape[0] * width,
    )


def mixed_kernel(sc, h, own, got, bias, out):
    m, i = pl.program_id(0), pl.program_id(1)
    rows = own.shape[1]
    first = sc[S_T] * rows * pl.num_programs(1) + i * rows
    ids = first + lax.broadcasted_iota(jnp.int32, (rows, 1), 0)
    value = h[...].astype(F32) + (own[0].astype(F32) + got[0].astype(F32)) + bias[...]
    out[0, 0] = jnp.where(ids < sc[S_LEN + m], value, 0.0).astype(LOW)


def mixed_call(line, h, own, got, bias, step):
    count, rows, width = own.shape
    blocks = rows // step
    block = pl.BlockSpec((1, step, width), lambda m, i, s: (m, i, 0))
    natural = pl.BlockSpec((step, width), lambda m, i, s: ((2 * m + s[S_T]) * blocks + i, 0))
    return line.run(
        mixed_kernel,
        "mixed_rows",
        (count, blocks),
        [(h, natural), (own, block), (got, block), (bias, whole((1, width)))],
        [
            (
                shape((count, 1, rows, width), LOW),
                pl.BlockSpec((1, 1, step, width), lambda m, i, s: (m, 0, i, 0)),
            )
        ],
    )[0]


def hidden_back_kernel(per_half, sc, da, got, h, e, gain, w, dhb, dctx, sums):
    i = pl.program_id(0)
    da2 = da[...].astype(F32) + got[...].astype(F32)
    normed, inv_std = center_rows(h[...].astype(F32))
    out_grad = e[...].astype(F32)
    low = (out_grad + norm_back(normed, inv_std, da2 * gain[...])).astype(LOW)
    dhb[...] = low
    dctx[...] = dot(low, w[...], NT).astype(LOW)
    own = jnp.where((i // per_half) % 2 == sc[S_T], 1.0, 0.0)
    terms = jnp.concatenate(
        [
            column_sum(low.astype(F32)),
            column_sum(da2 * normed),
            column_sum(da2),
            column_sum(out_grad),
        ],
        axis=0,
    )

    @pl.when(i == 0)
    def _():
        sums[...] = terms * own

    @pl.when(i > 0)
    def _():
        sums[...] += terms * own


def hidden_back_call(line, rows, da, got, h, e, gain, w, step):
    total, width = da.shape
    local = w.shape[0]
    strip = lambda wide: pl.BlockSpec((step, wide), lambda i, s: (i, 0))
    wide = strip(width)
    return line.run(
        lambda *refs: hidden_back_kernel(rows // step, *refs),
        "hidden_back",
        (total // step,),
        [(da, wide), (got, wide), (h, wide), (e, wide), (gain, whole((1, width))), (w, whole(w.shape))],
        [
            (shape((total, width), LOW), wide),
            (shape((total, local), LOW), strip(local)),
            (shape((4, width), F32), whole((4, width))),
        ],
        flops=2 * total * width * local,
    )


def attend_back_kernel(shards, pair_places, out_places, sc, q, k, v, ctx, inv, dctx, probs, a1_hbm, *refs):
    extra = [a1_hbm]
    group = len(pair_places)
    if out_places:
        extra, refs = extra + list(refs[:2]), refs[2:]
    pieces = len(shards.outs())
    refs = refs[-(3 + pieces + 1 + len(extra) + 1) :]
    dq, dk, dv = refs[:3]
    grads = refs[3 : 3 + pieces]
    rows_all = refs[3 + pieces]
    held = refs[4 + pieces : 4 + pieces + len(extra)]
    sems = refs[-1]
    j, m = pl.program_id(0), pl.program_id(1)

    def copies():
        return [
            pltpu.make_async_copy(source, target, sems.at[n])
            for n, (source, target) in enumerate(zip(extra, held))
        ]

    @pl.when((j == 0) & (m == 0))
    def _():
        for copy in copies():
            copy.start()

    slot = q.shape[1]
    lane = lax.broadcasted_iota(jnp.int32, (slot, 128), 1) < HD
    scaled = dctx[0].astype(F32) * inv[0]
    product = scaled * ctx[0].astype(F32)
    low = scaled.astype(LOW)
    key, query, value = k[0], q[0], v[0]
    cuts = splits(slot)
    per_head = []
    for h in range(2):
        here = lane if h == 0 else ~lane
        delta = jnp.sum(jnp.where(here, product, 0.0), axis=1, keepdims=True)
        masked = jnp.where(here, low, LOW(0))
        dqs, dks, dvs = [], [], []
        for lo, hi, ext in cuts:
            p = probs[0, h, lo:hi, :ext]
            dp = dot(masked[lo:hi], value[:ext], NT)
            ds = (p.astype(F32) * (dp - delta[lo:hi])).astype(LOW)
            dqs.append(dot(ds, key[:ext]))
            dks.append(dot(ds, query[lo:hi], TN))
            dvs.append(dot(p, low[lo:hi], TN))
        first = cuts[0][2]
        join = lambda two: jnp.concatenate([two[0] + two[1][:first], two[1][first:]], axis=0)
        per_head.append((jnp.concatenate(dqs, axis=0), join(dks), join(dvs)))
    root = 1.0 / math.sqrt(HD)
    start = pl.multiple_of(m * slot, slot)
    for c, (ref, scale) in enumerate(((dq, root), (dk, root), (dv, 1.0))):
        both = (jnp.where(lane, per_head[0][c], per_head[1][c]) * scale).astype(LOW)
        ref[0] = both
        rows_all[j, pl.ds(start, slot), c * 128 : (c + 1) * 128] = both

    @pl.when((m == pl.num_programs(1) - 1) & (j == group - 1))
    def _():
        for copy in copies():
            copy.wait()
        for g in range(group):
            side, column = pair_places[g]
            shards.emit(sc, dot(held[0][...], rows_all[g], TN), side, column, grads)
        for side, column, first, wide in out_places:
            term = dot(held[1][...], held[2][:, first : first + wide], TN)
            shards.emit(sc, term, side, column, grads)


def attend_back_call(
    line, shards, at, pair_places, out_places, qkv, ctx, inv, dctx, probs, a1, out_pair=(), before=None
):
    count, slot, local = ctx.shape
    group = len(pair_places)
    pair = pl.BlockSpec((1, slot, 128), lambda j, m, s: (m, 0, at + j))
    ins = [(a, pair) for a in (*qkv, ctx, inv, dctx)]
    ins.append((probs, pl.BlockSpec((1, 2, slot, slot), lambda j, m, s: (m, at + j, 0, 0))))
    extra = [a1, *out_pair]
    ins += [(a, pl.BlockSpec(memory_space=pltpu.HBM)) for a in extra]
    aliases = {}
    if before is not None:
        aliases = {len(ins) + i: i for i in range(3)}
        ins += [(b, anywhere()) for b in before]
    found = line.run(
        lambda *refs: attend_back_kernel(shards, pair_places, out_places, *refs),
        "attend_back",
        (group, count),
        ins,
        [(near((count, slot, local), LOW), pair)] * 3 + [(o, whole(o.shape)) for o in shards.outs()],
        scratch=[pltpu.VMEM((group, count * slot, 384), LOW)]
        + [pltpu.VMEM(a.shape, LOW) for a in extra]
        + [pltpu.SemaphoreType.DMA((len(extra),))],
        mib=32,
        flops=12e9,
        aliases=aliases,
    )
    return found[:3], found[3:]


def rows_back_kernel(sc, dq, dk, dv, w, x, x_far, keep, send, sums):
    m, j, i = pl.program_id(0), pl.program_id(1), pl.program_id(2)
    total = dot(dq[...], w[0], NT) + dot(dk[...], w[1], NT) + dot(dv[...], w[2], NT)

    @pl.when(j == 0)
    def _():
        send[0] = total.astype(LOW)

    @pl.when(j == 1)
    def _():
        keep[0] = total.astype(LOW)

    mine = jnp.full(x.shape[1:], j) == 1
    normed, _ = center_rows(jnp.where(mine, x[0], x_far[0]).astype(F32))
    terms = jnp.concatenate([column_sum(total * normed), column_sum(total)], axis=0)
    start = (m == 0) & (j == 0) & (i == 0)

    @pl.when(start)
    def _():
        sums[...] = terms

    @pl.when(~start)
    def _():
        sums[...] += terms


def rows_back_call(line, grads, w, x, x_far, step):
    count, rows, width = x.shape
    total, local = 2 * count * rows, w.shape[2]
    blocks, place, send, keep = own_rows(rows, step)
    out = shape((count, rows, width), LOW)
    block = (1, step, width)
    return line.run(
        rows_back_kernel,
        "rows_back",
        (count, 2, blocks),
        [(g, pl.BlockSpec((step, local), place)) for g in grads]
        + [(w, whole(w.shape, pipeline_mode=pl.Buffered(1)))]
        + [(v, pl.BlockSpec((1, step, width), lambda m, j, i, s: (m, i, 0))) for v in (x, x_far)],
        [
            (out, pl.BlockSpec(block, keep)),
            (out, pl.BlockSpec(block, send)),
            (shape((2, width), F32), whole((2, width))),
        ],
        flops=6 * total * width * local,
    )


def tokens_back_kernel(sc, x, dh, own, got, gain, out):
    normed, inv_std = center_rows(x[0].astype(F32))
    da1 = own[0].astype(F32) + got[0].astype(F32)
    back = norm_back(normed, inv_std, da1 * gain[...])
    out[0, 0] = (dh[...].astype(F32) + back).astype(LOW)


def tokens_back_call(line, x, dh, own, got, gain, step):
    count, rows, width = own.shape
    blocks = rows // step
    block = pl.BlockSpec((1, step, width), lambda m, i, s: (m, i, 0))
    natural = pl.BlockSpec((step, width), lambda m, i, s: ((2 * m + s[S_T]) * blocks + i, 0))
    return line.run(
        tokens_back_kernel,
        "tokens_back",
        (count, blocks),
        [(x, block), (dh, natural), (own, block), (got, block), (gain, whole((1, width)))],
        [
            (
                shape((count, 1, rows, width), LOW),
                pl.BlockSpec((1, 1, step, width), lambda m, i, s: (m, 0, i, 0)),
            )
        ],
    )[0]


def swap(value):
    return lax.ppermute(value, "tensor", [(0, 1), (1, 0)])


def vector_kernel(sc, one, two, out):
    out[...] = one[...] + two[...]


class Vectors:
    def __init__(self, line, dp_count, values, shared):
        self.line, self.dp_count, self.values = line, dp_count, values
        rows = lax.broadcasted_iota(jnp.int32, (values.shape[0], 1), 0)
        self.got = swap(jnp.where(rows < shared, values, 0.0))
        self.mask = 1
        if dp_count & (dp_count - 1):
            self.values, self.got = lax.psum(values + self.got, "dp"), None

    def rest(self):
        while self.got is not None and self.mask < self.dp_count:
            self.advance()
        got = jnp.zeros_like(self.values) if self.got is None else self.got
        return [self.values, got]

    def advance(self):
        if self.got is None:
            return
        dims = self.values.shape
        self.values = self.line.run(
            vector_kernel,
            "add_vectors",
            (1,),
            [(a, whole(dims)) for a in (self.values, self.got)],
            [(jax.ShapeDtypeStruct(dims, F32), whole(dims))],
            mib=8,
        )[0]
        self.got = move(self.values, self.dp_count, self.mask) if self.mask < self.dp_count else None
        self.mask *= 2


def head_places(pairs, out_width):
    sides = [0, 0]
    places, out_places = [], []
    for pair in range(pairs):
        side = pair * 2 // pairs
        places.append((side, sides[side]))
        sides[side] += 384
    for side in range(2 if out_width else 0):
        wide = out_width // 2
        out_places.append((side, sides[side], side * wide, wide))
        sides[side] += wide
    return places, out_places, sides


def local(
    tokens,
    d_mixed,
    phone_len,
    frame_len,
    ln1_gain,
    ln1_bias,
    w_qkv,
    w_out,
    attn_bias,
    ln2_gain,
    ln2_bias,
    w_up,
    up_bias,
    w_down,
    down_bias,
):
    count, _, rows, width = tokens.shape
    dp_count = lax.axis_size("dp")
    slot = 2 * rows
    local_width = w_qkv.shape[2]
    units = w_up.shape[1]
    shard_rows = width // dp_count
    step = rows
    row = lambda v: v.reshape(1, -1)
    x, dm = tokens[:, 0], d_mixed[:, 0]
    phones = phone_len[:, 0]
    sc = jnp.concatenate(
        [
            jnp.stack([lax.axis_index("tensor"), lax.axis_index("dp")]).astype(jnp.int32),
            phones + frame_len[:, 0],
            phones,
        ]
    )
    line = Line(sc)
    w3 = jnp.transpose(w_qkv, (1, 0, 2))
    g1, b1, g2, b2 = row(ln1_gain), row(ln1_bias), row(ln2_gain), row(ln2_bias)
    flat = lambda v: v.reshape(count * slot, v.shape[-1])

    x_far, dm_far, w_out_far = swap(x), swap(dm), swap(w_out)
    x_near, w_near = bring([x, w3])
    a1, *qkv, ctx, probs, inv = front_call(line, x_near, x_far, g1, b1, w_near)
    ctx_far = swap(ctx)
    en = mark_call(line, dm, dm_far)
    h, a2 = project_call(line, ctx, ctx_far, w_out, w_out_far, x, x_far, row(attn_bias), g2, b2)

    chunks = (units // 2, units // 2)
    reds, acts, dus, up_sums, at = [], [], [], [], 0
    for chunk in chunks:
        shards = Shards(dp_count, width, (chunk, chunk))
        (act, du, up_sum), grads = feed_call(
            line, shards, a2, en, w_up, w_down, row(up_bias), at, chunk
        )
        reds.append(Reduction(line, shards, grads))
        acts.append(act)
        dus.append(du)
        up_sums.append(up_sum)
        at += chunk
    da = up_back_call(line, dus, w_up, step)
    da_far = swap(da)
    red1, red2 = reds
    red1.advance()
    dhb, dctx, hidden_sums = hidden_back_call(line, rows, da, da_far, h, en, g2, w_out, step)
    own_down, far_down = down_call(line, count, rows, acts, w_down, step)
    far_down = swap(far_down)
    red2.advance()
    mixed = mixed_call(line, h, own_down, far_down, row(down_bias), step // 2)
    red1.advance()

    pairs = local_width // 128
    dctx = dctx.reshape(count, slot, local_width)
    half = pairs // 2
    places3, outs3, sides3 = head_places(half, local_width)
    places4, _, sides4 = head_places(pairs - half, 0)
    shards3, shards4 = Shards(dp_count, width, sides3), Shards(dp_count, width, sides4)
    rest = (qkv, ctx, inv, dctx, probs, flat(a1))
    grads, parts = attend_back_call(line, shards3, 0, places3, outs3, *rest, (dhb, flat(ctx)))
    red3 = Reduction(line, shards3, parts)
    red2.advance()
    red1.advance()
    grads, parts = attend_back_call(line, shards4, half, places4, [], *rest, (), grads)
    red4 = Reduction(line, shards4, parts)
    feed_dims = [(shard_rows, units)] * 2
    feed_places = lambda at, chunk: [(n, None, at, n * chunk, chunk) for n in range(2)]
    red3.advance()
    red2.advance()
    own, far, token_sums = rows_back_call(
        line, [flat(g) for g in grads], w3, x, x_far, step
    )
    far = swap(far)
    up_rows = [v.reshape(-1, width) for v in up_sums]
    sums = Vectors(line, dp_count, jnp.concatenate([token_sums, hidden_sums, *up_rows]), 6)
    red3.advance()
    red4.advance()
    sums.advance()
    d_tokens = tokens_back_call(line, x, dhb, own, far, g1, step // 2)
    sums.advance()
    feed_grads, _ = last_call(line, [(red1, feed_places(0, chunks[0]))], feed_dims)
    red3.advance()
    red4.advance()
    sums.advance()
    (grad_down, grad_up), _ = last_call(
        line, [(red2, feed_places(chunks[0], chunks[1]))], feed_dims, before=feed_grads
    )
    sums.advance()
    red4.advance()

    def head_plan(at, pair_places, out_places, sides):
        starts = [sum(sides[:n]) for n in range(len(sides))]
        plan = []
        for g, (side, column) in enumerate(pair_places):
            for c in range(3):
                plan.append((0, c, (at + g) * 128, starts[side] + column + c * 128, 128))
        for side, column, first, wide in out_places:
            plan.append((1, None, first, starts[side] + column, wide))
        return plan

    (grad_qkv, grad_out), vectors = last_call(
        line,
        [
            (red3, head_plan(0, places3, outs3, sides3)),
            (red4, head_plan(half, places4, [], sides4)),
        ],
        [(3, shard_rows, local_width), (shard_rows, local_width)],
        sums,
    )

    return (
        mixed,
        d_tokens,
        vectors[0],
        vectors[1],
        jnp.transpose(grad_qkv, (1, 0, 2)),
        grad_out.T,
        vectors[2],
        vectors[3],
        vectors[4],
        grad_up,
        vectors[6],
        grad_down.T,
        vectors[5],
    )


def solution(mesh):
    in_specs = (
        P(None, "dp", "tensor", None),
        P(None, "dp", "tensor", None),
        P(None, "dp"),
        P(None, "dp"),
        P(),
        P(),
        P(None, None, "tensor"),
        P("tensor", None),
        P(),
        P(),
        P(),
        P(None, "tensor"),
        P("tensor"),
        P("tensor", None),
        P(),
    )
    out_specs = (
        P(None, "dp", "tensor", None),
        P(None, "dp", "tensor", None),
        P(),
        P(),
        P("dp", None, "tensor"),
        P("tensor", "dp"),
        P(),
        P(),
        P(),
        P("dp", "tensor"),
        P("tensor"),
        P("tensor", "dp"),
        P(),
    )
    return jax.shard_map(local, mesh=mesh, in_specs=in_specs, out_specs=out_specs, check_vma=False)
```

```python
import math

import jax
import jax.numpy as jnp
from jax import lax
from jax.experimental import pallas as pl
from jax.experimental.pallas import tpu as pltpu
from jax.sharding import PartitionSpec as P

HD = 64
EPS = 1e-05
LOW = jnp.bfloat16
F32 = jnp.float32
NT = (((1,), (1,)), ((), ()))
TN = (((0,), (0,)), ((), ()))
GELU_A = math.sqrt(2.0 / math.pi)
GELU_B = 0.044715

S_T, S_DP, S_LEN, S_PH = 0, 1, 2, 4


def dot(a, b, dims=(((1,), (0,)), ((), ()))):
    return lax.dot_general(a, b, dims, preferred_element_type=F32)


def shape(dims, dtype):
    if math.prod(dims) * jnp.dtype(dtype).itemsize >= 1 << 17:
        return pltpu.HBM(dims, dtype)
    return jax.ShapeDtypeStruct(dims, dtype)


def near(dims, dtype):
    return pltpu.VMEM(dims, dtype)


def whole(dims, **more):
    return pl.BlockSpec(dims, lambda *_: (0,) * len(dims), **more)


def anywhere():
    return pl.BlockSpec(memory_space=pl.ANY)


ADD_FLOPS = 3e10


class Line:
    def __init__(self, sc):
        self.sc = sc
        self.token = jnp.zeros((8, 128), F32)
        self.pending, self.carried = [], []

    def run(self, kernel, name, grid, ins, outs, scratch=(), mib=24, flops=0, aliases=None):
        count_in, count_out = len(ins), len(outs)
        through, self.pending = [self.token, *self.pending], []
        extra = len(through)

        def body(*refs):
            mid = 1 + count_in
            end = mid + extra + count_out
            kernel(*refs[:mid], *refs[mid + extra : end], *refs[end + extra :])

        arrays = [a for a, _ in ins]
        nbytes = sum(math.prod(a.shape) * a.dtype.itemsize for a in arrays)
        aliases = {1 + i: o for i, o in (aliases or {}).items()}
        aliases.update({1 + count_in + n: count_out + n for n in range(extra)})
        found = pl.pallas_call(
            body,
            grid_spec=pltpu.PrefetchScalarGridSpec(
                num_scalar_prefetch=1,
                grid=grid,
                in_specs=[s for _, s in ins] + [anywhere()] * extra,
                out_specs=[s for _, s in outs] + [anywhere()] * extra,
                scratch_shapes=list(scratch),
            ),
            out_shape=[o for o, _ in outs]
            + [jax.ShapeDtypeStruct(t.shape, t.dtype) for t in through],
            input_output_aliases=aliases,
            compiler_params=pltpu.CompilerParams(vmem_limit_bytes=mib << 20),
            cost_estimate=pl.CostEstimate(
                flops=int(flops * 1), bytes_accessed=int(nbytes * 1), transcendentals=0
            ),
            name=name,
        )(self.sc, *arrays, *through)
        self.token, self.carried = found[count_out], list(found[count_out + 1 :])
        return found[:count_out]


def center_rows(values):
    center = values - jnp.mean(values, axis=-1, keepdims=True)
    inv_std = lax.rsqrt(jnp.mean(center * center, axis=-1, keepdims=True) + EPS)
    return center * inv_std, inv_std


def norm_back(normed, inv_std, t):
    return inv_std * (
        t
        - jnp.mean(t, axis=-1, keepdims=True)
        - normed * jnp.mean(t * normed, axis=-1, keepdims=True)
    )


def column_sum(values):
    return jnp.sum(values, axis=0, keepdims=True)


def bring(arrays):
    vm = pl.BlockSpec(memory_space=pltpu.VMEM)
    hbm = pl.BlockSpec(memory_space=pltpu.HBM)

    def kernel(*refs):
        count = len(arrays)
        sems = refs[-1]
        copies = [
            pltpu.make_async_copy(source, target, sems.at[n])
            for n, (source, target) in enumerate(zip(refs[:count], refs[count:-1]))
        ]
        for copy in copies:
            copy.start()
        for copy in copies:
            copy.wait()

    return pl.pallas_call(
        kernel,
        in_specs=[hbm] * len(arrays),
        out_specs=[vm] * len(arrays),
        out_shape=[near(a.shape, a.dtype) for a in arrays],
        scratch_shapes=[pltpu.SemaphoreType.DMA((len(arrays),))],
        compiler_params=pltpu.CompilerParams(vmem_limit_bytes=4 << 20),
        name="bring",
    )(*arrays)


def splits(slot):
    half = slot // 2
    cut = -(-half // 128) * 128
    return [(0, cut, cut), (cut, slot, slot)]


def front_kernel(
    sc, x, x_far, gain, shift, w,
    a1, q, k, v, ctx, probs, inv,
    low, qkv, bias, sem,
):
    m, j = pl.program_id(0), pl.program_id(1)
    rows = x.shape[1]
    slot = 2 * rows
    local = w.shape[2]
    here = pl.multiple_of(sc[S_T] * rows, rows)
    there = pl.multiple_of((1 - sc[S_T]) * rows, rows)

    def copy():
        return pltpu.make_async_copy(low, a1.at[m], sem.at[0])

    @pl.when(j == 0)
    def _():
        for source, at in ((x, here), (x_far, there)):
            normed, _ = center_rows(source[0].astype(F32))
            low[pl.ds(at, rows), :] = (normed * gain[...] + shift[...]).astype(LOW)
        copy().start()
        for c in range(3):
            qkv[:, c * local : (c + 1) * local] = dot(low[...], w[c]).astype(LOW)
        qi = lax.broadcasted_iota(jnp.int32, (slot, slot), 0)
        ki = lax.broadcasted_iota(jnp.int32, (slot, slot), 1)
        bias[...] = jnp.where((ki <= qi) | (ki < sc[S_PH + m]), 0.0, -1e30)

    def part(c):
        return qkv[:, pl.ds(pl.multiple_of(c * local + j * 128, 128), 128)]

    lane = lax.broadcasted_iota(jnp.int32, (slot, 128), 1) < HD
    query_all, key, value = part(0), part(1), part(2)
    q[0], k[0], v[0] = query_all, key, value
    widened = jnp.concatenate([value, jnp.ones_like(value)], axis=1)
    for lo, hi, ext in splits(slot):
        query = query_all[lo:hi] * LOW(1.0 / math.sqrt(HD))
        first = lane[lo:hi]
        sums = []
        for h in range(2):
            masked = jnp.where(first if h == 0 else ~first, query, LOW(0))
            s = dot(masked, key[:ext], NT) + bias[lo:hi, :ext]
            p = jnp.exp(s - jnp.max(s, axis=1, keepdims=True)).astype(LOW)
            probs[0, h, lo:hi, :ext] = p
            sums.append(dot(p, widened[:ext]))
        total = jnp.where(first, sums[0][:, :128], sums[1][:, :128])
        scale = 1.0 / jnp.where(first, sums[0][:, 128:], sums[1][:, 128:])
        ctx[0, lo:hi, :] = (total * scale).astype(LOW)
        inv[0, lo:hi, :] = scale.astype(LOW)

    @pl.when(j == pl.num_programs(1) - 1)
    def _():
        copy().wait()


def front_call(line, x, x_far, gain, shift, w):
    count, rows, width = x.shape
    slot, local = 2 * rows, w.shape[2]
    heads = local // HD
    own = pl.BlockSpec((1, rows, width), lambda m, j, s: (m, 0, 0))
    pair = pl.BlockSpec((1, slot, 128), lambda m, j, s: (m, 0, j))
    natural = shape((count, slot, width), LOW)
    heads_out = shape((count, slot, local), LOW)
    return line.run(
        front_kernel,
        "norm_attend",
        (count, local // 128),
        [(x, own), (x_far, own)]
        + [(gain, whole((1, width))), (shift, whole((1, width)))]
        + [(w, whole(w.shape, pipeline_mode=pl.Buffered(1)))],
        [(natural, anywhere())]
        + [(heads_out, pair)] * 4
        + [
            (
                shape((count, heads, slot, slot), LOW),
                pl.BlockSpec((1, 2, slot, slot), lambda m, j, s: (m, j, 0, 0)),
            ),
            (heads_out, pair),
        ],
        scratch=[
            pltpu.VMEM((slot, width), LOW),
            pltpu.VMEM((slot, 3 * local), LOW),
            pltpu.VMEM((slot, slot), F32),
            pltpu.SemaphoreType.DMA((1,)),
        ],
        mib=30,
        flops=2e10,
    )


def mark_kernel(sc, dm, dm_far, e):
    m, half = pl.program_id(0), pl.program_id(1)
    rows = dm.shape[1]
    mine = jnp.full(dm.shape[1:], half) == sc[S_T]
    ids = half * rows + lax.broadcasted_iota(jnp.int32, (rows, 1), 0)
    e[...] = jnp.where(ids < sc[S_LEN + m], jnp.where(mine, dm[0], dm_far[0]), LOW(0))


def mark_call(line, dm, dm_far):
    count, rows, width = dm.shape
    held = pl.BlockSpec((1, rows, width), lambda m, i, s: (m, 0, 0))
    return line.run(
        mark_kernel,
        "mark_rows",
        (count, 2),
        [(dm, held), (dm_far, held)],
        [(near((2 * count * rows, width), LOW), pl.BlockSpec((rows, width), lambda m, i, s: (2 * m + i, 0)))],
    )[0]


def project_kernel(sc, ctx, far, w, w_far, x, x_far, bias, gain, shift, h, a2):
    m, half = pl.program_id(0), pl.program_id(1)
    mine = jnp.full(x.shape[1:], half) == sc[S_T]
    both = dot(ctx[0], w[...]) + dot(far[0], w_far[...])
    hidden = jnp.where(mine, x[0], x_far[0]).astype(F32) + both + bias[...]
    h[...] = hidden.astype(LOW)
    normed, _ = center_rows(hidden)
    a2[...] = (normed * gain[...] + shift[...]).astype(LOW)


def project_call(line, ctx, far, w, w_far, x, x_far, bias, gain, shift):
    count, rows, width = x.shape
    local = ctx.shape[2]
    strip = pl.BlockSpec((1, rows, local), lambda m, i, s: (m, i, 0))
    held = pl.BlockSpec((1, rows, width), lambda m, i, s: (m, 0, 0))
    one = whole((1, width))
    out = (shape((2 * count * rows, width), LOW), pl.BlockSpec((rows, width), lambda m, i, s: (2 * m + i, 0)))
    return line.run(
        project_kernel,
        "project",
        (count, 2),
        [(ctx, strip), (far, strip), (w, whole(w.shape)), (w_far, whole(w.shape))]
        + [(x, held), (x_far, held)]
        + [(bias, one), (gain, one), (shift, one)],
        [out, (near((2 * count * rows, width), LOW), out[1])],
        flops=4 * count * rows * width * width,
    )


class Shards:
    def __init__(self, dp_count, width, sides):
        self.dp_count = dp_count
        self.width = width
        self.rows = width // dp_count
        self.sides = sides
        self.bits = dp_count.bit_length() - 1
        self.halving = dp_count == 1 << self.bits and self.bits > 2 and self.rows % 16 == 0
        late = list(range(3, self.bits))
        orders = ([0, 1, 2], [1, 0, 2]) if len(sides) == 2 else ([0, 1, 2], [1, 2, 0], [2, 0, 1])
        self.orders = [order + late for order in orders]

    def outs(self):
        if not self.halving:
            return [jax.ShapeDtypeStruct((self.width, n), LOW) for n in self.sides]
        return [
            kind((self.dp_count // 2, self.rows, n), LOW)
            for n in self.sides
            for kind in (pltpu.HBM, near if sum(self.sides) < 0 else pltpu.HBM)
        ]

    def emit(self, sc, value, side, at, refs):
        value = value.astype(LOW)
        span = slice(at, at + value.shape[1])
        if not self.halving:
            refs[side][:, span] = value
            return
        send, keep = refs[2 * side], refs[2 * side + 1]
        blocks = value.reshape(self.dp_count, self.rows, value.shape[1])
        order = self.orders[side]
        mine = jnp.full((self.rows, value.shape[1]), (sc[S_DP] >> order[0]) & 1) == 1
        for i in range(self.dp_count // 2):
            at_zero = sum(((i >> n) & 1) << bit for n, bit in enumerate(order[1:]))
            zero = blocks[at_zero]
            one = blocks[at_zero + (1 << order[0])]
            send[i, :, span] = jnp.where(mine, zero, one)
            keep[i, :, span] = jnp.where(mine, one, zero)


def split_kernel(bits, sc, *refs):
    sides = len(bits)
    ins, outs = refs[: 2 * sides], refs[2 * sides :]
    joined = len(outs) == 2
    at = 0
    for n, bit in enumerate(bits):
        keep, got = ins[2 * n], ins[2 * n + 1]
        send_out, keep_out = outs[:2] if joined else outs[2 * n : 2 * n + 2]
        columns = keep.shape[2]
        mine = (sc[S_DP] >> bit) & 1
        for j, ref in ((1 - mine, send_out), (mine, keep_out)):
            total = (keep[j].astype(F32) + got[j].astype(F32)).astype(LOW)
            ref[0, :, at : at + columns] = total
        if joined:
            at += columns


def far_keep_kernel(bits, sc, *refs):
    sides = len(bits)
    keeps, gots, outs = refs[:sides], refs[sides : 2 * sides], refs[2 * sides : 4 * sides]
    held, sems = refs[4 * sides : 5 * sides], refs[-1]
    i, blocks = pl.program_id(0), keeps[0].shape[0] // 2

    def copy(n, side):
        span = pl.ds(2 * n, 2)
        return pltpu.make_async_copy(keeps[side].at[span], held[side].at[span], sems.at[n, side])

    @pl.when(i == 0)
    def _():
        for n in range(blocks):
            for side in range(sides):
                copy(n, side).start()

    for n in range(blocks):

        @pl.when(i == n)
        def _():
            for side in range(sides):
                copy(n, side).wait()

    for side, bit in enumerate(bits):
        mine = (sc[S_DP] >> bit) & 1
        for j, ref in ((1 - mine, outs[2 * side]), (mine, outs[2 * side + 1])):
            keep = held[side][2 * i + j]
            ref[0] = (keep.astype(F32) + gots[side][j].astype(F32)).astype(LOW)


def far_keep_call(line, bits, args, flops):
    blocks, rows, _ = args[0].shape
    keeps, gots = args[::2], args[1::2]
    return line.run(
        lambda *refs: far_keep_kernel(bits, *refs),
        "add_far",
        (blocks // 2,),
        [(a, pl.BlockSpec(memory_space=pltpu.HBM)) for a in keeps]
        + [(a, pl.BlockSpec((2, rows, a.shape[2]), lambda i, s: (i, 0, 0))) for a in gots],
        [
            (
                jax.ShapeDtypeStruct((blocks // 2, rows, a.shape[2]), LOW),
                pl.BlockSpec((1, rows, a.shape[2]), lambda i, s: (i, 0, 0)),
            )
            for a in keeps
            for _ in range(2)
        ],
        scratch=[pltpu.VMEM(a.shape, LOW) for a in keeps]
        + [pltpu.SemaphoreType.DMA((blocks // 2, len(keeps)))],
        mib=12,
        flops=flops,
    )


def split_call(line, bits, args, widths, name, flops):
    blocks, rows, _ = args[0].shape
    if len(widths) == len(bits) > 1 and sum(math.prod(a.shape) for a in args) >= 1 << 21:
        return far_keep_call(line, bits, args, flops)
    return line.run(
        lambda *refs: split_kernel(bits, *refs),
        name,
        (blocks // 2,),
        [(a, pl.BlockSpec((2, rows, a.shape[2]), lambda i, s: (i, 0, 0))) for a in args],
        [
            (
                jax.ShapeDtypeStruct((blocks // 2, rows, n), LOW),
                pl.BlockSpec((1, rows, n), lambda i, s: (i, 0, 0)),
            )
            for n in widths
            for _ in range(2)
        ],
        mib=12,
        flops=flops,
    )


def move(value, dp_count, mask):
    return lax.ppermute(value, "dp", [(i, i ^ mask) for i in range(dp_count)])


class Reduction:
    def __init__(self, line, shards, arrays):
        self.line, self.shards = line, shards
        self.step = 0
        if not shards.halving:
            self.keep = jnp.concatenate(
                [
                    lax.psum_scatter(a.astype(F32), "dp", scatter_dimension=0, tiled=True)
                    for a in arrays
                ],
                axis=1,
            )
            self.got, self.step = [], shards.bits
            return
        self.orders = shards.orders
        self.sides = shards.sides
        self.keep = arrays[1::2]
        self.send(arrays[::2])

    def send(self, arrays):
        count = self.shards.dp_count
        self.got = [
            lax.ppermute(a, "dp", [(i, i ^ (1 << order[self.step])) for i in range(count)])
            for a, order in zip(arrays, self.orders)
        ]
        self.step += 1

    def advance(self, flops=ADD_FLOPS):
        if self.step >= self.shards.bits:
            return
        bits = [order[self.step] for order in self.orders]
        joined = all(order[self.step :] == self.orders[0][self.step :] for order in self.orders)
        args = [a for pair in zip(self.keep, self.got) for a in pair]
        widths = [sum(self.sides)] if joined else self.sides
        found = split_call(self.line, bits, args, widths, "add_split", flops)
        if joined:
            self.orders, self.sides = self.orders[:1], widths
        self.keep = found[1::2]
        self.send(found[::2])

    def rest(self):
        while self.step < self.shards.bits:
            self.advance()
        if not self.shards.halving:
            return [self.keep]
        return [v[0].reshape(v[0].shape[-2:]) for v in (self.keep, self.got)]


def last_kernel(plans, terms, rest, count_out, sc, *refs):
    groups = len(plans)
    values, sems = refs[-1 - groups : -1], refs[-1]
    made = refs[: -1 - groups]
    outs, vectors = made[len(made) - count_out :], []
    if rest is not None:
        outs, vectors = outs[: count_out - rest - 1], outs[count_out - rest - 1 :]
    copies, at, used = [], 0, 0
    for plan, count, value in zip(plans, terms, values):
        total = refs[at][...].astype(F32)
        for ref in refs[at + 1 : at + count]:
            total = total + ref[...].astype(F32)
        at += count
        value[...] = total
        for out, lead, column, source, columns in plan:
            target = outs[out] if lead is None else outs[out].at[lead]
            copy = pltpu.make_async_copy(
                value.at[:, pl.ds(source, columns)],
                target.at[:, pl.ds(column, columns)],
                sems.at[used],
            )
            used += 1
            copy.start()
            copies.append(copy)
    if rest is not None:
        write_vectors(refs[at][...] + refs[at + 1][...], vectors)
    for copy in copies:
        copy.wait()


def write_vectors(total, outs):
    for n, out in enumerate(outs[:-1]):
        out[...] = total[n : n + 1, :]
    rest, width = len(outs) - 1, total.shape[1]
    for n in range(rest, total.shape[0]):
        outs[-1][:, (n - rest) * width : (n - rest + 1) * width] = total[n : n + 1, :]


def last_call(line, groups, out_dims, sums=None, rest=6, before=()):
    ins, plans, terms, scratch = [], [], [], []
    for red, plan in groups:
        arrays = red.rest()
        ins += [(a, whole(a.shape)) for a in arrays]
        plans.append(plan)
        terms.append(len(arrays))
        scratch.append(pltpu.VMEM(arrays[0].shape, F32))
    outs = [(pltpu.HBM(d, F32), anywhere()) for d in out_dims]
    if sums is not None:
        pair = sums.rest()
        ins += [(a, whole(a.shape)) for a in pair]
        count, width = pair[0].shape
        for d in [(1, width)] * rest + [(1, (count - rest) * width)]:
            outs.append((jax.ShapeDtypeStruct(d, F32), whole(d)))
    aliases = {len(ins) + n: n for n in range(len(before))}
    ins += [(b, anywhere()) for b in before]
    found = line.run(
        lambda *refs: last_kernel(plans, terms, None if sums is None else rest, len(outs), *refs),
        "add_last",
        (1,),
        ins,
        outs,
        scratch=scratch + [pltpu.SemaphoreType.DMA((sum(len(p) for p in plans),))],
        mib=12,
        aliases=aliases,
    )
    return found[: len(out_dims)], [v.reshape(-1) for v in found[len(out_dims) :]]


def gelu_both(u):
    square = u * u
    t = jnp.tanh(u * (GELU_A + (GELU_A * GELU_B) * square))
    half = 0.5 + 0.5 * t
    slope = half + (0.5 * u) * (1.0 - t * t) * (GELU_A + (3.0 * GELU_A * GELU_B) * square)
    return u * half, slope


def feed_kernel(shards, sc, a2, e, wu, wd, ub, gb, du, bias, *grads):
    rows = a2.shape[0]
    step = rows // 2
    total = jnp.zeros(bias.shape, F32)
    for r in range(0, rows, step):
        u = dot(a2[r : r + step, :], wu[...]) + ub[...]
        act, slope = gelu_both(u)
        gb[r : r + step, :] = act.astype(LOW)
        low = (dot(e[r : r + step, :], wd[...], NT) * slope).astype(LOW)
        du[r : r + step, :] = low
        total = total + column_sum(low.astype(F32))
    bias[...] = total
    shards.emit(sc, dot(e[...], gb[...], TN), 0, 0, grads)
    shards.emit(sc, dot(a2[...], du[...], TN), 1, 0, grads)


def feed_call(line, shards, a2, e, w_up, w_down, up_bias, at, chunk, tile=512):
    rows, width = a2.shape
    tile = min(tile, chunk)
    first = at // tile
    one = pl.Buffered(1)
    strip = pl.BlockSpec((rows, tile), lambda i, s: (0, i))
    outs = [(shape((rows, chunk), LOW), strip), (near((rows, chunk), LOW), strip)]
    outs.append((shape((1, chunk), F32), pl.BlockSpec((1, tile), lambda i, s: (0, i))))
    for o in shards.outs():
        block = o.shape[:-1] + (tile,)
        lead = (0,) * (len(block) - 1)
        outs.append((o, pl.BlockSpec(block, lambda i, s, lead=lead: (*lead, i))))
    found = line.run(
        lambda *refs: feed_kernel(shards, *refs),
        "feed_forward",
        (chunk // tile,),
        [
            (a2, whole(a2.shape, pipeline_mode=one)),
            (e, whole(e.shape, pipeline_mode=one)),
            (w_up, pl.BlockSpec((width, tile), lambda i, s: (0, first + i))),
            (w_down, pl.BlockSpec((tile, width), lambda i, s: (first + i, 0))),
            (up_bias, pl.BlockSpec((1, tile), lambda i, s: (0, first + i))),
        ],
        outs,
        mib=40,
        flops=8 * rows * width * chunk,
    )
    return found[:3], found[3:]


def up_back_kernel(sc, *refs):
    dus, (w, out) = refs[:-2], refs[-2:]
    total, at = None, 0
    for du in dus:
        term = dot(du[...], w[:, at : at + du.shape[1]], NT)
        at += du.shape[1]
        total = term if total is None else total + term
    out[...] = total.astype(LOW)


def up_back_call(line, dus, w_up, step):
    rows = dus[0].shape[0]
    width, units = w_up.shape
    return line.run(
        up_back_kernel,
        "up_back",
        (rows // step,),
        [(du, pl.BlockSpec((step, du.shape[1]), lambda i, s: (i, 0))) for du in dus]
        + [(w_up, whole(w_up.shape, pipeline_mode=pl.Buffered(1)))],
        [(shape((rows, width), LOW), pl.BlockSpec((step, width), lambda i, s: (i, 0)))],
        mib=32,
        flops=2 * rows * width * units,
    )[0]


def own_rows(rows, step):
    blocks = rows // step

    def place(m, j, i, s):
        half = jnp.where(j == 1, s[S_T], 1 - s[S_T])
        return ((2 * m + half) * blocks + i, 0)

    def send(m, j, i, s):
        return (m, jnp.where(j == 0, i, blocks - 1), 0)

    def keep(m, j, i, s):
        return (m, jnp.where(j == 1, i, 0), 0)

    return blocks, place, send, keep


def down_kernel(sc, *refs):
    acts, (w, keep, send) = refs[:-3], refs[-3:]
    total, at = None, 0
    for act in acts:
        term = dot(act[...], w[at : at + act.shape[1], :])
        at += act.shape[1]
        total = term if total is None else total + term

    @pl.when(pl.program_id(1) == 0)
    def _():
        send[0] = total.astype(LOW)

    @pl.when(pl.program_id(1) == 1)
    def _():
        keep[0] = total.astype(LOW)


def down_call(line, count, rows, acts, w, step):
    width = w.shape[1]
    blocks, place, send, keep = own_rows(rows, step)
    out = shape((count, rows, width), LOW)
    block = (1, step, width)
    return line.run(
        down_kernel,
        "feed_down",
        (count, 2, blocks),
        [(a, pl.BlockSpec((step, a.shape[1]), place)) for a in acts]
        + [(w, whole(w.shape, pipeline_mode=pl.Buffered(1)))],
        [(out, pl.BlockSpec(block, keep)), (out, pl.BlockSpec(block, send))],
        flops=4 * count * rows * w.shape[0] * width,
    )


def mixed_kernel(sc, h, own, got, bias, out):
    m, i = pl.program_id(0), pl.program_id(1)
    rows = own.shape[1]
    first = sc[S_T] * rows * pl.num_programs(1) + i * rows
    ids = first + lax.broadcasted_iota(jnp.int32, (rows, 1), 0)
    value = h[...].astype(F32) + (own[0].astype(F32) + got[0].astype(F32)) + bias[...]
    out[0, 0] = jnp.where(ids < sc[S_LEN + m], value, 0.0).astype(LOW)


def mixed_call(line, h, own, got, bias, step):
    count, rows, width = own.shape
    blocks = rows // step
    block = pl.BlockSpec((1, step, width), lambda m, i, s: (m, i, 0))
    natural = pl.BlockSpec((step, width), lambda m, i, s: ((2 * m + s[S_T]) * blocks + i, 0))
    return line.run(
        mixed_kernel,
        "mixed_rows",
        (count, blocks),
        [(h, natural), (own, block), (got, block), (bias, whole((1, width)))],
        [
            (
                shape((count, 1, rows, width), LOW),
                pl.BlockSpec((1, 1, step, width), lambda m, i, s: (m, 0, i, 0)),
            )
        ],
    )[0]


def hidden_back_kernel(per_half, sc, da, got, h, e, gain, w, dhb, dctx, sums):
    i = pl.program_id(0)
    da2 = da[...].astype(F32) + got[...].astype(F32)
    normed, inv_std = center_rows(h[...].astype(F32))
    out_grad = e[...].astype(F32)
    low = (out_grad + norm_back(normed, inv_std, da2 * gain[...])).astype(LOW)
    dhb[...] = low
    dctx[...] = dot(low, w[...], NT).astype(LOW)
    own = jnp.where((i // per_half) % 2 == sc[S_T], 1.0, 0.0)
    terms = jnp.concatenate(
        [
            column_sum(low.astype(F32)),
            column_sum(da2 * normed),
            column_sum(da2),
            column_sum(out_grad),
        ],
        axis=0,
    )

    @pl.when(i == 0)
    def _():
        sums[...] = terms * own

    @pl.when(i > 0)
    def _():
        sums[...] += terms * own


def hidden_back_call(line, rows, da, got, h, e, gain, w, step):
    total, width = da.shape
    local = w.shape[0]
    strip = lambda wide: pl.BlockSpec((step, wide), lambda i, s: (i, 0))
    wide = strip(width)
    return line.run(
        lambda *refs: hidden_back_kernel(rows // step, *refs),
        "hidden_back",
        (total // step,),
        [(da, wide), (got, wide), (h, wide), (e, wide), (gain, whole((1, width))), (w, whole(w.shape))],
        [
            (shape((total, width), LOW), wide),
            (shape((total, local), LOW), strip(local)),
            (shape((4, width), F32), whole((4, width))),
        ],
        flops=2 * total * width * local,
    )


def attend_back_kernel(shards, pair_places, out_places, sc, q, k, v, ctx, inv, dctx, probs, a1_hbm, *refs):
    extra = [a1_hbm]
    group = len(pair_places)
    if out_places:
        extra, refs = extra + list(refs[:2]), refs[2:]
    pieces = len(shards.outs())
    refs = refs[-(3 + pieces + 1 + len(extra) + 1) :]
    dq, dk, dv = refs[:3]
    grads = refs[3 : 3 + pieces]
    rows_all = refs[3 + pieces]
    held = refs[4 + pieces : 4 + pieces + len(extra)]
    sems = refs[-1]
    j, m = pl.program_id(0), pl.program_id(1)

    def copies():
        return [
            pltpu.make_async_copy(source, target, sems.at[n])
            for n, (source, target) in enumerate(zip(extra, held))
        ]

    @pl.when((j == 0) & (m == 0))
    def _():
        for copy in copies():
            copy.start()

    slot = q.shape[1]
    lane = lax.broadcasted_iota(jnp.int32, (slot, 128), 1) < HD
    scaled = dctx[0].astype(F32) * inv[0].astype(F32)
    product = scaled * ctx[0].astype(F32)
    low = scaled.astype(LOW)
    key, query, value = k[0], q[0], v[0]
    cuts = splits(slot)
    per_head = []
    for h in range(2):
        here = lane if h == 0 else ~lane
        delta = jnp.sum(jnp.where(here, product, 0.0), axis=1, keepdims=True)
        masked = jnp.where(here, low, LOW(0))
        dqs, dks, dvs = [], [], []
        for lo, hi, ext in cuts:
            p = probs[0, h, lo:hi, :ext]
            dp = dot(masked[lo:hi], value[:ext], NT)
            ds = (p.astype(F32) * (dp - delta[lo:hi])).astype(LOW)
            dqs.append(dot(ds, key[:ext]))
            dks.append(dot(ds, query[lo:hi], TN))
            dvs.append(dot(p, low[lo:hi], TN))
        first = cuts[0][2]
        join = lambda two: jnp.concatenate([two[0] + two[1][:first], two[1][first:]], axis=0)
        per_head.append((jnp.concatenate(dqs, axis=0), join(dks), join(dvs)))
    root = 1.0 / math.sqrt(HD)
    start = pl.multiple_of(m * slot, slot)
    for c, (ref, scale) in enumerate(((dq, root), (dk, root), (dv, 1.0))):
        both = (jnp.where(lane, per_head[0][c], per_head[1][c]) * scale).astype(LOW)
        ref[0] = both
        rows_all[j, pl.ds(start, slot), c * 128 : (c + 1) * 128] = both

    @pl.when((m == pl.num_programs(1) - 1) & (j == group - 1))
    def _():
        for copy in copies():
            copy.wait()
        for g in range(group):
            side, column = pair_places[g]
            shards.emit(sc, dot(held[0][...], rows_all[g], TN), side, column, grads)
        for side, column, first, wide in out_places:
            term = dot(held[1][...], held[2][:, first : first + wide], TN)
            shards.emit(sc, term, side, column, grads)


def attend_back_call(
    line, shards, at, pair_places, out_places, qkv, ctx, inv, dctx, probs, a1, out_pair=(), before=None
):
    count, slot, local = ctx.shape
    group = len(pair_places)
    pair = pl.BlockSpec((1, slot, 128), lambda j, m, s: (m, 0, at + j))
    ins = [(a, pair) for a in (*qkv, ctx, inv, dctx)]
    ins.append((probs, pl.BlockSpec((1, 2, slot, slot), lambda j, m, s: (m, at + j, 0, 0))))
    extra = [a1, *out_pair]
    ins += [(a, pl.BlockSpec(memory_space=pltpu.HBM)) for a in extra]
    aliases = {}
    if before is not None:
        aliases = {len(ins) + i: i for i in range(3)}
        ins += [(b, anywhere()) for b in before]
    found = line.run(
        lambda *refs: attend_back_kernel(shards, pair_places, out_places, *refs),
        "attend_back",
        (group, count),
        ins,
        [(near((count, slot, local), LOW), pair)] * 3 + [(o, whole(o.shape)) for o in shards.outs()],
        scratch=[pltpu.VMEM((group, count * slot, 384), LOW)]
        + [pltpu.VMEM(a.shape, LOW) for a in extra]
        + [pltpu.SemaphoreType.DMA((len(extra),))],
        mib=32,
        flops=12e9,
        aliases=aliases,
    )
    return found[:3], found[3:]


def rows_back_kernel(sc, dq, dk, dv, w, x, x_far, keep, send, sums):
    m, j, i = pl.program_id(0), pl.program_id(1), pl.program_id(2)
    total = dot(dq[...], w[0], NT) + dot(dk[...], w[1], NT) + dot(dv[...], w[2], NT)

    @pl.when(j == 0)
    def _():
        send[0] = total.astype(LOW)

    @pl.when(j == 1)
    def _():
        keep[0] = total.astype(LOW)

    mine = jnp.full(x.shape[1:], j) == 1
    normed, _ = center_rows(jnp.where(mine, x[0], x_far[0]).astype(F32))
    terms = jnp.concatenate([column_sum(total * normed), column_sum(total)], axis=0)
    start = (m == 0) & (j == 0) & (i == 0)

    @pl.when(start)
    def _():
        sums[...] = terms

    @pl.when(~start)
    def _():
        sums[...] += terms


def rows_back_call(line, grads, w, x, x_far, step):
    count, rows, width = x.shape
    total, local = 2 * count * rows, w.shape[2]
    blocks, place, send, keep = own_rows(rows, step)
    out = shape((count, rows, width), LOW)
    block = (1, step, width)
    return line.run(
        rows_back_kernel,
        "rows_back",
        (count, 2, blocks),
        [(g, pl.BlockSpec((step, local), place)) for g in grads]
        + [(w, whole(w.shape, pipeline_mode=pl.Buffered(1)))]
        + [(v, pl.BlockSpec((1, step, width), lambda m, j, i, s: (m, i, 0))) for v in (x, x_far)],
        [
            (out, pl.BlockSpec(block, keep)),
            (out, pl.BlockSpec(block, send)),
            (shape((2, width), F32), whole((2, width))),
        ],
        flops=6 * total * width * local,
    )


def tokens_back_kernel(sc, x, dh, own, got, gain, out):
    normed, inv_std = center_rows(x[0].astype(F32))
    da1 = own[0].astype(F32) + got[0].astype(F32)
    back = norm_back(normed, inv_std, da1 * gain[...])
    out[0, 0] = (dh[...].astype(F32) + back).astype(LOW)


def tokens_back_call(line, x, dh, own, got, gain, step):
    count, rows, width = own.shape
    blocks = rows // step
    block = pl.BlockSpec((1, step, width), lambda m, i, s: (m, i, 0))
    natural = pl.BlockSpec((step, width), lambda m, i, s: ((2 * m + s[S_T]) * blocks + i, 0))
    return line.run(
        tokens_back_kernel,
        "tokens_back",
        (count, blocks),
        [(x, block), (dh, natural), (own, block), (got, block), (gain, whole((1, width)))],
        [
            (
                shape((count, 1, rows, width), LOW),
                pl.BlockSpec((1, 1, step, width), lambda m, i, s: (m, 0, i, 0)),
            )
        ],
    )[0]


def swap(value):
    return lax.ppermute(value, "tensor", [(0, 1), (1, 0)])


def vector_kernel(sc, one, two, out):
    out[...] = one[...] + two[...]


class Vectors:
    def __init__(self, line, dp_count, values, shared):
        self.line, self.dp_count, self.values = line, dp_count, values
        rows = lax.broadcasted_iota(jnp.int32, (values.shape[0], 1), 0)
        self.got = swap(jnp.where(rows < shared, values, 0.0))
        self.mask = 1
        if dp_count & (dp_count - 1):
            self.values, self.got = lax.psum(values + self.got, "dp"), None

    def rest(self):
        while self.got is not None and self.mask < self.dp_count:
            self.advance()
        got = jnp.zeros_like(self.values) if self.got is None else self.got
        return [self.values, got]

    def advance(self):
        if self.got is None:
            return
        dims = self.values.shape
        self.values = self.line.run(
            vector_kernel,
            "add_vectors",
            (1,),
            [(a, whole(dims)) for a in (self.values, self.got)],
            [(jax.ShapeDtypeStruct(dims, F32), whole(dims))],
            mib=8,
        )[0]
        self.got = move(self.values, self.dp_count, self.mask) if self.mask < self.dp_count else None
        self.mask *= 2


def head_places(pairs, out_width):
    sides = [0, 0]
    places, out_places = [], []
    for pair in range(pairs):
        side = pair * 2 // pairs
        places.append((side, sides[side]))
        sides[side] += 384
    for side in range(2 if out_width else 0):
        wide = out_width // 2
        out_places.append((side, sides[side], side * wide, wide))
        sides[side] += wide
    return places, out_places, sides


def local(
    tokens,
    d_mixed,
    phone_len,
    frame_len,
    ln1_gain,
    ln1_bias,
    w_qkv,
    w_out,
    attn_bias,
    ln2_gain,
    ln2_bias,
    w_up,
    up_bias,
    w_down,
    down_bias,
):
    count, _, rows, width = tokens.shape
    dp_count = lax.axis_size("dp")
    slot = 2 * rows
    local_width = w_qkv.shape[2]
    units = w_up.shape[1]
    shard_rows = width // dp_count
    step = rows
    row = lambda v: v.reshape(1, -1)
    x, dm = tokens[:, 0], d_mixed[:, 0]
    phones = phone_len[:, 0]
    sc = jnp.concatenate(
        [
            jnp.stack([lax.axis_index("tensor"), lax.axis_index("dp")]).astype(jnp.int32),
            phones + frame_len[:, 0],
            phones,
        ]
    )
    line = Line(sc)
    w3 = jnp.transpose(w_qkv, (1, 0, 2))
    g1, b1, g2, b2 = row(ln1_gain), row(ln1_bias), row(ln2_gain), row(ln2_bias)
    flat = lambda v: v.reshape(count * slot, v.shape[-1])

    x_far, dm_far, w_out_far = swap(x), swap(dm), swap(w_out)
    x_near, w_near = bring([x, w3])
    a1, *qkv, ctx, probs, inv = front_call(line, x_near, x_far, g1, b1, w_near)
    ctx_far = swap(ctx)
    en = mark_call(line, dm, dm_far)
    h, a2 = project_call(line, ctx, ctx_far, w_out, w_out_far, x, x_far, row(attn_bias), g2, b2)

    chunks = (units // 2, units // 2)
    reds, acts, dus, up_sums, at = [], [], [], [], 0
    for chunk in chunks:
        shards = Shards(dp_count, width, (chunk, chunk))
        (act, du, up_sum), grads = feed_call(
            line, shards, a2, en, w_up, w_down, row(up_bias), at, chunk
        )
        reds.append(Reduction(line, shards, grads))
        acts.append(act)
        dus.append(du)
        up_sums.append(up_sum)
        at += chunk
    da = up_back_call(line, dus, w_up, step)
    da_far = swap(da)
    red1, red2 = reds
    red1.advance()
    dhb, dctx, hidden_sums = hidden_back_call(line, rows, da, da_far, h, en, g2, w_out, step)
    own_down, far_down = down_call(line, count, rows, acts, w_down, step)
    far_down = swap(far_down)
    red2.advance()
    mixed = mixed_call(line, h, own_down, far_down, row(down_bias), step // 2)
    red1.advance()

    pairs = local_width // 128
    dctx = dctx.reshape(count, slot, local_width)
    half = pairs // 2
    places3, outs3, sides3 = head_places(half, local_width)
    places4, _, sides4 = head_places(pairs - half, 0)
    shards3, shards4 = Shards(dp_count, width, sides3), Shards(dp_count, width, sides4)
    rest = (qkv, ctx, inv, dctx, probs, flat(a1))
    grads, parts = attend_back_call(line, shards3, 0, places3, outs3, *rest, (dhb, flat(ctx)))
    red3 = Reduction(line, shards3, parts)
    red2.advance()
    red1.advance()
    grads, parts = attend_back_call(line, shards4, half, places4, [], *rest, (), grads)
    red4 = Reduction(line, shards4, parts)
    feed_dims = [(shard_rows, units)] * 2
    feed_places = lambda at, chunk: [(n, None, at, n * chunk, chunk) for n in range(2)]
    red3.advance()
    red2.advance()
    own, far, token_sums = rows_back_call(
        line, [flat(g) for g in grads], w3, x, x_far, step
    )
    far = swap(far)
    up_rows = [v.reshape(-1, width) for v in up_sums]
    sums = Vectors(line, dp_count, jnp.concatenate([token_sums, hidden_sums, *up_rows]), 6)
    red3.advance()
    red4.advance()
    sums.advance()
    d_tokens = tokens_back_call(line, x, dhb, own, far, g1, step // 2)
    sums.advance()
    feed_grads, _ = last_call(line, [(red1, feed_places(0, chunks[0]))], feed_dims)
    red3.advance()
    red4.advance()
    sums.advance()
    (grad_down, grad_up), _ = last_call(
        line, [(red2, feed_places(chunks[0], chunks[1]))], feed_dims, before=feed_grads
    )
    sums.advance()
    red4.advance()

    def head_plan(at, pair_places, out_places, sides):
        starts = [sum(sides[:n]) for n in range(len(sides))]
        plan = []
        for g, (side, column) in enumerate(pair_places):
            for c in range(3):
                plan.append((0, c, (at + g) * 128, starts[side] + column + c * 128, 128))
        for side, column, first, wide in out_places:
            plan.append((1, None, first, starts[side] + column, wide))
        return plan

    (grad_qkv, grad_out), vectors = last_call(
        line,
        [
            (red3, head_plan(0, places3, outs3, sides3)),
            (red4, head_plan(half, places4, [], sides4)),
        ],
        [(3, shard_rows, local_width), (shard_rows, local_width)],
        sums,
    )

    return (
        mixed,
        d_tokens,
        vectors[0],
        vectors[1],
        jnp.transpose(grad_qkv, (1, 0, 2)),
        grad_out.T,
        vectors[2],
        vectors[3],
        vectors[4],
        grad_up,
        vectors[6],
        grad_down.T,
        vectors[5],
    )


def solution(mesh):
    in_specs = (
        P(None, "dp", "tensor", None),
        P(None, "dp", "tensor", None),
        P(None, "dp"),
        P(None, "dp"),
        P(),
        P(),
        P(None, None, "tensor"),
        P("tensor", None),
        P(),
        P(),
        P(),
        P(None, "tensor"),
        P("tensor"),
        P("tensor", None),
        P(),
    )
    out_specs = (
        P(None, "dp", "tensor", None),
        P(None, "dp", "tensor", None),
        P(),
        P(),
        P("dp", None, "tensor"),
        P("tensor", "dp"),
        P(),
        P(),
        P(),
        P("dp", "tensor"),
        P("tensor"),
        P("tensor", "dp"),
        P(),
    )
    return jax.shard_map(local, mesh=mesh, in_specs=in_specs, out_specs=out_specs, check_vma=False)
```
